512 devices in a mesh: cuts: 4 (over y_hi, core), mode: 128 (over y_lo, x, z).
Axes of the slice: x: 4, y: 4 (y_hi: 2, y_lo: 2; y = y_hi * 2 + y_lo), z: 16, core: 2. Of those that a mesh axis runs over, the one named last changes fastest.
Arguments:
- left_tensor: float32 [8, 2, 128, 512, 128], P('cuts', None, 'mode'), may hold values from -6 to 6
- right_tensor: float32 [8, 2, 512, 512], P('cuts', None, None, 'mode'), may hold values from -0.1875 to 0.1875
- closing_tensor: float32 [8, 2, 128, 4], P('cuts'), may hold values from -0.375 to 0.375
Outputs:
- amplitudes: float32 [512, 4, 2, 128], P(('cuts', 'mode'))
The draws below stay inside these ranges and needn't reach their ends.
All inputs are finite; a program needn't handle non-finite values.
Results may differ from the reference program's by a relative error of at most 0.0001.
Values sent between devices are 32-bit elements; how exact they have to be, the bound alone decides.
No kernel may reach another device: no remote copies, remote signals or barrier semaphores. Data moves between devices by JAX's collectives and lax.ppermute only.
A program may use at most 64 MiB of HBM per device.

```python
import jax
import jax.numpy as jnp
from jax import lax

R = 128
K1 = 512
K2 = 512
O = 4
H = 128
SLICES = 8


def steps_of(key, extent, cuts, low, high):
    def one(dim, parts):
        heights = jax.random.uniform(jax.random.fold_in(jax.random.fold_in(key, 6), dim), (parts,), jnp.float32, low / len(cuts), high / len(cuts))
        return jnp.repeat(jnp.exp(heights), extent[dim] // parts).reshape((-1,) + (1,) * (len(extent) - dim - 1))

    level = one(*cuts[0])
    for cut in cuts[1:]:
        level = level * one(*cut)
    return level


def noise(key, extent, width, most, split=(), held_as=jnp.bfloat16):
    values = width * jax.random.normal(key, extent, jnp.float32)
    if split:
        values = values * steps_of(key, extent, split, -0.22, 0.18)
    return jnp.clip(values, -most, most).astype(held_as)


def setup_inputs(seed: int = 0) -> dict:
    arg_keys = jax.random.split(jax.random.key(seed), 4)
    left_tensor = noise(arg_keys[0], (SLICES, 2, H, K1, R), 1.0, 6.0, ((0, 4), (2, 128)), jnp.float32)
    right_tensor = noise(arg_keys[1], (SLICES, 2, K1, K2), (2 * K1) ** -0.5, 0.1875, ((0, 4), (3, 128)), jnp.float32)
    closing_tensor = noise(arg_keys[2], (SLICES, 2, H, O), (2 * H) ** -0.5, 0.375, ((0, 4),), jnp.float32)
    return {"left_tensor": left_tensor, "right_tensor": right_tensor, "closing_tensor": closing_tensor}


def one_slice(total, pieces):
    left, right, closing = pieces
    hi = lax.Precision.HIGHEST
    left_re, left_im = (left[0], left[1])
    right_re, right_im = (right[0], right[1])
    mid_re = jnp.einsum('kq,hkr->hqr', right_re, left_re, precision=hi) - jnp.einsum('kq,hkr->hqr', right_im, left_im, precision=hi)
    mid_im = jnp.einsum('kq,hkr->hqr', right_re, left_im, precision=hi) + jnp.einsum('kq,hkr->hqr', right_im, left_re, precision=hi)
    close_re, close_im = (closing[0], closing[1])
    out_re = jnp.einsum('ho,hqr->qor', close_re, mid_re, precision=hi) - jnp.einsum('ho,hqr->qor', close_im, mid_im, precision=hi)
    out_im = jnp.einsum('ho,hqr->qor', close_re, mid_im, precision=hi) + jnp.einsum('ho,hqr->qor', close_im, mid_re, precision=hi)
    return (total + jnp.stack([out_re, out_im], axis=2), None)

def reference(left_tensor, right_tensor, closing_tensor):
    start = jnp.zeros((K2, O, 2, R), jnp.float32)
    total, unused = lax.scan(one_slice, start, (left_tensor, right_tensor, closing_tensor))
    return total / jnp.sqrt(jnp.float32(SLICES))
```

```python
import jax
import jax.numpy as jnp
from jax import lax
from jax.experimental import pallas as pl
from jax.experimental.pallas import tpu as pltpu
from jax.sharding import Mesh
from jax.sharding import PartitionSpec as P

PARTS = (("yh", 2), ("core", 2), ("yl", 2), ("x", 4), ("za", 8), ("zb", 2))
CUTS = ("yh", "core")
MODE = ("yl", "x", "za", "zb")
NEAR = ("yl", "x", "zb")
FAR = "za"

F32 = jnp.float32
LANES = 128
GROUP = 16


def swap_blocks(v):
    block = lax.broadcasted_iota(jnp.int32, v[0].shape, 1) // GROUP
    v = list(v)
    for bit in (1, 2, 4):
        low = (block & bit) == 0
        for i in range(8):
            if i & bit:
                continue
            a, b = v[i], v[i | bit]
            v[i] = jnp.where(low, a, pltpu.roll(b, GROUP * bit, 1))
            v[i | bit] = jnp.where(low, pltpu.roll(a, LANES - GROUP * bit, 1), b)
    return v


def close_kernel(coef_ref, left_ref, out_ref):
    heads, slices, _, depth, _ = left_ref.shape
    outs = coef_ref.shape[0] // (2 * slices)
    rows = 8
    for s in range(slices):
        acc = [[None] * (depth // rows) for _ in range(2 * outs)]
        for h in range(heads):
            co = [coef_ref[s * 2 * outs + j, h] for j in range(2 * outs)]
            for kb in range(depth // rows):
                at = pl.ds(kb * rows, rows)
                re, im = left_ref[h, s, 0, at, :], left_ref[h, s, 1, at, :]
                for o in range(outs):
                    cre, cim = co[o], co[outs + o]
                    new_re = cre * re - cim * im
                    new_im = cre * im + cim * re
                    if h:
                        new_re, new_im = acc[o][kb] + new_re, acc[outs + o][kb] + new_im
                    acc[o][kb], acc[outs + o][kb] = new_re, new_im
        for kb in range(depth // rows):
            w = swap_blocks([acc[j][kb] for j in range(2 * outs)])
            for g in range(8):
                out_ref[g, pl.ds(s * depth + kb * rows, rows), :] = w[g]


def join_kernel(parts_ref, right_ref, out_ref):
    m = parts_ref[0]
    for i in range(1, parts_ref.shape[0]):
        m = m + parts_ref[i]
    turned = pltpu.roll(m, LANES // 2, 1)
    lane = lax.broadcasted_iota(jnp.int32, m.shape, 1)
    rhs = jnp.concatenate([m, jnp.where(lane < LANES // 2, -turned, turned)], axis=0)
    out = jnp.dot(right_ref[...], rhs, precision=lax.Precision.HIGHEST, preferred_element_type=F32)
    out_ref[...] = out


def shards(left_tensor, right_tensor, closing_tensor):
    slices, _, _, depth, rows = left_tensor.shape
    width = right_tensor.shape[3]
    outs = closing_tensor.shape[3]
    near = 16
    kk = depth // near
    scale = 1.0 / jnp.sqrt(F32(slices * 4))

    with jax.named_scope("right_move"):
        r = right_tensor.reshape(slices, 2, 8, 2, kk, width)
        r = r.transpose(2, 3, 5, 1, 0, 4).reshape(8, 1, 2, width, LANES)
        r = jnp.broadcast_to(r, (8, 8, 2, width, LANES)).reshape(128, width, LANES)
        r = lax.all_to_all(r, MODE, 0, 0, tiled=True)
        r = r.reshape(32, 8, 2, LANES).transpose(0, 2, 1, 3).reshape(512, LANES)

    with jax.named_scope("left_move"):
        x = left_tensor.reshape(slices, 2, near, kk, rows).transpose(2, 0, 1, 3, 4)
        x = lax.all_to_all(x, NEAR, 0, 0, tiled=True)

    with jax.named_scope("coefs"):
        co = closing_tensor.reshape(slices, 2, 8, 8, 2, outs)
        co = lax.dynamic_index_in_dim(co, lax.axis_index(FAR), 3, keepdims=False)
        co = co.transpose(0, 1, 4, 2, 3).reshape(slices * 2 * outs, near) * scale

    with jax.named_scope("close"):
        x = pl.pallas_call(
            close_kernel,
            out_shape=jax.ShapeDtypeStruct((8, slices * kk, LANES), F32),
            in_specs=[pl.BlockSpec(memory_space=pltpu.SMEM), pl.BlockSpec(memory_space=pltpu.VMEM)],
            out_specs=pl.BlockSpec(memory_space=pltpu.VMEM),
            compiler_params=pltpu.CompilerParams(vmem_limit_bytes=16 * 2**20),
            cost_estimate=pl.CostEstimate(flops=2**22, bytes_accessed=5 * 2**18, transcendentals=0),
        )(co, x)

    with jax.named_scope("middle_move"):
        x = lax.all_to_all(x, FAR, 0, 0, tiled=True)

    with jax.named_scope("join"):
        p = pl.pallas_call(
            join_kernel,
            out_shape=jax.ShapeDtypeStruct((512, LANES), F32),
            in_specs=[pl.BlockSpec(memory_space=pltpu.VMEM)] * 2,
            out_specs=pl.BlockSpec(memory_space=pltpu.VMEM),
            compiler_params=pltpu.CompilerParams(vmem_limit_bytes=16 * 2**20),
            cost_estimate=pl.CostEstimate(flops=2**26, bytes_accessed=3 * 2**18, transcendentals=0),
        )(x, r)

    with jax.named_scope("sum_move"):
        p = lax.all_to_all(p.reshape(64, 8, LANES), CUTS + NEAR, 0, 0, tiled=True)
        p = jnp.sum(p, axis=0)

    with jax.named_scope("row_move"):
        p = lax.all_to_all(p, FAR, 0, 0, tiled=True)
        p = p.reshape(8, 2, outs, GROUP).transpose(2, 1, 0, 3)
    return p.reshape(1, outs, 2, rows)


def solution(mesh):
    fine = Mesh(mesh.devices.reshape([n for _, n in PARTS]), [name for name, _ in PARTS])
    return jax.shard_map(
        shards,
        mesh=fine,
        in_specs=(
            P(CUTS, None, MODE, None, None),
            P(CUTS, None, None, MODE),
            P(CUTS, None, None, None),
        ),
        out_specs=P(CUTS + MODE, None, None, None),
        check_vma=False,
    )
```

```python
import jax
import jax.numpy as jnp
from jax import lax
from jax.experimental import pallas as pl
from jax.experimental.pallas import tpu as pltpu
from jax.sharding import Mesh
from jax.sharding import PartitionSpec as P

PARTS = (("yh", 2), ("core", 2), ("yl", 2), ("x", 4), ("za", 8), ("zb", 2))
CUTS = ("yh", "core")
MODE = ("yl", "x", "za", "zb")
NEAR = ("yl", "x", "zb")
FAR = "za"

F32 = jnp.float32
LANES = 128
GROUP = 16


def swap_blocks(v):
    n = len(v)
    size = LANES // n
    block = lax.broadcasted_iota(jnp.int32, v[0].shape, 1) // size
    v = list(v)
    bit = 1
    while bit < n:
        low = (block & bit) == 0
        for i in range(n):
            if i & bit:
                continue
            a, b = v[i], v[i | bit]
            v[i] = jnp.where(low, a, pltpu.roll(b, size * bit, 1))
            v[i | bit] = jnp.where(low, pltpu.roll(a, LANES - size * bit, 1), b)
        bit *= 2
    return v


def pack_kernel(left_ref, right_ref, out_ref, sems):
    slices, _, near, depth, _ = left_ref.shape
    copies = []
    for i in range(2 * slices):
        to = out_ref.at[:, pl.ds(i * depth, depth), :]
        copies.append(pltpu.make_async_copy(left_ref.at[i // 2, i % 2], to, sems.at[i]))
        copies[-1].start()
    width = right_ref.shape[2]
    each = 2 * slices
    for t in range(near // each):
        lanes = pl.ds(t * LANES, LANES)
        w = swap_blocks([right_ref[j % slices, j // slices, :, lanes] for j in range(each)])
        for g in range(each):
            out_ref[t * each + g, pl.ds(each * depth, width), :] = w[g]
    for copy in copies:
        copy.wait()


def close_kernel(far_ref, coef_ref, left_ref, out_ref):
    heads = left_ref.shape[0]
    slices, _, outs, _ = coef_ref.shape
    depth = out_ref.shape[1] // slices
    first = far_ref[0] * 2
    rows = 8
    for s in range(slices):
        acc = [[None] * (depth // rows) for _ in range(2 * outs)]
        for h in range(heads):
            head = (h // 2) * 16 + first + h % 2
            co = [coef_ref[s, j // outs, j % outs, head] for j in range(2 * outs)]
            for kb in range(depth // rows):
                at = 2 * s * depth + kb * rows
                re = left_ref[h, pl.ds(at, rows), :]
                im = left_ref[h, pl.ds(at + depth, rows), :]
                for o in range(outs):
                    cre, cim = co[o], co[outs + o]
                    new_re = cre * re - cim * im
                    new_im = cre * im + cim * re
                    if h:
                        new_re, new_im = acc[o][kb] + new_re, acc[outs + o][kb] + new_im
                    acc[o][kb], acc[outs + o][kb] = new_re, new_im
        for kb in range(depth // rows):
            w = swap_blocks([acc[j][kb] for j in range(2 * outs)])
            for g in range(8):
                out_ref[g, pl.ds(s * depth + kb * rows, rows), :] = w[g]


def join_kernel(parts_ref, right_ref, out_ref):
    m = parts_ref[0]
    for i in range(1, parts_ref.shape[0]):
        m = m + parts_ref[i]
    turned = pltpu.roll(m, LANES // 2, 1)
    lane = lax.broadcasted_iota(jnp.int32, m.shape, 1)
    rhs = jnp.concatenate([m, jnp.where(lane < LANES // 2, -turned, turned)], axis=0)
    out = jnp.dot(right_ref[...], rhs, precision=lax.Precision.HIGHEST, preferred_element_type=F32)
    out_ref[...] = out


def shards(left_tensor, right_tensor, closing_tensor):
    slices, _, _, depth, rows = left_tensor.shape
    width = right_tensor.shape[3]
    outs = closing_tensor.shape[3]
    near = 16
    kk = depth // near
    scale = 1.0 / jnp.sqrt(F32(slices * 4))

    with jax.named_scope("pack"):
        body = slices * 2 * kk
        x = pl.pallas_call(
            pack_kernel,
            out_shape=jax.ShapeDtypeStruct((near, body + width, LANES), F32),
            in_specs=[pl.BlockSpec(memory_space=pl.ANY), pl.BlockSpec(memory_space=pltpu.VMEM)],
            out_specs=pl.BlockSpec(memory_space=pltpu.VMEM),
            scratch_shapes=[pltpu.SemaphoreType.DMA((slices * 2,))],
            compiler_params=pltpu.CompilerParams(vmem_limit_bytes=16 * 2**20),
            cost_estimate=pl.CostEstimate(flops=0, bytes_accessed=2**21, transcendentals=0),
        )(left_tensor.reshape(slices, 2, near, kk, rows), right_tensor.transpose(0, 1, 3, 2))

    with jax.named_scope("near_move"):
        x = lax.all_to_all(x, NEAR, 0, 0, tiled=True)

    with jax.named_scope("right_move"):
        r = lax.all_gather(x[:, body:], FAR, axis=0, tiled=True)
        r = r.reshape(4, 2, 2, 4, 2, 2, 2, LANES)
        r = r.transpose(2, 3, 0, 6, 1, 4, 5, 7).reshape(512, LANES)

    with jax.named_scope("close"):
        x = pl.pallas_call(
            close_kernel,
            out_shape=jax.ShapeDtypeStruct((8, slices * kk, LANES), F32),
            in_specs=[pl.BlockSpec(memory_space=pltpu.SMEM)] * 2 + [pl.BlockSpec(memory_space=pltpu.VMEM)],
            out_specs=pl.BlockSpec(memory_space=pltpu.VMEM),
            compiler_params=pltpu.CompilerParams(vmem_limit_bytes=16 * 2**20),
            cost_estimate=pl.CostEstimate(flops=2**22, bytes_accessed=5 * 2**18, transcendentals=0),
        )(lax.axis_index(FAR).reshape(1), closing_tensor.transpose(0, 1, 3, 2), x)

    with jax.named_scope("middle_move"):
        x = lax.all_to_all(x, FAR, 0, 0, tiled=True)

    with jax.named_scope("join"):
        p = pl.pallas_call(
            join_kernel,
            out_shape=jax.ShapeDtypeStruct((512, LANES), F32),
            in_specs=[pl.BlockSpec(memory_space=pltpu.VMEM)] * 2,
            out_specs=pl.BlockSpec(memory_space=pltpu.VMEM),
            compiler_params=pltpu.CompilerParams(vmem_limit_bytes=16 * 2**20),
            cost_estimate=pl.CostEstimate(flops=2**26, bytes_accessed=3 * 2**18, transcendentals=0),
        )(x, r)

    with jax.named_scope("sum_move"):
        p = lax.all_to_all(p.reshape(64, 8, LANES), CUTS + NEAR, 0, 0, tiled=True)
        p = jnp.sum(p, axis=0) * scale

    with jax.named_scope("row_move"):
        p = lax.all_to_all(p, FAR, 0, 0, tiled=True)
        p = p.reshape(8, 2, outs, GROUP).transpose(2, 1, 0, 3)
    return p.reshape(1, outs, 2, rows)


def solution(mesh):
    fine = Mesh(mesh.devices.reshape([n for _, n in PARTS]), [name for name, _ in PARTS])
    return jax.shard_map(
        shards,
        mesh=fine,
        in_specs=(
            P(CUTS, None, MODE, None, None),
            P(CUTS, None, None, MODE),
            P(CUTS, None, None, None),
        ),
        out_specs=P(CUTS + MODE, None, None, None),
        check_vma=False,
    )
```

```python
import jax
import jax.numpy as jnp
from jax import lax
from jax.experimental import pallas as pl
from jax.experimental.pallas import tpu as pltpu
from jax.sharding import Mesh
from jax.sharding import PartitionSpec as P

PARTS = (("yh", 2), ("core", 2), ("yl", 2), ("x", 4), ("za", 8), ("zb", 2))
CUTS = ("yh", "core")
MODE = ("yl", "x", "za", "zb")
NEAR = ("yl", "x", "zb")
FAR = "za"

F32 = jnp.float32
LANES = 128
GROUP = 16
OTHERS = (0, 4, 2, 6)
SMEM = pl.BlockSpec(memory_space=pltpu.SMEM)
VMEM = pl.BlockSpec(memory_space=pltpu.VMEM)


def swap_blocks(v):
    n = len(v)
    size = LANES // n
    block = lax.broadcasted_iota(jnp.int32, v[0].shape, 1) // size
    v = list(v)
    bit = 1
    while bit < n:
        low = (block & bit) == 0
        for i in range(n):
            if i & bit:
                continue
            a, b = v[i], v[i | bit]
            v[i] = jnp.where(low, a, pltpu.roll(b, size * bit, 1))
            v[i | bit] = jnp.where(low, pltpu.roll(a, LANES - size * bit, 1), b)
        bit *= 2
    return v


def pack_kernel(left_ref, right_ref, out_ref, sems):
    slices, _, near, depth, _ = left_ref.shape
    copies = []
    for i in range(2 * slices):
        to = out_ref.at[:, pl.ds(i * depth, depth), :]
        copies.append(pltpu.make_async_copy(left_ref.at[i // 2, i % 2], to, sems.at[i]))
        copies[-1].start()
    width = right_ref.shape[2]
    each = 2 * slices
    for t in range(near // each):
        lanes = pl.ds(t * LANES, LANES)
        w = swap_blocks([right_ref[j % slices, j // slices, :, lanes] for j in range(each)])
        for g in range(each):
            out_ref[t * each + g, pl.ds(each * depth, width), :] = w[g]
    for copy in copies:
        copy.wait()


def close_kernel(far_ref, coef_ref, left_ref, out_ref):
    heads = left_ref.shape[0]
    slices, _, outs, _ = coef_ref.shape
    depth = out_ref.shape[1] // slices
    first = far_ref[0] * 2
    rows = 8
    for s in range(slices):
        acc = [[None] * (depth // rows) for _ in range(2 * outs)]
        for h in range(heads):
            head = (h // 2) * 16 + first + h % 2
            co = [coef_ref[s, j // outs, j % outs, head] for j in range(2 * outs)]
            for kb in range(depth // rows):
                at = 2 * s * depth + kb * rows
                re = left_ref[h, pl.ds(at, rows), :]
                im = left_ref[h, pl.ds(at + depth, rows), :]
                for o in range(outs):
                    cre, cim = co[o], co[outs + o]
                    new_re = cre * re - cim * im
                    new_im = cre * im + cim * re
                    if h:
                        new_re, new_im = acc[o][kb] + new_re, acc[outs + o][kb] + new_im
                    acc[o][kb], acc[outs + o][kb] = new_re, new_im
        for kb in range(depth // rows):
            w = swap_blocks([acc[j][kb] for j in range(2 * outs)])
            for g in range(8):
                out_ref[g, pl.ds(s * depth + kb * rows, rows), :] = w[g]


def join_kernel(far_ref, parts_ref, even_ref, odd_ref, out_ref):
    m = parts_ref[0]
    for i in range(1, parts_ref.shape[0]):
        m = m + parts_ref[i]
    turned = pltpu.roll(m, LANES // 2, 1)
    lane = lax.broadcasted_iota(jnp.int32, m.shape, 1)
    rhs = jnp.concatenate([m, jnp.where(lane < LANES // 2, -turned, turned)], axis=0)

    def times(ref):
        out = jnp.dot(ref[...], rhs, precision=lax.Precision.HIGHEST, preferred_element_type=F32)
        return out.reshape(4, 8, 8, LANES)

    even, odd = times(even_ref), times(odd_ref)
    here = far_ref[0]
    straight = (here & 1) == 0
    first = lax.broadcasted_iota(jnp.int32, even.shape[1:], 1) < 4
    for i, other in enumerate(OTHERS):
        low = jnp.where(straight, even[i], odd[i])
        high = jnp.where(straight, odd[i], even[i])
        top = jnp.where(first, low, pltpu.roll(high, 4, 1))
        bottom = jnp.where(first, pltpu.roll(low, 4, 1), high)
        at = (here ^ other) // 2
        out_ref[:, at, :, 0:8, :] = top.reshape(4, 2, 8, LANES)
        out_ref[:, at, :, 8:16, :] = bottom.reshape(4, 2, 8, LANES)


def finish_kernel(parts_ref, out_ref):
    w = swap_blocks([parts_ref[i] for i in range(parts_ref.shape[0])])
    outs = out_ref.shape[0]
    for c in range(2):
        for o in range(outs):
            out_ref[o, pl.ds(c, 1), :] = w[c * outs + o]


def kernel_call(body, shape, specs, cost, name, scratch=(), vmem=16):
    flops, size = cost
    return pl.pallas_call(
        body,
        out_shape=jax.ShapeDtypeStruct(shape, F32),
        in_specs=specs,
        out_specs=VMEM,
        scratch_shapes=scratch,
        compiler_params=pltpu.CompilerParams(vmem_limit_bytes=vmem * 2**20),
        cost_estimate=pl.CostEstimate(flops=flops, bytes_accessed=size, transcendentals=0),
        name=name,
    )


def shards(left_tensor, right_tensor, closing_tensor):
    slices, _, _, depth, rows = left_tensor.shape
    width = right_tensor.shape[3]
    outs = closing_tensor.shape[3]
    near = 16
    kk = depth // near
    body = slices * 2 * kk
    scale = 1.0 / jnp.sqrt(F32(slices * 4))
    here = lax.axis_index(FAR).reshape(1)

    x = kernel_call(
        pack_kernel,
        (near, body + width, LANES),
        [pl.BlockSpec(memory_space=pltpu.HBM), VMEM],
        (0, 2**21),
        "pack",
        [pltpu.SemaphoreType.DMA((slices * 2,))],
        60,
    )(left_tensor.reshape(slices, 2, near, kk, rows), right_tensor.transpose(0, 1, 3, 2))

    with jax.named_scope("near_move"):
        x = lax.all_to_all(x, NEAR, 0, 0, tiled=True)

    with jax.named_scope("right_move"):
        r = x[:, body:].reshape(2, 2, 2, 2, 2, 2, LANES).transpose(1, 2, 5, 0, 3, 4, 6)
        r = r.reshape(near * width, LANES)
        for step in (4, 2):
            r = jnp.concatenate([r, lax.ppermute(r, FAR, [(i, i ^ step) for i in range(8)])])
        odd = lax.ppermute(r, FAR, [(i, i ^ 1) for i in range(8)])

    x = kernel_call(
        close_kernel, (8, slices * kk, LANES), [SMEM, SMEM, VMEM], (2**22, 5 * 2**18), "close"
    )(here, closing_tensor.transpose(0, 1, 3, 2), x)

    with jax.named_scope("middle_move"):
        x = lax.all_to_all(x, FAR, 0, 0, tiled=True)

    p = kernel_call(
        join_kernel, (4, 4, 2, 16, LANES), [SMEM, VMEM, VMEM, VMEM], (2**26, 3 * 2**18), "join"
    )(here, x, r, odd)

    with jax.named_scope("sum_move"):
        p = lax.all_to_all(p.reshape(32, 16, LANES), ("core",) + NEAR, 0, 0, tiled=True)
        p = jnp.sum(p, axis=0) * scale

    with jax.named_scope("row_move"):
        p = lax.all_to_all(p.reshape(16, 1, LANES), ("yh", FAR), 0, 0, tiled=True)
        p = p[:8] + p[8:]

    p = kernel_call(finish_kernel, (outs, 2, rows), [VMEM], (0, 2**13), "finish")(p)
    return p.reshape(1, outs, 2, rows)


def solution(mesh):
    fine = Mesh(mesh.devices.reshape([n for _, n in PARTS]), [name for name, _ in PARTS])
    return jax.shard_map(
        shards,
        mesh=fine,
        in_specs=(
            P(CUTS, None, MODE, None, None),
            P(CUTS, None, None, MODE),
            P(CUTS, None, None, None),
        ),
        out_specs=P(CUTS + MODE, None, None, None),
        check_vma=False,
    )
```

```python
import jax
import jax.numpy as jnp
from jax import lax
from jax.experimental import pallas as pl
from jax.experimental.pallas import tpu as pltpu
from jax.sharding import Mesh
from jax.sharding import PartitionSpec as P

PARTS = (("yh", 2), ("core", 2), ("yl", 2), ("x", 4), ("za", 8), ("zb", 2))
CUTS = ("yh", "core")
MODE = ("yl", "x", "za", "zb")
NEAR = ("yl", "x", "zb")
FAR = "za"

F32 = jnp.float32
LANES = 128
GROUP = 16
SMEM = pl.BlockSpec(memory_space=pltpu.SMEM)
VMEM = pl.BlockSpec(memory_space=pltpu.VMEM)
ANY = pl.BlockSpec(memory_space=pl.ANY)


def swap_blocks(v):
    n = len(v)
    size = LANES // n
    block = lax.broadcasted_iota(jnp.int32, v[0].shape, 1) // size
    v = list(v)
    bit = 1
    while bit < n:
        low = (block & bit) == 0
        for i in range(n):
            if i & bit:
                continue
            a, b = v[i], v[i | bit]
            v[i] = jnp.where(low, a, pltpu.roll(b, size * bit, 1))
            v[i | bit] = jnp.where(low, pltpu.roll(a, LANES - size * bit, 1), b)
        bit *= 2
    return v


def pack_kernel(left_ref, right_ref, out_ref, held, sems):
    slices, _, near, depth, _ = left_ref.shape
    copies = []
    for i in range(2 * slices):
        to = out_ref.at[:, pl.ds(i * depth, depth), :]
        copies.append(pltpu.make_async_copy(left_ref.at[i // 2, i % 2], to, sems.at[i]))
        copies[-1].start()
    width = right_ref.shape[2]
    each = 2 * slices
    for t in range(near // each):
        lanes = pl.ds(t * LANES, LANES)
        w = swap_blocks([right_ref[j % slices, j // slices, :, lanes] for j in range(each)])
        for g in range(each):
            held[t * each + g] = w[g]
    to = out_ref.at[:, pl.ds(each * depth, width), :]
    copies.append(pltpu.make_async_copy(held, to, sems.at[2 * slices]))
    copies[-1].start()
    for copy in copies:
        copy.wait()


def close_kernel(far_ref, coef_ref, left_ref, out_ref, held):
    heads = left_ref.shape[0]
    slices, _, outs, _ = coef_ref.shape
    body = left_ref.shape[1] - held.shape[0] // heads
    depth = body // (2 * slices)
    for q8 in range(2):
        for q76 in range(4):
            for q0 in range(2):
                for q2 in range(2):
                    two = left_ref[q8 * 8 + q76 * 2 + q2, pl.ds(body + q0, 2, stride=2), :]
                    held[pl.ds(q76 * 16 + q0 * 8 + q8 * 4 + q2 * 2, 2), :] = two
    for g in range(8):
        out_ref[g, pl.ds(slices * depth, 64), :] = held[...]
    first = far_ref[0] * 2
    rows = 8
    for s in range(slices):
        acc = [[None] * (depth // rows) for _ in range(2 * outs)]
        for h in range(heads):
            head = (h // 2) * 16 + first + h % 2
            co = [coef_ref[s, j // outs, j % outs, head] for j in range(2 * outs)]
            for kb in range(depth // rows):
                at = 2 * s * depth + kb * rows
                re = left_ref[h, pl.ds(at, rows), :]
                im = left_ref[h, pl.ds(at + depth, rows), :]
                for o in range(outs):
                    cre, cim = co[o], co[outs + o]
                    new_re = cre * re - cim * im
                    new_im = cre * im + cim * re
                    if h:
                        new_re, new_im = acc[o][kb] + new_re, acc[outs + o][kb] + new_im
                    acc[o][kb], acc[outs + o][kb] = new_re, new_im
        for kb in range(depth // rows):
            w = swap_blocks([acc[j][kb] for j in range(2 * outs)])
            for g in range(8):
                out_ref[g, pl.ds(s * depth + kb * rows, rows), :] = w[g]


def join_kernel(parts_ref, out_ref):
    half = parts_ref.shape[1] // 2
    m = parts_ref[0, :half, :]
    for i in range(1, parts_ref.shape[0]):
        m = m + parts_ref[i, :half, :]
    turned = pltpu.roll(m, LANES // 2, 1)
    lane = lax.broadcasted_iota(jnp.int32, m.shape, 1)
    rhs = jnp.concatenate([m, jnp.where(lane < LANES // 2, -turned, turned)], axis=0)
    right = parts_ref[:, half:, :].reshape(8 * half, LANES)
    out = jnp.dot(right, rhs, precision=lax.Precision.HIGHEST, preferred_element_type=F32)
    out = out.reshape(4, 2, 8, 8, LANES)
    first = lax.broadcasted_iota(jnp.int32, (8, 8, LANES), 1) < 4
    for i in range(4):
        low, high = out[i, 0], out[i, 1]
        top = jnp.where(first, low, pltpu.roll(high, 4, 1))
        bottom = jnp.where(first, pltpu.roll(low, 4, 1), high)
        out_ref[:, i, :, 0:8, :] = top.reshape(4, 2, 8, LANES)
        out_ref[:, i, :, 8:16, :] = bottom.reshape(4, 2, 8, LANES)


def finish_kernel(parts_ref, out_ref):
    w = swap_blocks([parts_ref[i] for i in range(parts_ref.shape[0])])
    outs = out_ref.shape[0]
    for c in range(2):
        for o in range(outs):
            out_ref[o, pl.ds(c, 1), :] = w[c * outs + o]


def kernel_call(body, shape, specs, cost, name, scratch=(), vmem=16, to=VMEM):
    flops, size = cost
    return pl.pallas_call(
        body,
        out_shape=jax.ShapeDtypeStruct(shape, F32),
        in_specs=specs,
        out_specs=to,
        scratch_shapes=scratch,
        compiler_params=pltpu.CompilerParams(vmem_limit_bytes=vmem * 2**20),
        cost_estimate=pl.CostEstimate(flops=flops, bytes_accessed=size, transcendentals=0),
        name=name,
    )


def shards(left_tensor, right_tensor, closing_tensor):
    slices, _, _, depth, rows = left_tensor.shape
    width = right_tensor.shape[3]
    outs = closing_tensor.shape[3]
    near = 16
    kk = depth // near
    body = slices * 2 * kk
    scale = 1.0 / jnp.sqrt(F32(slices * 4))
    here = lax.axis_index(FAR).reshape(1)

    x = kernel_call(
        pack_kernel,
        (near, body + width, LANES),
        [ANY, VMEM],
        (0, 2**21),
        "pack",
        [pltpu.VMEM((near, width, LANES), F32), pltpu.SemaphoreType.DMA((slices * 2 + 1,))],
        60,
        ANY,
    )(left_tensor.reshape(slices, 2, near, kk, rows), right_tensor.transpose(0, 1, 3, 2))

    with jax.named_scope("near_move"):
        x = lax.all_to_all(x, NEAR, 0, 0, tiled=True)

    x = kernel_call(
        close_kernel,
        (8, slices * kk + near * width, LANES),
        [SMEM, SMEM, VMEM],
        (2**22, 6 * 2**18),
        "close",
        [pltpu.VMEM((near * width, LANES), F32)],
    )(here, closing_tensor.transpose(0, 1, 3, 2), x)

    with jax.named_scope("far_move"):
        x = lax.all_to_all(x, FAR, 0, 0, tiled=True)

    p = kernel_call(join_kernel, (4, 4, 2, 16, LANES), [VMEM], (2**26, 3 * 2**18), "join")(x)

    with jax.named_scope("sum_move"):
        p = lax.all_to_all(p.reshape(32, 16, LANES), ("core",) + NEAR, 0, 0, tiled=True)
        p = jnp.sum(p, axis=0) * scale

    with jax.named_scope("row_move"):
        p = lax.all_to_all(p.reshape(16, 1, LANES), ("yh", FAR), 0, 0, tiled=True)
        p = p[:8] + p[8:]

    p = kernel_call(finish_kernel, (outs, 2, rows), [VMEM], (0, 2**13), "finish")(p)
    return p.reshape(1, outs, 2, rows)


def solution(mesh):
    fine = Mesh(mesh.devices.reshape([n for _, n in PARTS]), [name for name, _ in PARTS])
    return jax.shard_map(
        shards,
        mesh=fine,
        in_specs=(
            P(CUTS, None, MODE, None, None),
            P(CUTS, None, None, MODE),
            P(CUTS, None, None, None),
        ),
        out_specs=P(CUTS + MODE, None, None, None),
        check_vma=False,
    )
```

```python
import jax
import jax.numpy as jnp
from jax import lax
from jax.experimental import pallas as pl
from jax.experimental.pallas import tpu as pltpu
from jax.sharding import Mesh
from jax.sharding import PartitionSpec as P

PARTS = (("yh", 2), ("core", 2), ("yl", 2), ("x", 4), ("za", 8), ("zb", 2))
CUTS = ("yh", "core")
MODE = ("yl", "x", "za", "zb")
NEAR = ("yl", "x", "zb")
FAR = "za"

F32 = jnp.float32
LANES = 128
GROUP = 16
SMEM = pl.BlockSpec(memory_space=pltpu.SMEM)
VMEM = pl.BlockSpec(memory_space=pltpu.VMEM)
ANY = pl.BlockSpec(memory_space=pl.ANY)


def swap_blocks(v):
    n = len(v)
    size = LANES // n
    block = lax.broadcasted_iota(jnp.int32, v[0].shape, 1) // size
    v = list(v)
    bit = 1
    while bit < n:
        low = (block & bit) == 0
        for i in range(n):
            if i & bit:
                continue
            a, b = v[i], v[i | bit]
            v[i] = jnp.where(low, a, pltpu.roll(b, size * bit, 1))
            v[i | bit] = jnp.where(low, pltpu.roll(a, LANES - size * bit, 1), b)
        bit *= 2
    return v


def pack_kernel(left_ref, right_ref, out_ref, held, piece, into, out_of):
    slices, _, near, depth, _ = left_ref.shape
    each = 2 * slices
    copies = []
    for i in range(each):
        copies.append(pltpu.make_async_copy(left_ref.at[i // 2, i % 2], held.at[i], into.at[i]))
        copies[-1].start()
    width = right_ref.shape[2]
    for t in range(near // each):
        lanes = pl.ds(t * LANES, LANES)
        w = swap_blocks([right_ref[j % slices, j // slices, :, lanes] for j in range(each)])
        for g in range(each):
            piece[t * each + g] = w[g]
    to = out_ref.at[:, pl.ds(each * depth, width), :]
    last = [pltpu.make_async_copy(piece, to, out_of.at[each])]
    last[0].start()
    for i in range(each):
        copies[i].wait()
        to = out_ref.at[:, pl.ds(i * depth, depth), :]
        last.append(pltpu.make_async_copy(held.at[i], to, out_of.at[i]))
        last[-1].start()
    for copy in last:
        copy.wait()


def close_kernel(far_ref, coef_ref, left_ref, out_ref, held):
    heads = left_ref.shape[0]
    slices, _, outs, _ = coef_ref.shape
    body = left_ref.shape[1] - held.shape[0] // heads
    depth = body // (2 * slices)
    for q8 in range(2):
        for q76 in range(4):
            for q0 in range(2):
                for q2 in range(2):
                    two = left_ref[q8 * 8 + q76 * 2 + q2, pl.ds(body + q0, 2, stride=2), :]
                    held[pl.ds(q76 * 16 + q0 * 8 + q8 * 4 + q2 * 2, 2), :] = two
    for g in range(8):
        out_ref[g, pl.ds(slices * depth, 64), :] = held[...]
    first = far_ref[0] * 2
    rows = 8
    for s in range(slices):
        acc = [[None] * (depth // rows) for _ in range(2 * outs)]
        for h in range(heads):
            head = (h // 2) * 16 + first + h % 2
            co = [coef_ref[s, j // outs, j % outs, head] for j in range(2 * outs)]
            for kb in range(depth // rows):
                at = 2 * s * depth + kb * rows
                re = left_ref[h, pl.ds(at, rows), :]
                im = left_ref[h, pl.ds(at + depth, rows), :]
                for o in range(outs):
                    cre, cim = co[o], co[outs + o]
                    new_re = cre * re - cim * im
                    new_im = cre * im + cim * re
                    if h:
                        new_re, new_im = acc[o][kb] + new_re, acc[outs + o][kb] + new_im
                    acc[o][kb], acc[outs + o][kb] = new_re, new_im
        for kb in range(depth // rows):
            w = swap_blocks([acc[j][kb] for j in range(2 * outs)])
            for g in range(8):
                out_ref[g, pl.ds(s * depth + kb * rows, rows), :] = w[g]


def join_kernel(parts_ref, out_ref):
    half = parts_ref.shape[1] // 2
    m = parts_ref[0, :half, :]
    for i in range(1, parts_ref.shape[0]):
        m = m + parts_ref[i, :half, :]
    turned = pltpu.roll(m, LANES // 2, 1)
    lane = lax.broadcasted_iota(jnp.int32, m.shape, 1)
    rhs = jnp.concatenate([m, jnp.where(lane < LANES // 2, -turned, turned)], axis=0)
    right = parts_ref[:, half:, :].reshape(8 * half, LANES)
    out = jnp.dot(right, rhs, precision=lax.Precision.HIGHEST, preferred_element_type=F32)
    out = out.reshape(4, 2, 8, 8, LANES)
    first = lax.broadcasted_iota(jnp.int32, (8, 8, LANES), 1) < 4
    for i in range(4):
        low, high = out[i, 0], out[i, 1]
        top = jnp.where(first, low, pltpu.roll(high, 4, 1))
        bottom = jnp.where(first, pltpu.roll(low, 4, 1), high)
        out_ref[:, i, :, 0:8, :] = top.reshape(4, 2, 8, LANES)
        out_ref[:, i, :, 8:16, :] = bottom.reshape(4, 2, 8, LANES)


def finish_kernel(parts_ref, out_ref):
    w = swap_blocks([parts_ref[i] for i in range(parts_ref.shape[0])])
    outs = out_ref.shape[0]
    for c in range(2):
        for o in range(outs):
            out_ref[o, pl.ds(c, 1), :] = w[c * outs + o]


def kernel_call(body, shape, specs, cost, name, scratch=(), vmem=16, to=VMEM):
    flops, size = cost
    return pl.pallas_call(
        body,
        out_shape=jax.ShapeDtypeStruct(shape, F32),
        in_specs=specs,
        out_specs=to,
        scratch_shapes=scratch,
        compiler_params=pltpu.CompilerParams(vmem_limit_bytes=vmem * 2**20),
        cost_estimate=pl.CostEstimate(flops=flops, bytes_accessed=size, transcendentals=0),
        name=name,
    )


def shards(left_tensor, right_tensor, closing_tensor):
    slices, _, _, depth, rows = left_tensor.shape
    width = right_tensor.shape[3]
    outs = closing_tensor.shape[3]
    near = 16
    kk = depth // near
    body = slices * 2 * kk
    scale = 1.0 / jnp.sqrt(F32(slices * 4))
    here = lax.axis_index(FAR).reshape(1)

    x = kernel_call(
        pack_kernel,
        (near, body + width, LANES),
        [ANY, VMEM],
        (0, 2**21),
        "pack",
        [
            pltpu.VMEM((slices * 2, near, kk, rows), F32),
            pltpu.VMEM((near, width, LANES), F32),
            pltpu.SemaphoreType.DMA((slices * 2,)),
            pltpu.SemaphoreType.DMA((slices * 2 + 1,)),
        ],
        60,
        ANY,
    )(left_tensor.reshape(slices, 2, near, kk, rows), right_tensor.transpose(0, 1, 3, 2))

    with jax.named_scope("near_move"):
        x = lax.all_to_all(x, NEAR, 0, 0, tiled=True)

    x = kernel_call(
        close_kernel,
        (8, slices * kk + near * width, LANES),
        [SMEM, SMEM, VMEM],
        (2**22, 6 * 2**18),
        "close",
        [pltpu.VMEM((near * width, LANES), F32)],
    )(here, closing_tensor.transpose(0, 1, 3, 2), x)

    with jax.named_scope("far_move"):
        x = lax.all_to_all(x, FAR, 0, 0, tiled=True)

    p = kernel_call(join_kernel, (4, 4, 2, 16, LANES), [VMEM], (2**26, 3 * 2**18), "join")(x)

    with jax.named_scope("sum_move"):
        p = lax.all_to_all(p.reshape(32, 16, LANES), ("core",) + NEAR, 0, 0, tiled=True)
        p = jnp.sum(p, axis=0) * scale

    with jax.named_scope("row_move"):
        p = lax.all_to_all(p.reshape(16, 1, LANES), ("yh", FAR), 0, 0, tiled=True)
        p = p[:8] + p[8:]

    p = kernel_call(finish_kernel, (outs, 2, rows), [VMEM], (0, 2**13), "finish")(p)
    return p.reshape(1, outs, 2, rows)


def solution(mesh):
    fine = Mesh(mesh.devices.reshape([n for _, n in PARTS]), [name for name, _ in PARTS])
    return jax.shard_map(
        shards,
        mesh=fine,
        in_specs=(
            P(CUTS, None, MODE, None, None),
            P(CUTS, None, None, MODE),
            P(CUTS, None, None, None),
        ),
        out_specs=P(CUTS + MODE, None, None, None),
        check_vma=False,
    )
```

```python
import functools

import jax
import jax.numpy as jnp
from jax import lax
from jax.experimental import pallas as pl
from jax.experimental.pallas import tpu as pltpu
from jax.sharding import Mesh
from jax.sharding import PartitionSpec as P

PARTS = (("yh", 2), ("core", 2), ("yl", 2), ("x", 4), ("za", 8), ("zb", 2))
CUTS = ("yh", "core")
MODE = ("yl", "x", "za", "zb")
NEAR = ("yl", "x", "zb")
FAR = "za"

F32 = jnp.float32
LANES = 128
SMEM = pl.BlockSpec(memory_space=pltpu.SMEM)
VMEM = pl.BlockSpec(memory_space=pltpu.VMEM)
ANY = pl.BlockSpec(memory_space=pl.ANY)


def swap_blocks(v):
    n = len(v)
    size = LANES // n
    block = lax.broadcasted_iota(jnp.int32, v[0].shape, 1) // size
    v = list(v)
    bit = 1
    while bit < n:
        low = (block & bit) == 0
        for i in range(n):
            if i & bit:
                continue
            a, b = v[i], v[i | bit]
            v[i] = jnp.where(low, a, pltpu.roll(b, size * bit, 1))
            v[i | bit] = jnp.where(low, pltpu.roll(a, LANES - size * bit, 1), b)
        bit *= 2
    return v


def pack_kernel(left_ref, right_ref, out_ref, held, piece, into, out_of):
    slices, _, near, depth, _ = left_ref.shape
    each = 2 * slices
    copies = []
    for i in range(each):
        copies.append(pltpu.make_async_copy(left_ref.at[i // 2, i % 2], held.at[i], into.at[i]))
        copies[-1].start()
    width = right_ref.shape[2]
    for t in range(near // each):
        lanes = pl.ds(t * LANES, LANES)
        w = swap_blocks([right_ref[j % slices, j // slices, :, lanes] for j in range(each)])
        for g in range(each):
            piece[t * each + g] = w[g]
    to = out_ref.at[:, pl.ds(each * depth, width), :]
    last = [pltpu.make_async_copy(piece, to, out_of.at[each])]
    last[0].start()
    for i in range(each):
        copies[i].wait()
        to = out_ref.at[:, pl.ds(i * depth, depth), :]
        last.append(pltpu.make_async_copy(held.at[i], to, out_of.at[i]))
        last[-1].start()
    for copy in last:
        copy.wait()


def spread_kernel(near_ref, out_ref):
    heads = near_ref.shape[0]
    body = near_ref.shape[1] - out_ref.shape[2] * 2 // heads
    for q7 in range(2):
        for q6 in range(2):
            for q0 in range(2):
                for q8 in range(2):
                    for q2 in range(2):
                        two = near_ref[q8 * 8 + q7 * 4 + q6 * 2 + q2, pl.ds(body + q0, 2, stride=2), :]
                        out_ref[q7, 0, pl.ds(q6 * 16 + q0 * 8 + q8 * 4 + q2 * 2, 2), :] = two
    for q7 in range(2):
        for g in range(1, out_ref.shape[1]):
            out_ref[q7, g] = out_ref[q7, 0]


def close_kernel(far_ref, coef_ref, left_ref, out_ref):
    heads = left_ref.shape[0]
    slices, _, outs, _ = coef_ref.shape
    depth = out_ref.shape[0] // slices
    first = far_ref[0] * 2
    rows = 8
    for s in range(slices):
        acc = [[None] * (depth // rows) for _ in range(2 * outs)]
        for h in range(heads):
            head = (h // 2) * 16 + first + h % 2
            co = [coef_ref[s, j // outs, j % outs, head] for j in range(2 * outs)]
            for kb in range(depth // rows):
                at = 2 * s * depth + kb * rows
                re = left_ref[h, pl.ds(at, rows), :]
                im = left_ref[h, pl.ds(at + depth, rows), :]
                for o in range(outs):
                    cre, cim = co[o], co[outs + o]
                    new_re = cre * re - cim * im
                    new_im = cre * im + cim * re
                    if h:
                        new_re, new_im = acc[o][kb] + new_re, acc[outs + o][kb] + new_im
                    acc[o][kb], acc[outs + o][kb] = new_re, new_im
        for kb in range(depth // rows):
            for j in range(2 * outs):
                out_ref[pl.ds(s * depth + kb * rows, rows), pl.ds(j * LANES, LANES)] = acc[j][kb]


def join_kernel(core_ref, right_ref, mine_ref, other_ref, out_ref, lhs, rhs):
    depth, wide = mine_ref.shape
    half = wide // 2
    first = lax.broadcasted_iota(jnp.int32, (8, LANES), 0) < 4
    for i, x_ref in enumerate((mine_ref, other_ref)):
        core = core_ref[0] ^ i
        for t in range(4):
            for q6 in range(2):
                for q0 in range(2):
                    at = pl.ds((q6 * 2 + q0) * 8, 8)
                    low, high = right_ref[core, 2 * t, at, :], right_ref[core, 2 * t + 1, at, :]
                    to = (q6 * 8 + t * 2 + q0) * 16
                    lanes = pl.ds(i * LANES, LANES)
                    lhs[pl.ds(to, 8), lanes] = jnp.where(first, low, pltpu.roll(high, 4, 0))
                    lhs[pl.ds(to + 8, 8), lanes] = jnp.where(first, pltpu.roll(low, 4, 0), high)
        rhs[pl.ds(2 * i * depth, depth), :] = x_ref[...]
        rhs[pl.ds((2 * i + 1) * depth, depth), :half] = -x_ref[:, half:]
        rhs[pl.ds((2 * i + 1) * depth, depth), half:] = x_ref[:, :half]
    for j in range(wide // LANES):
        right = rhs[:, pl.ds(j * LANES, LANES)]
        out = jnp.dot(lhs[...], right, precision=lax.Precision.HIGHEST, preferred_element_type=F32)
        out_ref[:, j, :, :] = out.reshape(16, 16, LANES)


def sum_kernel(scale, parts_ref, out_ref):
    for j in range(parts_ref.shape[1]):
        total = parts_ref[0, j]
        for i in range(1, parts_ref.shape[0]):
            total = total + parts_ref[i, j]
        out_ref[:, j, :] = total * scale


def finish_kernel(parts_ref, out_ref):
    total = parts_ref[0]
    for i in range(1, parts_ref.shape[0]):
        total = total + parts_ref[i]
    outs = out_ref.shape[0]
    for c in range(2):
        for o in range(outs):
            out_ref[o, pl.ds(c, 1), :] = total[c * outs + o : c * outs + o + 1, :]


def kernel_call(body, shape, specs, cost, name, scratch=(), vmem=16, to=VMEM):
    flops, size = cost
    return pl.pallas_call(
        body,
        out_shape=jax.ShapeDtypeStruct(shape, F32),
        in_specs=specs,
        out_specs=to,
        scratch_shapes=scratch,
        compiler_params=pltpu.CompilerParams(vmem_limit_bytes=vmem * 2**20),
        cost_estimate=pl.CostEstimate(flops=flops, bytes_accessed=size, transcendentals=0),
        name=name,
    )


def shards(left_tensor, right_tensor, closing_tensor):
    slices, _, _, depth, rows = left_tensor.shape
    width = right_tensor.shape[3]
    outs = closing_tensor.shape[3]
    near = 16
    kk = depth // near
    body = slices * 2 * kk
    here = lax.axis_index(FAR).reshape(1)

    x = kernel_call(
        pack_kernel,
        (near, body + width, LANES),
        [ANY, VMEM],
        (0, 2**21),
        "pack",
        [
            pltpu.VMEM((slices * 2, near, kk, rows), F32),
            pltpu.VMEM((near, width, LANES), F32),
            pltpu.SemaphoreType.DMA((slices * 2,)),
            pltpu.SemaphoreType.DMA((slices * 2 + 1,)),
        ],
        60,
        ANY,
    )(left_tensor.reshape(slices, 2, near, kk, rows), right_tensor.transpose(0, 1, 3, 2))

    with jax.named_scope("near_move"):
        x = lax.all_to_all(x, NEAR, 0, 0, tiled=True)

    r = kernel_call(spread_kernel, (2, 8, near * width // 2, LANES), [VMEM], (0, 2**18), "spread")(x)
    with jax.named_scope("right_move"):
        r = r.reshape(16, near * width // 2, LANES)
        r = lax.all_to_all(r, ("core", FAR), 0, 0, tiled=True)
        r = r.reshape(2, 8, near * width // 2, LANES)

    x = kernel_call(
        close_kernel,
        (slices * kk, 2 * outs * rows),
        [SMEM, SMEM, VMEM],
        (2**22, 6 * 2**18),
        "close",
    )(here, closing_tensor.transpose(0, 1, 3, 2), x)
    with jax.named_scope("core_swap"):
        y = lax.ppermute(x, "core", [(0, 1), (1, 0)])

    wide = 2 * outs * rows
    p = kernel_call(
        join_kernel,
        (near, 2 * outs, 16, rows),
        [SMEM, VMEM, VMEM, VMEM],
        (2**27, 2**21),
        "join",
        [pltpu.VMEM((256, 2 * LANES), F32), pltpu.VMEM((4 * slices * kk, wide), F32)],
    )(lax.axis_index("core").reshape(1), r, x, y)

    with jax.named_scope("sum_move"):
        p = lax.all_to_all(p, NEAR, 0, 0, tiled=True)
    p = kernel_call(
        functools.partial(sum_kernel, (slices * 4) ** -0.5),
        (16, 2 * outs, rows),
        [VMEM],
        (2**18, 2**20),
        "sum",
    )(p)

    with jax.named_scope("last_move"):
        p = lax.all_to_all(p, ("yh", FAR), 0, 0, tiled=True)
    p = kernel_call(finish_kernel, (outs, 2, rows), [VMEM], (2**14, 2**17), "finish")(p)
    return p.reshape(1, outs, 2, rows)


def solution(mesh):
    fine = Mesh(mesh.devices.reshape([n for _, n in PARTS]), [name for name, _ in PARTS])
    return jax.shard_map(
        shards,
        mesh=fine,
        in_specs=(
            P(CUTS, None, MODE, None, None),
            P(CUTS, None, None, MODE),
            P(CUTS, None, None, None),
        ),
        out_specs=P(CUTS + MODE, None, None, None),
        check_vma=False,
    )
```

```python
import functools

import jax
import jax.numpy as jnp
from jax import lax
from jax.experimental import pallas as pl
from jax.experimental.pallas import tpu as pltpu
from jax.sharding import Mesh
from jax.sharding import PartitionSpec as P

PARTS = (("yh", 2), ("core", 2), ("yl", 2), ("x", 4), ("za", 8), ("zb", 2))
CUTS = ("yh", "core")
MODE = ("yl", "x", "za", "zb")
NEAR = ("yl", "x", "zb")
FAR = "za"

F32 = jnp.float32
LANES = 128
SMEM = pl.BlockSpec(memory_space=pltpu.SMEM)
VMEM = pl.BlockSpec(memory_space=pltpu.VMEM)
ANY = pl.BlockSpec(memory_space=pl.ANY)


def swap_blocks(v):
    n = len(v)
    size = LANES // n
    block = lax.broadcasted_iota(jnp.int32, v[0].shape, 1) // size
    v = list(v)
    bit = 1
    while bit < n:
        low = (block & bit) == 0
        for i in range(n):
            if i & bit:
                continue
            a, b = v[i], v[i | bit]
            v[i] = jnp.where(low, a, pltpu.roll(b, size * bit, 1))
            v[i | bit] = jnp.where(low, pltpu.roll(a, LANES - size * bit, 1), b)
        bit *= 2
    return v


def pack_kernel(left_ref, right_ref, out_ref, held, piece, into, out_of):
    slices, _, near, depth, _ = left_ref.shape
    each = 2 * slices
    copies = []
    for i in range(each):
        copies.append(pltpu.make_async_copy(left_ref.at[i // 2, i % 2], held.at[i], into.at[i]))
        copies[-1].start()
    width = right_ref.shape[2]
    for t in range(near // each):
        lanes = pl.ds(t * LANES, LANES)
        w = swap_blocks([right_ref[j % slices, j // slices, :, lanes] for j in range(each)])
        for g in range(each):
            piece[t * each + g] = w[g]
    to = out_ref.at[:, pl.ds(each * depth, width), :]
    last = [pltpu.make_async_copy(piece, to, out_of.at[each])]
    last[0].start()
    for i in range(each):
        copies[i].wait()
        to = out_ref.at[:, pl.ds(i * depth, depth), :]
        last.append(pltpu.make_async_copy(held.at[i], to, out_of.at[i]))
        last[-1].start()
    for copy in last:
        copy.wait()


def spread_kernel(near_ref, out_ref):
    cuts, far, width, _ = out_ref.shape
    body = near_ref.shape[1] - cuts * width // near_ref.shape[0]
    for q87 in range(cuts):
        for q6 in range(2):
            for q0 in range(2):
                for q2 in range(2):
                    two = near_ref[q87 * 4 + q6 * 2 + q2, pl.ds(body + q0, 2, stride=2), :]
                    out_ref[q87, 0, pl.ds(q6 * 8 + q0 * 4 + q2 * 2, 2), :] = two
        for g in range(1, far):
            out_ref[q87, g] = out_ref[q87, 0]


def close_kernel(far_ref, coef_ref, left_ref, out_ref):
    heads = left_ref.shape[0]
    slices, _, outs, _ = coef_ref.shape
    depth = out_ref.shape[0] // slices
    first = far_ref[0] * 2
    rows = 8
    for s in range(slices):
        acc = [[None] * (depth // rows) for _ in range(2 * outs)]
        for h in range(heads):
            head = (h // 2) * 16 + first + h % 2
            co = [coef_ref[s, j // outs, j % outs, head] for j in range(2 * outs)]
            for kb in range(depth // rows):
                at = 2 * s * depth + kb * rows
                re = left_ref[h, pl.ds(at, rows), :]
                im = left_ref[h, pl.ds(at + depth, rows), :]
                for o in range(outs):
                    cre, cim = co[o], co[outs + o]
                    new_re = cre * re - cim * im
                    new_im = cre * im + cim * re
                    if h:
                        new_re, new_im = acc[o][kb] + new_re, acc[outs + o][kb] + new_im
                    acc[o][kb], acc[outs + o][kb] = new_re, new_im
        for kb in range(depth // rows):
            for j in range(2 * outs):
                out_ref[pl.ds(s * depth + kb * rows, rows), pl.ds(j * LANES, LANES)] = acc[j][kb]


def join_kernel(cut_ref, right_ref, x0_ref, x1_ref, x2_ref, x3_ref, out_ref, lhs, rhs):
    depth, wide = x0_ref.shape
    half = wide // 2
    first = lax.broadcasted_iota(jnp.int32, (8, LANES), 0) < 4
    for i, x_ref in enumerate((x0_ref, x1_ref, x2_ref, x3_ref)):
        cut = cut_ref[0] ^ i
        lanes = pl.ds(i * LANES, LANES)
        for t in range(4):
            for q6 in range(2):
                at = pl.ds(q6 * 8, 8)
                low, high = right_ref[cut, 2 * t, at, :], right_ref[cut, 2 * t + 1, at, :]
                to = (q6 * 8 + t * 2) * 8
                lhs[pl.ds(to, 8), lanes] = jnp.where(first, low, pltpu.roll(high, 4, 0))
                lhs[pl.ds(to + 8, 8), lanes] = jnp.where(first, pltpu.roll(low, 4, 0), high)
        rhs[pl.ds(2 * i * depth, depth), :] = x_ref[...]
        rhs[pl.ds((2 * i + 1) * depth, depth), :half] = -x_ref[:, half:]
        rhs[pl.ds((2 * i + 1) * depth, depth), half:] = x_ref[:, :half]
    for j in range(0, wide // LANES, 2):
        right = rhs[:, pl.ds(j * LANES, 2 * LANES)]
        out = jnp.dot(lhs[...], right, precision=lax.Precision.HIGHEST, preferred_element_type=F32)
        out_ref[:, j, :, :] = out[:, :LANES].reshape(16, 8, LANES)
        out_ref[:, j + 1, :, :] = out[:, LANES:].reshape(16, 8, LANES)


def sum_kernel(scale, parts_ref, out_ref):
    for j in range(parts_ref.shape[1]):
        total = parts_ref[0, j]
        for i in range(1, parts_ref.shape[0]):
            total = total + parts_ref[i, j]
        out_ref[:, j, :] = total * scale


def finish_kernel(parts_ref, out_ref):
    total = parts_ref[0]
    for i in range(1, parts_ref.shape[0]):
        total = total + parts_ref[i]
    outs = out_ref.shape[0]
    for c in range(2):
        for o in range(outs):
            out_ref[o, pl.ds(c, 1), :] = total[c * outs + o : c * outs + o + 1, :]


def kernel_call(body, shape, specs, cost, name, scratch=(), vmem=16, to=VMEM):
    flops, size = cost
    return pl.pallas_call(
        body,
        out_shape=jax.ShapeDtypeStruct(shape, F32),
        in_specs=specs,
        out_specs=to,
        scratch_shapes=scratch,
        compiler_params=pltpu.CompilerParams(vmem_limit_bytes=vmem * 2**20),
        cost_estimate=pl.CostEstimate(flops=flops, bytes_accessed=size, transcendentals=0),
        name=name,
    )


def shards(left_tensor, right_tensor, closing_tensor):
    slices, _, _, depth, rows = left_tensor.shape
    width = right_tensor.shape[3]
    outs = closing_tensor.shape[3]
    near = 16
    kk = depth // near
    body = slices * 2 * kk
    here = lax.axis_index(FAR).reshape(1)

    x = kernel_call(
        pack_kernel,
        (near, body + width, LANES),
        [ANY, VMEM],
        (0, 2**21),
        "pack",
        [
            pltpu.VMEM((slices * 2, near, kk, rows), F32),
            pltpu.VMEM((near, width, LANES), F32),
            pltpu.SemaphoreType.DMA((slices * 2,)),
            pltpu.SemaphoreType.DMA((slices * 2 + 1,)),
        ],
        60,
        ANY,
    )(left_tensor.reshape(slices, 2, near, kk, rows), right_tensor.transpose(0, 1, 3, 2))

    with jax.named_scope("near_move"):
        x = lax.all_to_all(x, NEAR, 0, 0, tiled=True)

    cuts = 4
    r = kernel_call(
        spread_kernel, (cuts, 8, near * width // cuts, LANES), [VMEM], (0, 2**18), "spread"
    )(x)
    with jax.named_scope("right_move"):
        r = r.reshape(cuts * 8, near * width // cuts, LANES)
        r = lax.all_to_all(r, CUTS + (FAR,), 0, 0, tiled=True)
        r = r.reshape(cuts, 8, near * width // cuts, LANES)

    x = kernel_call(
        close_kernel,
        (slices * kk, 2 * outs * rows),
        [SMEM, SMEM, VMEM],
        (2**22, 6 * 2**18),
        "close",
    )(here, closing_tensor.transpose(0, 1, 3, 2), x)
    swap = [(0, 1), (1, 0)]
    with jax.named_scope("cuts_gather"):
        x2 = lax.ppermute(x, "yh", swap)
        x1 = lax.ppermute(x, "core", swap)
        x3 = lax.ppermute(x2, "core", swap)

    wide = 2 * outs * rows
    p = kernel_call(
        join_kernel,
        (near, 2 * outs, 8, rows),
        [SMEM] + [VMEM] * 5,
        (2**27, 2**21),
        "join",
        [pltpu.VMEM((128, cuts * LANES), F32), pltpu.VMEM((2 * cuts * slices * kk, wide), F32)],
    )(lax.axis_index(CUTS).reshape(1), r, x, x1, x2, x3)

    with jax.named_scope("sum_move"):
        p = lax.all_to_all(p, NEAR, 0, 0, tiled=True)
    p = kernel_call(
        functools.partial(sum_kernel, (slices * cuts) ** -0.5),
        (8, 2 * outs, rows),
        [VMEM],
        (2**18, 2**20),
        "sum",
    )(p)

    with jax.named_scope("last_move"):
        p = lax.all_to_all(p, FAR, 0, 0, tiled=True)
    p = kernel_call(finish_kernel, (outs, 2, rows), [VMEM], (2**14, 2**17), "finish")(p)
    return p.reshape(1, outs, 2, rows)


def solution(mesh):
    fine = Mesh(mesh.devices.reshape([n for _, n in PARTS]), [name for name, _ in PARTS])
    return jax.shard_map(
        shards,
        mesh=fine,
        in_specs=(
            P(CUTS, None, MODE, None, None),
            P(CUTS, None, None, MODE),
            P(CUTS, None, None, None),
        ),
        out_specs=P(CUTS + MODE, None, None, None),
        check_vma=False,
    )
```

```python
import functools

import jax
import jax.numpy as jnp
from jax import lax
from jax.experimental import pallas as pl
from jax.experimental.pallas import tpu as pltpu
from jax.sharding import Mesh
from jax.sharding import PartitionSpec as P

PARTS = (("yh", 2), ("core", 2), ("yl", 2), ("x", 4), ("za", 8), ("zb", 2))
CUTS = ("yh", "core")
MODE = ("yl", "x", "za", "zb")
NEAR = ("yl", "x", "zb")
FAR = "za"

F32 = jnp.float32
LANES = 128
MID = 5
LAST = 4
SMEM = pl.BlockSpec(memory_space=pltpu.SMEM)
VMEM = pl.BlockSpec(memory_space=pltpu.VMEM)
ANY = pl.BlockSpec(memory_space=pl.ANY)


def swap_blocks(v):
    n = len(v)
    size = LANES // n
    block = lax.broadcasted_iota(jnp.int32, v[0].shape, 1) // size
    v = list(v)
    bit = 1
    while bit < n:
        low = (block & bit) == 0
        for i in range(n):
            if i & bit:
                continue
            a, b = v[i], v[i | bit]
            v[i] = jnp.where(low, a, pltpu.roll(b, size * bit, 1))
            v[i | bit] = jnp.where(low, pltpu.roll(a, LANES - size * bit, 1), b)
        bit *= 2
    return v


def pack_kernel(left_ref, right_ref, out_ref, held, piece, into, out_of):
    slices, _, near, depth, _ = left_ref.shape
    each = 2 * slices
    copies = []
    for i in range(each):
        copies.append(pltpu.make_async_copy(left_ref.at[i // 2, i % 2], held.at[i], into.at[i]))
        copies[-1].start()
    width = right_ref.shape[2]
    for t in range(near // each):
        lanes = pl.ds(t * LANES, LANES)
        w = swap_blocks([right_ref[j % slices, j // slices, :, lanes] for j in range(each)])
        for g in range(each):
            piece[t * each + g] = w[g]
    to = out_ref.at[:, pl.ds(each * depth, width), :]
    last = [pltpu.make_async_copy(piece, to, out_of.at[each])]
    last[0].start()
    for i in range(each):
        copies[i].wait()
        to = out_ref.at[:, pl.ds(i * depth, depth), :]
        last.append(pltpu.make_async_copy(held.at[i], to, out_of.at[i]))
        last[-1].start()
    for copy in last:
        copy.wait()


def spread_kernel(near_ref, out_ref):
    cuts, far, width, _ = out_ref.shape
    body = near_ref.shape[1] - cuts * width // near_ref.shape[0]
    for q87 in range(cuts):
        for q6 in range(2):
            for q0 in range(2):
                for q2 in range(2):
                    two = near_ref[q87 * 4 + q6 * 2 + q2, pl.ds(body + q0, 2, stride=2), :]
                    out_ref[q87, 0, pl.ds(q6 * 8 + q0 * 4 + q2 * 2, 2), :] = two
        for g in range(1, far):
            out_ref[q87, g] = out_ref[q87, 0]


def close_kernel(far_ref, coef_ref, left_ref, out_ref):
    heads = left_ref.shape[0]
    slices, _, outs, _ = coef_ref.shape
    depth = out_ref.shape[0] // slices
    first = far_ref[0] * 2
    rows = 8
    for s in range(slices):
        acc = [[None] * (depth // rows) for _ in range(2 * outs)]
        for h in range(heads):
            head = (h // 2) * 16 + first + h % 2
            co = [coef_ref[s, j // outs, j % outs, head] for j in range(2 * outs)]
            for kb in range(depth // rows):
                at = 2 * s * depth + kb * rows
                re = left_ref[h, pl.ds(at, rows), :]
                im = left_ref[h, pl.ds(at + depth, rows), :]
                for o in range(outs):
                    cre, cim = co[o], co[outs + o]
                    new_re = cre * re - cim * im
                    new_im = cre * im + cim * re
                    if h:
                        new_re, new_im = acc[o][kb] + new_re, acc[outs + o][kb] + new_im
                    acc[o][kb], acc[outs + o][kb] = new_re, new_im
        for kb in range(depth // rows):
            for j in range(2 * outs):
                out_ref[pl.ds(s * depth + kb * rows, rows), pl.ds(j * LANES, LANES)] = acc[j][kb]


def join_kernel(cut_ref, right_ref, x0_ref, x1_ref, x2_ref, x3_ref, out_ref, lhs, rhs):
    depth, wide = x0_ref.shape
    half = wide // 2
    first = lax.broadcasted_iota(jnp.int32, (8, LANES), 0) < 4
    for i, x_ref in enumerate((x0_ref, x1_ref, x2_ref, x3_ref)):
        cut = cut_ref[0] ^ i
        lanes = pl.ds(i * LANES, LANES)
        for t in range(4):
            for q6 in range(2):
                at = pl.ds(q6 * 8, 8)
                low = right_ref[cut, (2 * t - MID) % 8, at, :]
                high = right_ref[cut, (2 * t + 1 - MID) % 8, at, :]
                to = (q6 * 8 + t * 2) * 8
                lhs[pl.ds(to, 8), lanes] = jnp.where(first, low, pltpu.roll(high, 4, 0))
                lhs[pl.ds(to + 8, 8), lanes] = jnp.where(first, pltpu.roll(low, 4, 0), high)
        rhs[pl.ds(2 * i * depth, depth), :] = x_ref[...]
        rhs[pl.ds((2 * i + 1) * depth, depth), :half] = -x_ref[:, half:]
        rhs[pl.ds((2 * i + 1) * depth, depth), half:] = x_ref[:, :half]
    for j in range(0, wide // LANES, 2):
        right = rhs[:, pl.ds(j * LANES, 2 * LANES)]
        out = jnp.dot(lhs[...], right, precision=lax.Precision.HIGHEST, preferred_element_type=F32)
        out_ref[:, j, :, :] = out[:, :LANES].reshape(16, 8, LANES)
        out_ref[:, j + 1, :, :] = out[:, LANES:].reshape(16, 8, LANES)


def sum_kernel(scale, parts_ref, out_ref):
    for j in range(parts_ref.shape[1]):
        total = parts_ref[0, j]
        for i in range(1, parts_ref.shape[0]):
            total = total + parts_ref[i, j]
        out_ref[:, j, :] = pltpu.roll(total * scale, (8 - LAST) % 8, 0)


def finish_kernel(parts_ref, out_ref):
    total = parts_ref[0]
    for i in range(1, parts_ref.shape[0]):
        total = total + parts_ref[i]
    outs = out_ref.shape[0]
    for c in range(2):
        for o in range(outs):
            out_ref[o, pl.ds(c, 1), :] = total[c * outs + o : c * outs + o + 1, :]


def kernel_call(body, shape, specs, cost, name, scratch=(), vmem=16, to=VMEM):
    flops, size = cost
    return pl.pallas_call(
        body,
        out_shape=jax.ShapeDtypeStruct(shape, F32),
        in_specs=specs,
        out_specs=to,
        scratch_shapes=scratch,
        compiler_params=pltpu.CompilerParams(vmem_limit_bytes=vmem * 2**20),
        cost_estimate=pl.CostEstimate(flops=flops, bytes_accessed=size, transcendentals=0),
        name=name,
    )


def shards(left_tensor, right_tensor, closing_tensor):
    slices, _, _, depth, rows = left_tensor.shape
    width = right_tensor.shape[3]
    outs = closing_tensor.shape[3]
    near = 16
    kk = depth // near
    body = slices * 2 * kk
    here = lax.axis_index(FAR).reshape(1)

    x = kernel_call(
        pack_kernel,
        (near, body + width, LANES),
        [ANY, VMEM],
        (0, 2**21),
        "pack",
        [
            pltpu.VMEM((slices * 2, near, kk, rows), F32),
            pltpu.VMEM((near, width, LANES), F32),
            pltpu.SemaphoreType.DMA((slices * 2,)),
            pltpu.SemaphoreType.DMA((slices * 2 + 1,)),
        ],
        60,
        ANY,
    )(left_tensor.reshape(slices, 2, near, kk, rows), right_tensor.transpose(0, 1, 3, 2))

    with jax.named_scope("near_move"):
        x = lax.all_to_all(x, NEAR, 0, 0, tiled=True)

    cuts = 4
    r = kernel_call(
        spread_kernel, (cuts, 8, near * width // cuts, LANES), [VMEM], (0, 2**18), "spread"
    )(x)
    with jax.named_scope("right_move"):
        r = r.reshape(cuts * 8, near * width // cuts, LANES)
        group = [c * 8 + (f + MID) % 8 for c in range(cuts) for f in range(8)]
        r = lax.all_to_all(r, CUTS + (FAR,), 0, 0, tiled=True, axis_index_groups=[group])
        r = r.reshape(cuts, 8, near * width // cuts, LANES)

    x = kernel_call(
        close_kernel,
        (slices * kk, 2 * outs * rows),
        [SMEM, SMEM, VMEM],
        (2**22, 6 * 2**18),
        "close",
    )(here, closing_tensor.transpose(0, 1, 3, 2), x)
    swap = [(0, 1), (1, 0)]
    with jax.named_scope("cuts_gather"):
        x2 = lax.ppermute(x, "yh", swap)
        x1 = lax.ppermute(x, "core", swap)
        x3 = lax.ppermute(x2, "core", swap)

    wide = 2 * outs * rows
    p = kernel_call(
        join_kernel,
        (near, 2 * outs, 8, rows),
        [SMEM] + [VMEM] * 5,
        (2**27, 2**21),
        "join",
        [pltpu.VMEM((128, cuts * LANES), F32), pltpu.VMEM((2 * cuts * slices * kk, wide), F32)],
    )(lax.axis_index(CUTS).reshape(1), r, x, x1, x2, x3)

    with jax.named_scope("sum_move"):
        p = lax.all_to_all(p, NEAR, 0, 0, tiled=True)
    p = kernel_call(
        functools.partial(sum_kernel, (slices * cuts) ** -0.5),
        (8, 2 * outs, rows),
        [VMEM],
        (2**18, 2**20),
        "sum",
    )(p)

    with jax.named_scope("last_move"):
        group = [(f + LAST) % 8 for f in range(8)]
        p = lax.all_to_all(p, FAR, 0, 0, tiled=True, axis_index_groups=[group])
    p = kernel_call(finish_kernel, (outs, 2, rows), [VMEM], (2**14, 2**17), "finish")(p)
    return p.reshape(1, outs, 2, rows)


def solution(mesh):
    fine = Mesh(mesh.devices.reshape([n for _, n in PARTS]), [name for name, _ in PARTS])
    return jax.shard_map(
        shards,
        mesh=fine,
        in_specs=(
            P(CUTS, None, MODE, None, None),
            P(CUTS, None, None, MODE),
            P(CUTS, None, None, None),
        ),
        out_specs=P(CUTS + MODE, None, None, None),
        check_vma=False,
    )
```

```python
import functools

import jax
import jax.numpy as jnp
from jax import lax
from jax.experimental import pallas as pl
from jax.experimental.pallas import tpu as pltpu
from jax.sharding import Mesh
from jax.sharding import PartitionSpec as P

PARTS = (("yh", 2), ("core", 2), ("yl", 2), ("x", 4), ("za", 8), ("zb", 2))
CUTS = ("yh", "core")
MODE = ("yl", "x", "za", "zb")
NEAR = ("yl", "x", "zb")
FAR = "za"

F32 = jnp.float32
LANES = 128
MID = 7
LAST = 4
SMEM = pl.BlockSpec(memory_space=pltpu.SMEM)
VMEM = pl.BlockSpec(memory_space=pltpu.VMEM)
ANY = pl.BlockSpec(memory_space=pl.ANY)


def swap_blocks(v):
    n = len(v)
    size = LANES // n
    block = lax.broadcasted_iota(jnp.int32, v[0].shape, 1) // size
    v = list(v)
    bit = 1
    while bit < n:
        low = (block & bit) == 0
        for i in range(n):
            if i & bit:
                continue
            a, b = v[i], v[i | bit]
            v[i] = jnp.where(low, a, pltpu.roll(b, size * bit, 1))
            v[i | bit] = jnp.where(low, pltpu.roll(a, LANES - size * bit, 1), b)
        bit *= 2
    return v


def pack_kernel(left_ref, right_ref, out_ref, held, right, piece, into, out_of):
    slices, _, near, depth, _ = left_ref.shape
    each = 2 * slices
    halves = [pl.ds(0, near // 2), pl.ds(near // 2, near // 2)]
    parts = [(i, half) for half in halves for i in range(each)]
    copies = []
    for n, (i, half) in enumerate(parts):
        copies.append(pltpu.make_async_copy(left_ref.at[i // 2, i % 2, half], held.at[i, half], into.at[n]))
        copies[-1].start()
    given = pltpu.make_async_copy(right_ref, right, into.at[len(parts)])
    given.start()
    last = []
    for n, (i, half) in enumerate(parts):
        copies[n].wait()
        to = out_ref.at[half, pl.ds(i * depth, depth), :]
        last.append(pltpu.make_async_copy(held.at[i, half], to, out_of.at[n]))
        last[-1].start()
    given.wait()
    width = right.shape[2]
    for t in range(near // each):
        lanes = pl.ds(t * LANES, LANES)
        w = swap_blocks([right[j % slices, j // slices, :, lanes] for j in range(each)])
        for g in range(each):
            piece[t * each + g] = w[g]
    to = out_ref.at[:, pl.ds(each * depth, width), :]
    last.append(pltpu.make_async_copy(piece, to, out_of.at[len(parts)]))
    last[-1].start()
    for copy in last:
        copy.wait()


def spread_kernel(near_ref, out_ref):
    cuts, far, width, _ = out_ref.shape
    body = near_ref.shape[1] - cuts * width // near_ref.shape[0]
    for q87 in range(cuts):
        for q6 in range(2):
            for q0 in range(2):
                for q2 in range(2):
                    two = near_ref[q87 * 4 + q6 * 2 + q2, pl.ds(body + q0, 2, stride=2), :]
                    out_ref[q87, 0, pl.ds(q6 * 8 + q0 * 4 + q2 * 2, 2), :] = two
        for g in range(1, far):
            out_ref[q87, g] = out_ref[q87, 0]


def close_kernel(far_ref, coef_ref, left_ref, out_ref):
    heads = left_ref.shape[0]
    slices, _, outs, _ = coef_ref.shape
    depth = out_ref.shape[0] // slices
    first = far_ref[0] * 2
    rows = 8
    for s in range(slices):
        acc = [[None] * (depth // rows) for _ in range(2 * outs)]
        for h in range(heads):
            head = (h // 2) * 16 + first + h % 2
            co = [coef_ref[s, j // outs, j % outs, head] for j in range(2 * outs)]
            for kb in range(depth // rows):
                at = 2 * s * depth + kb * rows
                re = left_ref[h, pl.ds(at, rows), :]
                im = left_ref[h, pl.ds(at + depth, rows), :]
                for o in range(outs):
                    cre, cim = co[o], co[outs + o]
                    new_re = cre * re - cim * im
                    new_im = cre * im + cim * re
                    if h:
                        new_re, new_im = acc[o][kb] + new_re, acc[outs + o][kb] + new_im
                    acc[o][kb], acc[outs + o][kb] = new_re, new_im
        for kb in range(depth // rows):
            for j in range(2 * outs):
                out_ref[pl.ds(s * depth + kb * rows, rows), pl.ds(j * LANES, LANES)] = acc[j][kb]


def join_kernel(cut_ref, right_ref, x0_ref, x1_ref, x2_ref, x3_ref, out_ref, lhs, rhs):
    depth, wide = x0_ref.shape
    half = wide // 2
    first = lax.broadcasted_iota(jnp.int32, (8, LANES), 0) < 4
    for i, x_ref in enumerate((x0_ref, x1_ref, x2_ref, x3_ref)):
        cut = cut_ref[0] ^ i
        lanes = pl.ds(i * LANES, LANES)
        for t in range(4):
            for q6 in range(2):
                at = pl.ds(q6 * 8, 8)
                low = right_ref[cut, (2 * t - MID) % 8, at, :]
                high = right_ref[cut, (2 * t + 1 - MID) % 8, at, :]
                to = (q6 * 8 + t * 2) * 8
                lhs[pl.ds(to, 8), lanes] = jnp.where(first, low, pltpu.roll(high, 4, 0))
                lhs[pl.ds(to + 8, 8), lanes] = jnp.where(first, pltpu.roll(low, 4, 0), high)
        rhs[pl.ds(2 * i * depth, depth), :] = x_ref[...]
        rhs[pl.ds((2 * i + 1) * depth, depth), :half] = -x_ref[:, half:]
        rhs[pl.ds((2 * i + 1) * depth, depth), half:] = x_ref[:, :half]
    for j in range(0, wide // LANES, 2):
        right = rhs[:, pl.ds(j * LANES, 2 * LANES)]
        out = jnp.dot(lhs[...], right, precision=lax.Precision.HIGHEST, preferred_element_type=F32)
        out_ref[:, j, :, :] = out[:, :LANES].reshape(16, 8, LANES)
        out_ref[:, j + 1, :, :] = out[:, LANES:].reshape(16, 8, LANES)


def sum_kernel(scale, parts_ref, out_ref):
    for j in range(parts_ref.shape[1]):
        total = parts_ref[0, j]
        for i in range(1, parts_ref.shape[0]):
            total = total + parts_ref[i, j]
        out_ref[:, j, :] = pltpu.roll(total * scale, (8 - LAST) % 8, 0)


def finish_kernel(parts_ref, out_ref):
    total = parts_ref[0]
    for i in range(1, parts_ref.shape[0]):
        total = total + parts_ref[i]
    outs = out_ref.shape[0]
    for c in range(2):
        for o in range(outs):
            out_ref[o, pl.ds(c, 1), :] = total[c * outs + o : c * outs + o + 1, :]


def kernel_call(body, shape, specs, cost, name, scratch=(), vmem=16, to=VMEM):
    flops, size = cost
    return pl.pallas_call(
        body,
        out_shape=jax.ShapeDtypeStruct(shape, F32),
        in_specs=specs,
        out_specs=to,
        scratch_shapes=scratch,
        compiler_params=pltpu.CompilerParams(vmem_limit_bytes=vmem * 2**20),
        cost_estimate=pl.CostEstimate(flops=flops, bytes_accessed=size, transcendentals=0),
        name=name,
    )


def shards(left_tensor, right_tensor, closing_tensor):
    slices, _, _, depth, rows = left_tensor.shape
    width = right_tensor.shape[3]
    outs = closing_tensor.shape[3]
    near = 16
    kk = depth // near
    body = slices * 2 * kk
    here = lax.axis_index(FAR).reshape(1)

    x = kernel_call(
        pack_kernel,
        (near, body + width, LANES),
        [ANY, ANY],
        (0, 2**21),
        "pack",
        [
            pltpu.VMEM((slices * 2, near, kk, rows), F32),
            pltpu.VMEM((slices, 2, width, depth), F32),
            pltpu.VMEM((near, width, LANES), F32),
            pltpu.SemaphoreType.DMA((slices * 4 + 1,)),
            pltpu.SemaphoreType.DMA((slices * 4 + 1,)),
        ],
        60,
        ANY,
    )(left_tensor.reshape(slices, 2, near, kk, rows), right_tensor.transpose(0, 1, 3, 2))

    with jax.named_scope("near_move"):
        x = lax.all_to_all(x, NEAR, 0, 0, tiled=True)

    cuts = 4
    r = kernel_call(
        spread_kernel, (cuts, 8, near * width // cuts, LANES), [VMEM], (0, 2**18), "spread"
    )(x)
    with jax.named_scope("right_move"):
        r = r.reshape(cuts * 8, near * width // cuts, LANES)
        group = [c * 8 + (f + MID) % 8 for c in range(cuts) for f in range(8)]
        r = lax.all_to_all(r, CUTS + (FAR,), 0, 0, tiled=True, axis_index_groups=[group])
        r = r.reshape(cuts, 8, near * width // cuts, LANES)

    x = kernel_call(
        close_kernel,
        (slices * kk, 2 * outs * rows),
        [SMEM, SMEM, VMEM],
        (2**22, 6 * 2**18),
        "close",
    )(here, closing_tensor.transpose(0, 1, 3, 2), x)
    swap = [(0, 1), (1, 0)]
    with jax.named_scope("cuts_gather"):
        x2 = lax.ppermute(x, "yh", swap)
        x1 = lax.ppermute(x, "core", swap)
        x3 = lax.ppermute(x2, "core", swap)

    wide = 2 * outs * rows
    p = kernel_call(
        join_kernel,
        (near, 2 * outs, 8, rows),
        [SMEM] + [VMEM] * 5,
        (2**27, 2**21),
        "join",
        [pltpu.VMEM((128, cuts * LANES), F32), pltpu.VMEM((2 * cuts * slices * kk, wide), F32)],
    )(lax.axis_index(CUTS).reshape(1), r, x, x1, x2, x3)

    with jax.named_scope("sum_move"):
        p = lax.all_to_all(p, NEAR, 0, 0, tiled=True)
    p = kernel_call(
        functools.partial(sum_kernel, (slices * cuts) ** -0.5),
        (8, 2 * outs, rows),
        [VMEM],
        (2**18, 2**20),
        "sum",
    )(p)

    with jax.named_scope("last_move"):
        group = [(f + LAST) % 8 for f in range(8)]
        p = lax.all_to_all(p, FAR, 0, 0, tiled=True, axis_index_groups=[group])
    p = kernel_call(finish_kernel, (outs, 2, rows), [VMEM], (2**14, 2**17), "finish")(p)
    return p.reshape(1, outs, 2, rows)


def solution(mesh):
    fine = Mesh(mesh.devices.reshape([n for _, n in PARTS]), [name for name, _ in PARTS])
    return jax.shard_map(
        shards,
        mesh=fine,
        in_specs=(
            P(CUTS, None, MODE, None, None),
            P(CUTS, None, None, MODE),
            P(CUTS, None, None, None),
        ),
        out_specs=P(CUTS + MODE, None, None, None),
        check_vma=False,
    )
```

```python
import functools

import jax
import jax.numpy as jnp
from jax import lax
from jax.experimental import pallas as pl
from jax.experimental.pallas import tpu as pltpu
from jax.sharding import Mesh
from jax.sharding import PartitionSpec as P

PARTS = (("yh", 2), ("core", 2), ("yl", 2), ("x", 4), ("za", 8), ("zb", 2))
CUTS = ("yh", "core")
MODE = ("yl", "x", "za", "zb")
NEAR = ("yl", "x", "zb")
FAR = "za"

F32 = jnp.float32
LANES = 128
MID = 5
LAST = 4
ORDER = [yl * 8 + x * 2 + zb for x in (0, 2, 1, 3) for yl in range(2) for zb in range(2)]
SMEM = pl.BlockSpec(memory_space=pltpu.SMEM)
VMEM = pl.BlockSpec(memory_space=pltpu.VMEM)
ANY = pl.BlockSpec(memory_space=pl.ANY)


def swap_blocks(v):
    n = len(v)
    size = LANES // n
    block = lax.broadcasted_iota(jnp.int32, v[0].shape, 1) // size
    v = list(v)
    bit = 1
    while bit < n:
        low = (block & bit) == 0
        for i in range(n):
            if i & bit:
                continue
            a, b = v[i], v[i | bit]
            v[i] = jnp.where(low, a, pltpu.roll(b, size * bit, 1))
            v[i | bit] = jnp.where(low, pltpu.roll(a, LANES - size * bit, 1), b)
        bit *= 2
    return v


def pack_kernel(left_ref, right_ref, out_ref, held, right, piece, into, out_of):
    slices, _, near, depth, _ = left_ref.shape
    each = 2 * slices
    halves = [pl.ds(0, near // 2), pl.ds(near // 2, near // 2)]
    parts = [(i, half) for half in halves for i in range(each)]
    copies = []
    for n, (i, half) in enumerate(parts):
        copies.append(pltpu.make_async_copy(left_ref.at[i // 2, i % 2, half], held.at[i, half], into.at[n]))
        copies[-1].start()
    given = pltpu.make_async_copy(right_ref, right, into.at[len(parts)])
    given.start()
    last = []
    for n, (i, half) in enumerate(parts):
        copies[n].wait()
        to = out_ref.at[half, pl.ds(i * depth, depth), :]
        last.append(pltpu.make_async_copy(held.at[i, half], to, out_of.at[n]))
        last[-1].start()
    given.wait()
    width = right.shape[2]
    for t in range(near // each):
        lanes = pl.ds(t * LANES, LANES)
        w = swap_blocks([right[j % slices, j // slices, :, lanes] for j in range(each)])
        for g in range(each):
            piece[t * each + g] = w[g]
    to = out_ref.at[:, pl.ds(each * depth, width), :]
    last.append(pltpu.make_async_copy(piece, to, out_of.at[len(parts)]))
    last[-1].start()
    for copy in last:
        copy.wait()


def spread_kernel(near_ref, out_ref):
    cuts, far, width, _ = out_ref.shape
    body = near_ref.shape[1] - cuts * width // near_ref.shape[0]
    for q87 in range(cuts):
        for q6 in range(2):
            for q0 in range(2):
                for q2 in range(2):
                    two = near_ref[ORDER.index(q87 * 4 + q6 * 2 + q2), pl.ds(body + q0, 2, stride=2), :]
                    out_ref[q87, 0, pl.ds(q6 * 8 + q0 * 4 + q2 * 2, 2), :] = two
        for g in range(1, far):
            out_ref[q87, g] = out_ref[q87, 0]


def close_kernel(far_ref, coef_ref, left_ref, out_ref):
    heads = left_ref.shape[0]
    slices, _, outs, _ = coef_ref.shape
    depth = out_ref.shape[0] // slices
    first = far_ref[0] * 2
    rows = 8
    for s in range(slices):
        acc = [[None] * (depth // rows) for _ in range(2 * outs)]
        for h in range(heads):
            head = (ORDER[h] // 2) * 16 + first + ORDER[h] % 2
            co = [coef_ref[s, j // outs, j % outs, head] for j in range(2 * outs)]
            for kb in range(depth // rows):
                at = 2 * s * depth + kb * rows
                re = left_ref[h, pl.ds(at, rows), :]
                im = left_ref[h, pl.ds(at + depth, rows), :]
                for o in range(outs):
                    cre, cim = co[o], co[outs + o]
                    new_re = cre * re - cim * im
                    new_im = cre * im + cim * re
                    if h:
                        new_re, new_im = acc[o][kb] + new_re, acc[outs + o][kb] + new_im
                    acc[o][kb], acc[outs + o][kb] = new_re, new_im
        for kb in range(depth // rows):
            for j in range(2 * outs):
                out_ref[pl.ds(s * depth + kb * rows, rows), pl.ds(j * LANES, LANES)] = acc[j][kb]


def join_kernel(cut_ref, right_ref, x0_ref, x1_ref, x2_ref, x3_ref, out_ref, lhs, rhs):
    depth, wide = x0_ref.shape
    half = wide // 2
    first = lax.broadcasted_iota(jnp.int32, (8, LANES), 0) < 4
    for i, x_ref in enumerate((x0_ref, x1_ref, x2_ref, x3_ref)):
        cut = cut_ref[0] ^ i
        lanes = pl.ds(i * LANES, LANES)
        for t in range(4):
            for q6 in range(2):
                at = pl.ds(q6 * 8, 8)
                low = right_ref[cut, (2 * t - MID) % 8, at, :]
                high = right_ref[cut, (2 * t + 1 - MID) % 8, at, :]
                to = (q6 * 8 + t * 2) * 8
                lhs[pl.ds(to, 8), lanes] = jnp.where(first, low, pltpu.roll(high, 4, 0))
                lhs[pl.ds(to + 8, 8), lanes] = jnp.where(first, pltpu.roll(low, 4, 0), high)
        rhs[pl.ds(2 * i * depth, depth), :] = x_ref[...]
        rhs[pl.ds((2 * i + 1) * depth, depth), :half] = -x_ref[:, half:]
        rhs[pl.ds((2 * i + 1) * depth, depth), half:] = x_ref[:, :half]
    for j in range(0, wide // LANES, 2):
        right = rhs[:, pl.ds(j * LANES, 2 * LANES)]
        out = jnp.dot(lhs[...], right, precision=lax.Precision.HIGHEST, preferred_element_type=F32)
        out_ref[:, j, :, :] = out[:, :LANES].reshape(16, 8, LANES)
        out_ref[:, j + 1, :, :] = out[:, LANES:].reshape(16, 8, LANES)


def sum_kernel(scale, parts_ref, out_ref):
    for j in range(parts_ref.shape[1]):
        total = parts_ref[0, j]
        for i in range(1, parts_ref.shape[0]):
            total = total + parts_ref[i, j]
        out_ref[:, j, :] = pltpu.roll(total * scale, (8 - LAST) % 8, 0)


def finish_kernel(parts_ref, out_ref):
    total = parts_ref[0]
    for i in range(1, parts_ref.shape[0]):
        total = total + parts_ref[i]
    outs = out_ref.shape[0]
    for c in range(2):
        for o in range(outs):
            out_ref[o, pl.ds(c, 1), :] = total[c * outs + o : c * outs + o + 1, :]


def kernel_call(body, shape, specs, cost, name, scratch=(), vmem=16, to=VMEM):
    flops, size = cost
    return pl.pallas_call(
        body,
        out_shape=jax.ShapeDtypeStruct(shape, F32),
        in_specs=specs,
        out_specs=to,
        scratch_shapes=scratch,
        compiler_params=pltpu.CompilerParams(vmem_limit_bytes=vmem * 2**20),
        cost_estimate=pl.CostEstimate(flops=flops, bytes_accessed=size, transcendentals=0),
        name=name,
    )


def shards(left_tensor, right_tensor, closing_tensor):
    slices, _, _, depth, rows = left_tensor.shape
    width = right_tensor.shape[3]
    outs = closing_tensor.shape[3]
    near = 16
    kk = depth // near
    body = slices * 2 * kk
    here = lax.axis_index(FAR).reshape(1)

    x = kernel_call(
        pack_kernel,
        (near, body + width, LANES),
        [ANY, ANY],
        (0, 2**21),
        "pack",
        [
            pltpu.VMEM((slices * 2, near, kk, rows), F32),
            pltpu.VMEM((slices, 2, width, depth), F32),
            pltpu.VMEM((near, width, LANES), F32),
            pltpu.SemaphoreType.DMA((slices * 4 + 1,)),
            pltpu.SemaphoreType.DMA((slices * 4 + 1,)),
        ],
        60,
        ANY,
    )(left_tensor.reshape(slices, 2, near, kk, rows), right_tensor.transpose(0, 1, 3, 2))

    with jax.named_scope("near_move"):
        x = lax.all_to_all(x, NEAR, 0, 0, tiled=True, axis_index_groups=[ORDER])

    cuts = 4
    r = kernel_call(
        spread_kernel, (cuts, 8, near * width // cuts, LANES), [VMEM], (0, 2**18), "spread"
    )(x)
    with jax.named_scope("right_move"):
        r = r.reshape(cuts * 8, near * width // cuts, LANES)
        group = [c * 8 + (f + MID) % 8 for c in range(cuts) for f in range(8)]
        r = lax.all_to_all(r, CUTS + (FAR,), 0, 0, tiled=True, axis_index_groups=[group])
        r = r.reshape(cuts, 8, near * width // cuts, LANES)

    x = kernel_call(
        close_kernel,
        (slices * kk, 2 * outs * rows),
        [SMEM, SMEM, VMEM],
        (2**22, 6 * 2**18),
        "close",
    )(here, closing_tensor.transpose(0, 1, 3, 2), x)
    swap = [(0, 1), (1, 0)]
    with jax.named_scope("cuts_gather"):
        x2 = lax.ppermute(x, "yh", swap)
        x1 = lax.ppermute(x, "core", swap)
        x3 = lax.ppermute(x2, "core", swap)

    wide = 2 * outs * rows
    p = kernel_call(
        join_kernel,
        (near, 2 * outs, 8, rows),
        [SMEM] + [VMEM] * 5,
        (2**27, 2**21),
        "join",
        [pltpu.VMEM((128, cuts * LANES), F32), pltpu.VMEM((2 * cuts * slices * kk, wide), F32)],
    )(lax.axis_index(CUTS).reshape(1), r, x, x1, x2, x3)

    with jax.named_scope("sum_move"):
        p = lax.all_to_all(p, NEAR, 0, 0, tiled=True)
    p = kernel_call(
        functools.partial(sum_kernel, (slices * cuts) ** -0.5),
        (8, 2 * outs, rows),
        [VMEM],
        (2**18, 2**20),
        "sum",
    )(p)

    with jax.named_scope("last_move"):
        group = [(f + LAST) % 8 for f in range(8)]
        p = lax.all_to_all(p, FAR, 0, 0, tiled=True, axis_index_groups=[group])
    p = kernel_call(finish_kernel, (outs, 2, rows), [VMEM], (2**14, 2**17), "finish")(p)
    return p.reshape(1, outs, 2, rows)


def solution(mesh):
    fine = Mesh(mesh.devices.reshape([n for _, n in PARTS]), [name for name, _ in PARTS])
    return jax.shard_map(
        shards,
        mesh=fine,
        in_specs=(
            P(CUTS, None, MODE, None, None),
            P(CUTS, None, None, MODE),
            P(CUTS, None, None, None),
        ),
        out_specs=P(CUTS + MODE, None, None, None),
        check_vma=False,
    )
```

```python
import functools

import jax
import jax.numpy as jnp
from jax import lax
from jax.experimental import pallas as pl
from jax.experimental.pallas import tpu as pltpu
from jax.sharding import Mesh
from jax.sharding import PartitionSpec as P

PARTS = (("yh", 2), ("core", 2), ("yl", 2), ("x", 4), ("za", 8), ("zb", 2))
CUTS = ("yh", "core")
MODE = ("yl", "x", "za", "zb")
NEAR = ("yl", "x", "zb")
FAR = "za"

F32 = jnp.float32
LANES = 128
MID = 5
LAST = 4
ORDER = [yl * 8 + x * 2 + zb for x in (0, 2, 1, 3) for yl in range(2) for zb in range(2)]
SMEM = pl.BlockSpec(memory_space=pltpu.SMEM)
VMEM = pl.BlockSpec(memory_space=pltpu.VMEM)
ANY = pl.BlockSpec(memory_space=pl.ANY)


def swap_blocks(v):
    n = len(v)
    size = LANES // n
    block = lax.broadcasted_iota(jnp.int32, v[0].shape, 1) // size
    v = list(v)
    bit = 1
    while bit < n:
        low = (block & bit) == 0
        for i in range(n):
            if i & bit:
                continue
            a, b = v[i], v[i | bit]
            v[i] = jnp.where(low, a, pltpu.roll(b, size * bit, 1))
            v[i | bit] = jnp.where(low, pltpu.roll(a, LANES - size * bit, 1), b)
        bit *= 2
    return v


def pack_kernel(left_ref, right_ref, out_ref, held, right, piece, into, out_of):
    slices, _, near, depth, _ = left_ref.shape
    each = 2 * slices
    halves = [pl.ds(0, near // 2), pl.ds(near // 2, near // 2)]
    parts = [(i, half) for half in halves for i in range(each)]
    copies = []
    for n, (i, half) in enumerate(parts):
        copies.append(pltpu.make_async_copy(left_ref.at[i // 2, i % 2, half], held.at[i, half], into.at[n]))
        copies[-1].start()
    given = pltpu.make_async_copy(right_ref, right, into.at[len(parts)])
    given.start()
    last = []
    for n, (i, half) in enumerate(parts):
        copies[n].wait()
        to = out_ref.at[half, pl.ds(i * depth, depth), :]
        last.append(pltpu.make_async_copy(held.at[i, half], to, out_of.at[n]))
        last[-1].start()
    given.wait()
    width = right.shape[2]
    for t in range(near // each):
        lanes = pl.ds(t * LANES, LANES)
        w = swap_blocks([right[j % slices, j // slices, :, lanes] for j in range(each)])
        for g in range(each):
            piece[t * each + g] = w[g]
    to = out_ref.at[:, pl.ds(each * depth, width), :]
    last.append(pltpu.make_async_copy(piece, to, out_of.at[len(parts)]))
    last[-1].start()
    for copy in last:
        copy.wait()


def spread_kernel(near_ref, out_ref):
    heads = near_ref.shape[0]
    body = near_ref.shape[1] - out_ref.shape[2] * 2 // heads
    for q7 in range(2):
        for q6 in range(2):
            for q0 in range(2):
                for q8 in range(2):
                    for q2 in range(2):
                        two = near_ref[ORDER.index(q8 * 8 + q7 * 4 + q6 * 2 + q2), pl.ds(body + q0, 2, stride=2), :]
                        out_ref[q7, 0, pl.ds(q6 * 16 + q0 * 8 + q8 * 4 + q2 * 2, 2), :] = two
    for q7 in range(2):
        for g in range(1, out_ref.shape[1]):
            out_ref[q7, g] = out_ref[q7, 0]


def close_kernel(far_ref, coef_ref, left_ref, out_ref):
    heads = left_ref.shape[0]
    slices, _, outs, _ = coef_ref.shape
    depth = out_ref.shape[0] // slices
    first = far_ref[0] * 2
    rows = 8
    for s in range(slices):
        acc = [[None] * (depth // rows) for _ in range(2 * outs)]
        for h in range(heads):
            head = (ORDER[h] // 2) * 16 + first + ORDER[h] % 2
            co = [coef_ref[s, j // outs, j % outs, head] for j in range(2 * outs)]
            for kb in range(depth // rows):
                at = 2 * s * depth + kb * rows
                re = left_ref[h, pl.ds(at, rows), :]
                im = left_ref[h, pl.ds(at + depth, rows), :]
                for o in range(outs):
                    cre, cim = co[o], co[outs + o]
                    new_re = cre * re - cim * im
                    new_im = cre * im + cim * re
                    if h:
                        new_re, new_im = acc[o][kb] + new_re, acc[outs + o][kb] + new_im
                    acc[o][kb], acc[outs + o][kb] = new_re, new_im
        for kb in range(depth // rows):
            for j in range(2 * outs):
                out_ref[pl.ds(s * depth + kb * rows, rows), pl.ds(j * LANES, LANES)] = acc[j][kb]


def join_kernel(core_ref, right_ref, mine_ref, other_ref, out_ref, lhs, rhs):
    depth, wide = mine_ref.shape
    half = wide // 2
    first = lax.broadcasted_iota(jnp.int32, (8, LANES), 0) < 4
    for i, x_ref in enumerate((mine_ref, other_ref)):
        core = core_ref[0] ^ i
        for t in range(4):
            for q6 in range(2):
                for q0 in range(2):
                    at = pl.ds((q6 * 2 + q0) * 8, 8)
                    low = right_ref[core, (2 * t - MID) % 8, at, :]
                    high = right_ref[core, (2 * t + 1 - MID) % 8, at, :]
                    to = (q6 * 8 + t * 2 + q0) * 16
                    lanes = pl.ds(i * LANES, LANES)
                    lhs[pl.ds(to, 8), lanes] = jnp.where(first, low, pltpu.roll(high, 4, 0))
                    lhs[pl.ds(to + 8, 8), lanes] = jnp.where(first, pltpu.roll(low, 4, 0), high)
        rhs[pl.ds(2 * i * depth, depth), :] = x_ref[...]
        rhs[pl.ds((2 * i + 1) * depth, depth), :half] = -x_ref[:, half:]
        rhs[pl.ds((2 * i + 1) * depth, depth), half:] = x_ref[:, :half]
    for j in range(0, wide // LANES, 2):
        right = rhs[:, pl.ds(j * LANES, 2 * LANES)]
        out = jnp.dot(lhs[...], right, precision=lax.Precision.HIGHEST, preferred_element_type=F32)
        out_ref[:, j, :, :] = out[:, :LANES].reshape(16, 16, LANES)
        out_ref[:, j + 1, :, :] = out[:, LANES:].reshape(16, 16, LANES)


def sum_kernel(scale, parts_ref, out_ref):
    for j in range(parts_ref.shape[1]):
        total = parts_ref[0, j]
        for i in range(1, parts_ref.shape[0]):
            total = total + parts_ref[i, j]
        total = total * scale
        for half in range(0, total.shape[0], 8):
            out_ref[pl.ds(half, 8), j, :] = pltpu.roll(total[half : half + 8], (8 - LAST) % 8, 0)


def finish_kernel(parts_ref, out_ref):
    total = parts_ref[0]
    for i in range(1, parts_ref.shape[0]):
        total = total + parts_ref[i]
    outs = out_ref.shape[0]
    for c in range(2):
        for o in range(outs):
            out_ref[o, pl.ds(c, 1), :] = total[c * outs + o : c * outs + o + 1, :]


def kernel_call(body, shape, specs, cost, name, scratch=(), vmem=16, to=VMEM):
    flops, size = cost
    return pl.pallas_call(
        body,
        out_shape=jax.ShapeDtypeStruct(shape, F32),
        in_specs=specs,
        out_specs=to,
        scratch_shapes=scratch,
        compiler_params=pltpu.CompilerParams(vmem_limit_bytes=vmem * 2**20),
        cost_estimate=pl.CostEstimate(flops=flops, bytes_accessed=size, transcendentals=0),
        name=name,
    )


def shards(left_tensor, right_tensor, closing_tensor):
    slices, _, _, depth, rows = left_tensor.shape
    width = right_tensor.shape[3]
    outs = closing_tensor.shape[3]
    near = 16
    kk = depth // near
    body = slices * 2 * kk
    here = lax.axis_index(FAR).reshape(1)

    x = kernel_call(
        pack_kernel,
        (near, body + width, LANES),
        [ANY, ANY],
        (0, 2**21),
        "pack",
        [
            pltpu.VMEM((slices * 2, near, kk, rows), F32),
            pltpu.VMEM((slices, 2, width, depth), F32),
            pltpu.VMEM((near, width, LANES), F32),
            pltpu.SemaphoreType.DMA((slices * 4 + 1,)),
            pltpu.SemaphoreType.DMA((slices * 4 + 1,)),
        ],
        60,
        ANY,
    )(left_tensor.reshape(slices, 2, near, kk, rows), right_tensor.transpose(0, 1, 3, 2))

    with jax.named_scope("near_move"):
        x = lax.all_to_all(x, NEAR, 0, 0, tiled=True, axis_index_groups=[ORDER])

    r = kernel_call(spread_kernel, (2, 8, near * width // 2, LANES), [VMEM], (0, 2**18), "spread")(x)
    with jax.named_scope("right_move"):
        r = r.reshape(16, near * width // 2, LANES)
        group = [c * 8 + (f + MID) % 8 for c in range(2) for f in range(8)]
        r = lax.all_to_all(r, ("core", FAR), 0, 0, tiled=True, axis_index_groups=[group])
        r = r.reshape(2, 8, near * width // 2, LANES)

    x = kernel_call(
        close_kernel,
        (slices * kk, 2 * outs * rows),
        [SMEM, SMEM, VMEM],
        (2**22, 6 * 2**18),
        "close",
    )(here, closing_tensor.transpose(0, 1, 3, 2), x)
    with jax.named_scope("core_swap"):
        y = lax.ppermute(x, "core", [(0, 1), (1, 0)])

    wide = 2 * outs * rows
    p = kernel_call(
        join_kernel,
        (near, 2 * outs, 16, rows),
        [SMEM, VMEM, VMEM, VMEM],
        (2**27, 2**21),
        "join",
        [pltpu.VMEM((256, 2 * LANES), F32), pltpu.VMEM((4 * slices * kk, wide), F32)],
    )(lax.axis_index("core").reshape(1), r, x, y)

    with jax.named_scope("sum_move"):
        p = lax.all_to_all(p, NEAR, 0, 0, tiled=True)
    p = kernel_call(
        functools.partial(sum_kernel, (slices * 4) ** -0.5),
        (16, 2 * outs, rows),
        [VMEM],
        (2**18, 2**20),
        "sum",
    )(p)

    with jax.named_scope("last_move"):
        group = [c * 8 + (f + LAST) % 8 for c in range(2) for f in range(8)]
        p = lax.all_to_all(p, ("yh", FAR), 0, 0, tiled=True, axis_index_groups=[group])
    p = kernel_call(finish_kernel, (outs, 2, rows), [VMEM], (2**14, 2**17), "finish")(p)
    return p.reshape(1, outs, 2, rows)


def solution(mesh):
    fine = Mesh(mesh.devices.reshape([n for _, n in PARTS]), [name for name, _ in PARTS])
    return jax.shard_map(
        shards,
        mesh=fine,
        in_specs=(
            P(CUTS, None, MODE, None, None),
            P(CUTS, None, None, MODE),
            P(CUTS, None, None, None),
        ),
        out_specs=P(CUTS + MODE, None, None, None),
        check_vma=False,
    )
```

```python
import functools

import jax
import jax.numpy as jnp
from jax import lax
from jax.experimental import pallas as pl
from jax.experimental.pallas import tpu as pltpu
from jax.sharding import Mesh
from jax.sharding import PartitionSpec as P

PARTS = (("yh", 2), ("core", 2), ("yl", 2), ("x", 4), ("za", 8), ("zb", 2))
CUTS = ("yh", "core")
MODE = ("yl", "x", "za", "zb")
NEAR = ("yl", "x", "zb")
FAR = "za"

F32 = jnp.float32
LANES = 128
MID = 5
HALF = 2
LAST = 4
ORDER = [yl * 8 + x * 2 + zb for x in (0, 2, 1, 3) for yl in range(2) for zb in range(2)]
SMEM = pl.BlockSpec(memory_space=pltpu.SMEM)
VMEM = pl.BlockSpec(memory_space=pltpu.VMEM)
ANY = pl.BlockSpec(memory_space=pl.ANY)


def swap_blocks(v):
    n = len(v)
    size = LANES // n
    block = lax.broadcasted_iota(jnp.int32, v[0].shape, 1) // size
    v = list(v)
    bit = 1
    while bit < n:
        low = (block & bit) == 0
        for i in range(n):
            if i & bit:
                continue
            a, b = v[i], v[i | bit]
            v[i] = jnp.where(low, a, pltpu.roll(b, size * bit, 1))
            v[i | bit] = jnp.where(low, pltpu.roll(a, LANES - size * bit, 1), b)
        bit *= 2
    return v


def pack_kernel(left_ref, right_ref, out_ref, held, right, piece, into, out_of):
    slices, _, near, depth, _ = left_ref.shape
    each = 2 * slices
    halves = [pl.ds(0, near // 2), pl.ds(near // 2, near // 2)]
    parts = [(i, half) for half in halves for i in range(each)]
    copies = []
    for n, (i, half) in enumerate(parts):
        copies.append(pltpu.make_async_copy(left_ref.at[i // 2, i % 2, half], held.at[i, half], into.at[n]))
        copies[-1].start()
    given = pltpu.make_async_copy(right_ref, right, into.at[len(parts)])
    given.start()
    last = []
    for n, (i, half) in enumerate(parts):
        copies[n].wait()
        to = out_ref.at[half, pl.ds(i * depth, depth), :]
        last.append(pltpu.make_async_copy(held.at[i, half], to, out_of.at[n]))
        last[-1].start()
    given.wait()
    width = right.shape[2]
    for t in range(near // each):
        lanes = pl.ds(t * LANES, LANES)
        w = swap_blocks([right[j % slices, j // slices, :, lanes] for j in range(each)])
        for g in range(each):
            piece[t * each + g] = w[g]
    to = out_ref.at[:, pl.ds(each * depth, width), :]
    last.append(pltpu.make_async_copy(piece, to, out_of.at[len(parts)]))
    last[-1].start()
    for copy in last:
        copy.wait()


def spread_kernel(near_ref, out_ref):
    cuts, far, width, _ = out_ref.shape
    body = near_ref.shape[1] - cuts * width // near_ref.shape[0]
    for q87 in range(cuts):
        for q6 in range(2):
            for q0 in range(2):
                for q2 in range(2):
                    two = near_ref[ORDER.index(q87 * 4 + q6 * 2 + q2), pl.ds(body + q0, 2, stride=2), :]
                    out_ref[q87 ^ HALF, 0, pl.ds(q6 * 8 + q0 * 4 + q2 * 2, 2), :] = two
        for g in range(1, far):
            out_ref[q87 ^ HALF, g] = out_ref[q87 ^ HALF, 0]


def close_kernel(far_ref, coef_ref, left_ref, out_ref):
    heads = left_ref.shape[0]
    slices, _, outs, _ = coef_ref.shape
    depth = out_ref.shape[0] // slices
    first = far_ref[0] * 2
    rows = 8
    for s in range(slices):
        acc = [[None] * (depth // rows) for _ in range(2 * outs)]
        for h in range(heads):
            head = (ORDER[h] // 2) * 16 + first + ORDER[h] % 2
            co = [coef_ref[s, j // outs, j % outs, head] for j in range(2 * outs)]
            for kb in range(depth // rows):
                at = 2 * s * depth + kb * rows
                re = left_ref[h, pl.ds(at, rows), :]
                im = left_ref[h, pl.ds(at + depth, rows), :]
                for o in range(outs):
                    cre, cim = co[o], co[outs + o]
                    new_re = cre * re - cim * im
                    new_im = cre * im + cim * re
                    if h:
                        new_re, new_im = acc[o][kb] + new_re, acc[outs + o][kb] + new_im
                    acc[o][kb], acc[outs + o][kb] = new_re, new_im
        for kb in range(depth // rows):
            for j in range(2 * outs):
                out_ref[pl.ds(s * depth + kb * rows, rows), pl.ds(j * LANES, LANES)] = acc[j][kb]


def join_kernel(cut_ref, right_ref, x0_ref, x1_ref, x2_ref, x3_ref, out_ref, lhs, rhs):
    depth, wide = x0_ref.shape
    half = wide // 2
    first = lax.broadcasted_iota(jnp.int32, (8, LANES), 0) < 4
    for i, x_ref in enumerate((x0_ref, x1_ref, x2_ref, x3_ref)):
        cut = cut_ref[0] ^ (i ^ HALF)
        lanes = pl.ds(i * LANES, LANES)
        for t in range(4):
            for q6 in range(2):
                at = pl.ds(q6 * 8, 8)
                low = right_ref[cut, (2 * t - MID) % 8, at, :]
                high = right_ref[cut, (2 * t + 1 - MID) % 8, at, :]
                to = (q6 * 8 + t * 2) * 8
                lhs[pl.ds(to, 8), lanes] = jnp.where(first, low, pltpu.roll(high, 4, 0))
                lhs[pl.ds(to + 8, 8), lanes] = jnp.where(first, pltpu.roll(low, 4, 0), high)
        rhs[pl.ds(2 * i * depth, depth), :] = x_ref[...]
        rhs[pl.ds((2 * i + 1) * depth, depth), :half] = -x_ref[:, half:]
        rhs[pl.ds((2 * i + 1) * depth, depth), half:] = x_ref[:, :half]
    for j in range(0, wide // LANES, 2):
        right = rhs[:, pl.ds(j * LANES, 2 * LANES)]
        out = jnp.dot(lhs[...], right, precision=lax.Precision.HIGHEST, preferred_element_type=F32)
        out_ref[:, j, :, :] = out[:, :LANES].reshape(16, 8, LANES)
        out_ref[:, j + 1, :, :] = out[:, LANES:].reshape(16, 8, LANES)


def sum_kernel(scale, parts_ref, out_ref):
    for j in range(parts_ref.shape[1]):
        total = parts_ref[0, j]
        for i in range(1, parts_ref.shape[0]):
            total = total + parts_ref[i, j]
        out_ref[:, j, :] = pltpu.roll(total * scale, (8 - LAST) % 8, 0)


def finish_kernel(parts_ref, out_ref):
    total = parts_ref[0]
    for i in range(1, parts_ref.shape[0]):
        total = total + parts_ref[i]
    outs = out_ref.shape[0]
    for c in range(2):
        for o in range(outs):
            out_ref[o, pl.ds(c, 1), :] = total[c * outs + o : c * outs + o + 1, :]


def kernel_call(body, shape, specs, cost, name, scratch=(), vmem=16, to=VMEM):
    flops, size = cost
    return pl.pallas_call(
        body,
        out_shape=jax.ShapeDtypeStruct(shape, F32),
        in_specs=specs,
        out_specs=to,
        scratch_shapes=scratch,
        compiler_params=pltpu.CompilerParams(vmem_limit_bytes=vmem * 2**20),
        cost_estimate=pl.CostEstimate(flops=flops, bytes_accessed=size, transcendentals=0),
        name=name,
    )


def shards(left_tensor, right_tensor, closing_tensor):
    slices, _, _, depth, rows = left_tensor.shape
    width = right_tensor.shape[3]
    outs = closing_tensor.shape[3]
    near = 16
    kk = depth // near
    body = slices * 2 * kk
    here = lax.axis_index(FAR).reshape(1)

    x = kernel_call(
        pack_kernel,
        (near, body + width, LANES),
        [ANY, ANY],
        (0, 2**21),
        "pack",
        [
            pltpu.VMEM((slices * 2, near, kk, rows), F32),
            pltpu.VMEM((slices, 2, width, depth), F32),
            pltpu.VMEM((near, width, LANES), F32),
            pltpu.SemaphoreType.DMA((slices * 4 + 1,)),
            pltpu.SemaphoreType.DMA((slices * 4 + 1,)),
        ],
        60,
        ANY,
    )(left_tensor.reshape(slices, 2, near, kk, rows), right_tensor.transpose(0, 1, 3, 2))

    with jax.named_scope("near_move"):
        x = lax.all_to_all(x, NEAR, 0, 0, tiled=True, axis_index_groups=[ORDER])

    cuts = 4
    r = kernel_call(
        spread_kernel, (cuts, 8, near * width // cuts, LANES), [VMEM], (0, 2**18), "spread"
    )(x)
    with jax.named_scope("right_move"):
        r = r.reshape(cuts * 8, near * width // cuts, LANES)
        group = [(c ^ HALF) * 8 + (f + MID) % 8 for c in range(cuts) for f in range(8)]
        r = lax.all_to_all(r, CUTS + (FAR,), 0, 0, tiled=True, axis_index_groups=[group])
        r = r.reshape(cuts, 8, near * width // cuts, LANES)

    x = kernel_call(
        close_kernel,
        (slices * kk, 2 * outs * rows),
        [SMEM, SMEM, VMEM],
        (2**22, 6 * 2**18),
        "close",
    )(here, closing_tensor.transpose(0, 1, 3, 2), x)
    swap = [(0, 1), (1, 0)]
    with jax.named_scope("cuts_gather"):
        x2 = lax.ppermute(x, "yh", swap)
        x1 = lax.ppermute(x, "core", swap)
        x3 = lax.ppermute(x2, "core", swap)

    wide = 2 * outs * rows
    p = kernel_call(
        join_kernel,
        (near, 2 * outs, 8, rows),
        [SMEM] + [VMEM] * 5,
        (2**27, 2**21),
        "join",
        [pltpu.VMEM((128, cuts * LANES), F32), pltpu.VMEM((2 * cuts * slices * kk, wide), F32)],
    )(lax.axis_index(CUTS).reshape(1), r, x, x1, x2, x3)

    with jax.named_scope("sum_move"):
        p = lax.all_to_all(p, NEAR, 0, 0, tiled=True)
    p = kernel_call(
        functools.partial(sum_kernel, (slices * cuts) ** -0.5),
        (8, 2 * outs, rows),
        [VMEM],
        (2**18, 2**20),
        "sum",
    )(p)

    with jax.named_scope("last_move"):
        group = [(f + LAST) % 8 for f in range(8)]
        p = lax.all_to_all(p, FAR, 0, 0, tiled=True, axis_index_groups=[group])
    p = kernel_call(finish_kernel, (outs, 2, rows), [VMEM], (2**14, 2**17), "finish")(p)
    return p.reshape(1, outs, 2, rows)


def solution(mesh):
    fine = Mesh(mesh.devices.reshape([n for _, n in PARTS]), [name for name, _ in PARTS])
    return jax.shard_map(
        shards,
        mesh=fine,
        in_specs=(
            P(CUTS, None, MODE, None, None),
            P(CUTS, None, None, MODE),
            P(CUTS, None, None, None),
        ),
        out_specs=P(CUTS + MODE, None, None, None),
        check_vma=False,
    )
```

```python
import functools

import jax
import jax.numpy as jnp
from jax import lax
from jax.experimental import pallas as pl
from jax.experimental.pallas import tpu as pltpu
from jax.sharding import Mesh
from jax.sharding import PartitionSpec as P

PARTS = (("yh", 2), ("core", 2), ("yl", 2), ("x", 4), ("za", 8), ("zb", 2))
CUTS = ("yh", "core")
MODE = ("yl", "x", "za", "zb")
NEAR = ("yl", "x", "zb")
FAR = "za"

F32 = jnp.float32
LANES = 128
MID = 5
HALF = 2
LAST = 4
ORDER = [yl * 8 + x * 2 + zb for x in (3, 1, 2, 0) for yl in (1, 0) for zb in range(2)]
SMEM = pl.BlockSpec(memory_space=pltpu.SMEM)
VMEM = pl.BlockSpec(memory_space=pltpu.VMEM)
ANY = pl.BlockSpec(memory_space=pl.ANY)


def swap_blocks(v):
    n = len(v)
    size = LANES // n
    block = lax.broadcasted_iota(jnp.int32, v[0].shape, 1) // size
    v = list(v)
    bit = 1
    while bit < n:
        low = (block & bit) == 0
        for i in range(n):
            if i & bit:
                continue
            a, b = v[i], v[i | bit]
            v[i] = jnp.where(low, a, pltpu.roll(b, size * bit, 1))
            v[i | bit] = jnp.where(low, pltpu.roll(a, LANES - size * bit, 1), b)
        bit *= 2
    return v


def pack_kernel(left_ref, right_ref, out_ref, held, right, piece, into, out_of):
    slices, _, near, depth, _ = left_ref.shape
    each = 2 * slices
    halves = [pl.ds(0, near // 2), pl.ds(near // 2, near // 2)]
    parts = [(i, half) for half in halves for i in range(each)]
    copies = []
    for n, (i, half) in enumerate(parts):
        copies.append(pltpu.make_async_copy(left_ref.at[i // 2, i % 2, half], held.at[i, half], into.at[n]))
        copies[-1].start()
    given = pltpu.make_async_copy(right_ref, right, into.at[len(parts)])
    given.start()
    last = []
    for n, (i, half) in enumerate(parts):
        copies[n].wait()
        to = out_ref.at[half, pl.ds(i * depth, depth), :]
        last.append(pltpu.make_async_copy(held.at[i, half], to, out_of.at[n]))
        last[-1].start()
    given.wait()
    width = right.shape[2]
    for t in range(near // each):
        lanes = pl.ds(t * LANES, LANES)
        w = swap_blocks([right[j % slices, j // slices, :, lanes] for j in range(each)])
        for g in range(each):
            piece[t * each + g] = w[g]
    to = out_ref.at[:, pl.ds(each * depth, width), :]
    last.append(pltpu.make_async_copy(piece, to, out_of.at[len(parts)]))
    last[-1].start()
    for copy in last:
        copy.wait()


def spread_kernel(far_ref, near_ref, out_ref):
    cuts, far, width, _ = out_ref.shape
    body = near_ref.shape[1] - cuts * width // near_ref.shape[0]
    for q87 in range(cuts):
        for q6 in range(2):
            for q0 in range(2):
                for q2 in range(2):
                    two = near_ref[ORDER.index(q87 * 4 + q6 * 2 + q2), pl.ds(body + q0, 2, stride=2), :]
                    out_ref[q87 ^ HALF, 0, pl.ds(q6 * 8 + q0 * 4 + q2 * 2, 2), :] = two
        for g in range(1, far):
            out_ref[q87 ^ HALF, g] = out_ref[q87 ^ HALF, 0]


def close_kernel(far_ref, coef_ref, left_ref, out_ref):
    heads = left_ref.shape[0]
    slices, _, outs, _ = coef_ref.shape
    depth = out_ref.shape[0] // slices
    first = far_ref[0] * 2
    rows = 8
    for s in range(slices):
        acc = [[None] * (depth // rows) for _ in range(2 * outs)]
        for h in range(heads):
            head = (ORDER[h] // 2) * 16 + first + ORDER[h] % 2
            co = [coef_ref[s, j // outs, j % outs, head] for j in range(2 * outs)]
            for kb in range(depth // rows):
                at = 2 * s * depth + kb * rows
                re = left_ref[h, pl.ds(at, rows), :]
                im = left_ref[h, pl.ds(at + depth, rows), :]
                for o in range(outs):
                    cre, cim = co[o], co[outs + o]
                    new_re = cre * re - cim * im
                    new_im = cre * im + cim * re
                    if h:
                        new_re, new_im = acc[o][kb] + new_re, acc[outs + o][kb] + new_im
                    acc[o][kb], acc[outs + o][kb] = new_re, new_im
        for kb in range(depth // rows):
            for j in range(2 * outs):
                out_ref[pl.ds(s * depth + kb * rows, rows), pl.ds(j * LANES, LANES)] = acc[j][kb]


def join_kernel(cut_ref, right_ref, x0_ref, x1_ref, x2_ref, x3_ref, out_ref, lhs, rhs):
    depth, wide = x0_ref.shape
    half = wide // 2
    first = lax.broadcasted_iota(jnp.int32, (8, LANES), 0) < 4
    for i, x_ref in enumerate((x0_ref, x1_ref, x2_ref, x3_ref)):
        cut = cut_ref[0] ^ (i ^ HALF)
        lanes = pl.ds(i * LANES, LANES)
        for t in range(4):
            for q6 in range(2):
                at = pl.ds(q6 * 8, 8)
                low = right_ref[cut, (2 * t - MID) % 8, at, :]
                high = right_ref[cut, (2 * t + 1 - MID) % 8, at, :]
                to = (q6 * 8 + t * 2) * 8
                lhs[pl.ds(to, 8), lanes] = jnp.where(first, low, pltpu.roll(high, 4, 0))
                lhs[pl.ds(to + 8, 8), lanes] = jnp.where(first, pltpu.roll(low, 4, 0), high)
        rhs[pl.ds(2 * i * depth, depth), :] = x_ref[...]
        rhs[pl.ds((2 * i + 1) * depth, depth), :half] = -x_ref[:, half:]
        rhs[pl.ds((2 * i + 1) * depth, depth), half:] = x_ref[:, :half]
    for j in range(0, wide // LANES, 2):
        right = rhs[:, pl.ds(j * LANES, 2 * LANES)]
        out = jnp.dot(lhs[...], right, precision=lax.Precision.HIGHEST, preferred_element_type=F32)
        out_ref[:, j, :, :] = out[:, :LANES].reshape(16, 8, LANES)
        out_ref[:, j + 1, :, :] = out[:, LANES:].reshape(16, 8, LANES)


def sum_kernel(scale, parts_ref, out_ref):
    for j in range(parts_ref.shape[1]):
        total = parts_ref[0, j]
        for i in range(1, parts_ref.shape[0]):
            total = total + parts_ref[i, j]
        out_ref[:, j, :] = pltpu.roll(total * scale, (8 - LAST) % 8, 0)


def finish_kernel(parts_ref, out_ref):
    total = parts_ref[0]
    for i in range(1, parts_ref.shape[0]):
        total = total + parts_ref[i]
    outs = out_ref.shape[0]
    for c in range(2):
        for o in range(outs):
            out_ref[o, pl.ds(c, 1), :] = total[c * outs + o : c * outs + o + 1, :]


def kernel_call(body, shape, specs, cost, name, scratch=(), vmem=16, to=VMEM):
    flops, size = cost
    return pl.pallas_call(
        body,
        out_shape=jax.ShapeDtypeStruct(shape, F32),
        in_specs=specs,
        out_specs=to,
        scratch_shapes=scratch,
        compiler_params=pltpu.CompilerParams(vmem_limit_bytes=vmem * 2**20),
        cost_estimate=pl.CostEstimate(flops=flops, bytes_accessed=size, transcendentals=0),
        name=name,
    )


def shards(left_tensor, right_tensor, closing_tensor):
    slices, _, _, depth, rows = left_tensor.shape
    width = right_tensor.shape[3]
    outs = closing_tensor.shape[3]
    near = 16
    kk = depth // near
    body = slices * 2 * kk
    here = lax.axis_index(FAR).reshape(1)

    x = kernel_call(
        pack_kernel,
        (near, body + width, LANES),
        [ANY, ANY],
        (0, 2**21),
        "pack",
        [
            pltpu.VMEM((slices * 2, near, kk, rows), F32),
            pltpu.VMEM((slices, 2, width, depth), F32),
            pltpu.VMEM((near, width, LANES), F32),
            pltpu.SemaphoreType.DMA((slices * 4 + 1,)),
            pltpu.SemaphoreType.DMA((slices * 4 + 1,)),
        ],
        60,
        ANY,
    )(left_tensor.reshape(slices, 2, near, kk, rows), right_tensor.transpose(0, 1, 3, 2))

    with jax.named_scope("near_move"):
        x = lax.all_to_all(x, NEAR, 0, 0, tiled=True, axis_index_groups=[ORDER])

    cuts = 4
    r = kernel_call(
        spread_kernel, (cuts, 8, near * width // cuts, LANES), [SMEM, VMEM], (0, 2**18), "spread"
    )(here, x)
    with jax.named_scope("right_move"):
        r = r.reshape(cuts * 8, near * width // cuts, LANES)
        group = [(c ^ HALF) * 8 + (f + MID) % 8 for c in range(cuts) for f in range(8)]
        r = lax.all_to_all(r, CUTS + (FAR,), 0, 0, tiled=True, axis_index_groups=[group])
        r = r.reshape(cuts, 8, near * width // cuts, LANES)

    x = kernel_call(
        close_kernel,
        (slices * kk, 2 * outs * rows),
        [SMEM, SMEM, VMEM],
        (2**22, 6 * 2**18),
        "close",
    )(here, closing_tensor.transpose(0, 1, 3, 2), x)
    swap = [(0, 1), (1, 0)]
    with jax.named_scope("cuts_gather"):
        x2 = lax.ppermute(x, "yh", swap)
        x1 = lax.ppermute(x, "core", swap)
        x3 = lax.ppermute(x2, "core", swap)

    wide = 2 * outs * rows
    p = kernel_call(
        join_kernel,
        (near, 2 * outs, 8, rows),
        [SMEM] + [VMEM] * 5,
        (2**27, 2**21),
        "join",
        [pltpu.VMEM((128, cuts * LANES), F32), pltpu.VMEM((2 * cuts * slices * kk, wide), F32)],
    )(lax.axis_index(CUTS).reshape(1), r, x, x1, x2, x3)

    with jax.named_scope("sum_move"):
        p = lax.all_to_all(p, NEAR, 0, 0, tiled=True)
    p = kernel_call(
        functools.partial(sum_kernel, (slices * cuts) ** -0.5),
        (8, 2 * outs, rows),
        [VMEM],
        (2**18, 2**20),
        "sum",
    )(p)

    with jax.named_scope("last_move"):
        group = [(f + LAST) % 8 for f in range(8)]
        p = lax.all_to_all(p, FAR, 0, 0, tiled=True, axis_index_groups=[group])
    p = kernel_call(finish_kernel, (outs, 2, rows), [VMEM], (2**14, 2**17), "finish")(p)
    return p.reshape(1, outs, 2, rows)


def solution(mesh):
    fine = Mesh(mesh.devices.reshape([n for _, n in PARTS]), [name for name, _ in PARTS])
    return jax.shard_map(
        shards,
        mesh=fine,
        in_specs=(
            P(CUTS, None, MODE, None, None),
            P(CUTS, None, None, MODE),
            P(CUTS, None, None, None),
        ),
        out_specs=P(CUTS + MODE, None, None, None),
        check_vma=False,
    )
```

```python
import functools

import jax
import jax.numpy as jnp
from jax import lax
from jax.experimental import pallas as pl
from jax.experimental.pallas import tpu as pltpu
from jax.sharding import Mesh
from jax.sharding import PartitionSpec as P

PARTS = (("yh", 2), ("core", 2), ("yl", 2), ("x", 4), ("za", 8), ("zb", 2))
CUTS = ("yh", "core")
MODE = ("yl", "x", "za", "zb")
NEAR = ("yl", "x", "zb")
FAR = "za"

F32 = jnp.float32
LANES = 128
MID = 6
HALF = 2
LAST = 4
ORDER = [yl * 8 + x * 2 + zb for x in (3, 1, 2, 0) for yl in (1, 0) for zb in range(2)]
SMEM = pl.BlockSpec(memory_space=pltpu.SMEM)
VMEM = pl.BlockSpec(memory_space=pltpu.VMEM)
ANY = pl.BlockSpec(memory_space=pl.ANY)


def swap_blocks(v):
    n = len(v)
    size = LANES // n
    block = lax.broadcasted_iota(jnp.int32, v[0].shape, 1) // size
    v = list(v)
    bit = 1
    while bit < n:
        low = (block & bit) == 0
        for i in range(n):
            if i & bit:
                continue
            a, b = v[i], v[i | bit]
            v[i] = jnp.where(low, a, pltpu.roll(b, size * bit, 1))
            v[i | bit] = jnp.where(low, pltpu.roll(a, LANES - size * bit, 1), b)
        bit *= 2
    return v


def pack_kernel(left_ref, right_ref, out_ref, held, right, piece, into, out_of):
    slices, _, near, depth, _ = left_ref.shape
    each = 2 * slices
    halves = [pl.ds(0, near // 2), pl.ds(near // 2, near // 2)]
    parts = [(i, half) for half in halves for i in range(each)]
    copies = []
    for n, (i, half) in enumerate(parts):
        copies.append(pltpu.make_async_copy(left_ref.at[i // 2, i % 2, half], held.at[i, half], into.at[n]))
        copies[-1].start()
    given = pltpu.make_async_copy(right_ref, right, into.at[len(parts)])
    given.start()
    last = []
    for n, (i, half) in enumerate(parts):
        copies[n].wait()
        to = out_ref.at[half, pl.ds(i * depth, depth), :]
        last.append(pltpu.make_async_copy(held.at[i, half], to, out_of.at[n]))
        last[-1].start()
    given.wait()
    width = right.shape[2]
    for t in range(near // each):
        lanes = pl.ds(t * LANES, LANES)
        w = swap_blocks([right[j % slices, j // slices, :, lanes] for j in range(each)])
        for g in range(each):
            piece[t * each + g] = w[g]
    to = out_ref.at[:, pl.ds(each * depth, width), :]
    last.append(pltpu.make_async_copy(piece, to, out_of.at[len(parts)]))
    last[-1].start()
    for copy in last:
        copy.wait()


def spread_kernel(far_ref, near_ref, out_ref):
    cuts, far, width, _ = out_ref.shape
    body = near_ref.shape[1] - cuts * width // near_ref.shape[0]
    for q87 in range(cuts):
        for q6 in range(2):
            for q0 in range(2):
                for q2 in range(2):
                    two = near_ref[ORDER.index(q87 * 4 + q6 * 2 + q2), pl.ds(body + q0, 2, stride=2), :]
                    out_ref[q87 ^ HALF, 0, pl.ds(q6 * 8 + q0 * 4 + q2 * 2, 2), :] = two
        for g in range(1, far):
            out_ref[q87 ^ HALF, g] = out_ref[q87 ^ HALF, 0]


def close_kernel(s, far_ref, coef_ref, left_ref, out_ref):
    heads = left_ref.shape[0]
    outs = coef_ref.shape[2]
    depth = out_ref.shape[0]
    first = far_ref[0] * 2
    rows = 8
    acc = [[None] * (depth // rows) for _ in range(2 * outs)]
    for h in range(heads):
        head = (ORDER[h] // 2) * 16 + first + ORDER[h] % 2
        co = [coef_ref[s, j // outs, j % outs, head] for j in range(2 * outs)]
        for kb in range(depth // rows):
            at = 2 * s * depth + kb * rows
            re = left_ref[h, pl.ds(at, rows), :]
            im = left_ref[h, pl.ds(at + depth, rows), :]
            for o in range(outs):
                cre, cim = co[o], co[outs + o]
                new_re = cre * re - cim * im
                new_im = cre * im + cim * re
                if h:
                    new_re, new_im = acc[o][kb] + new_re, acc[outs + o][kb] + new_im
                acc[o][kb], acc[outs + o][kb] = new_re, new_im
    for kb in range(depth // rows):
        for j in range(2 * outs):
            out_ref[pl.ds(kb * rows, rows), pl.ds(j * LANES, LANES)] = acc[j][kb]


def join_kernel(cut_ref, right_ref, *refs):
    *x_refs, out_ref, lhs, rhs = refs
    depth, wide = x_refs[0].shape
    slices = len(x_refs) // 4
    half = wide // 2
    first = lax.broadcasted_iota(jnp.int32, (8, LANES), 0) < 4
    for i in range(4):
        cut = cut_ref[0] ^ (i ^ HALF)
        lanes = pl.ds(i * LANES, LANES)
        for t in range(4):
            for q6 in range(2):
                at = pl.ds(q6 * 8, 8)
                low = right_ref[cut, (2 * t - MID) % 8, at, :]
                high = right_ref[cut, (2 * t + 1 - MID) % 8, at, :]
                to = (q6 * 8 + t * 2) * 8
                lhs[pl.ds(to, 8), lanes] = jnp.where(first, low, pltpu.roll(high, 4, 0))
                lhs[pl.ds(to + 8, 8), lanes] = jnp.where(first, pltpu.roll(low, 4, 0), high)
        for s in range(slices):
            x_ref = x_refs[i * slices + s]
            re = pl.ds((2 * i * slices + s) * depth, depth)
            im = pl.ds(((2 * i + 1) * slices + s) * depth, depth)
            rhs[re, :] = x_ref[...]
            rhs[im, :half] = -x_ref[:, half:]
            rhs[im, half:] = x_ref[:, :half]
    for j in range(0, wide // LANES, 2):
        right = rhs[:, pl.ds(j * LANES, 2 * LANES)]
        out = jnp.dot(lhs[...], right, precision=lax.Precision.HIGHEST, preferred_element_type=F32)
        out_ref[:, j, :, :] = out[:, :LANES].reshape(16, 8, LANES)
        out_ref[:, j + 1, :, :] = out[:, LANES:].reshape(16, 8, LANES)


def sum_kernel(scale, parts_ref, out_ref):
    for j in range(parts_ref.shape[1]):
        total = parts_ref[0, j]
        for i in range(1, parts_ref.shape[0]):
            total = total + parts_ref[i, j]
        out_ref[:, j, :] = pltpu.roll(total * scale, (8 - LAST) % 8, 0)


def finish_kernel(parts_ref, out_ref):
    total = parts_ref[0]
    for i in range(1, parts_ref.shape[0]):
        total = total + parts_ref[i]
    outs = out_ref.shape[0]
    for c in range(2):
        for o in range(outs):
            out_ref[o, pl.ds(c, 1), :] = total[c * outs + o : c * outs + o + 1, :]


def kernel_call(body, shape, specs, cost, name, scratch=(), vmem=16, to=VMEM):
    flops, size = cost
    return pl.pallas_call(
        body,
        out_shape=jax.ShapeDtypeStruct(shape, F32),
        in_specs=specs,
        out_specs=to,
        scratch_shapes=scratch,
        compiler_params=pltpu.CompilerParams(vmem_limit_bytes=vmem * 2**20),
        cost_estimate=pl.CostEstimate(flops=flops, bytes_accessed=size, transcendentals=0),
        name=name,
    )


def shards(left_tensor, right_tensor, closing_tensor):
    slices, _, _, depth, rows = left_tensor.shape
    width = right_tensor.shape[3]
    outs = closing_tensor.shape[3]
    near = 16
    kk = depth // near
    body = slices * 2 * kk
    here = lax.axis_index(FAR).reshape(1)

    x = kernel_call(
        pack_kernel,
        (near, body + width, LANES),
        [ANY, ANY],
        (0, 2**21),
        "pack",
        [
            pltpu.VMEM((slices * 2, near, kk, rows), F32),
            pltpu.VMEM((slices, 2, width, depth), F32),
            pltpu.VMEM((near, width, LANES), F32),
            pltpu.SemaphoreType.DMA((slices * 4 + 1,)),
            pltpu.SemaphoreType.DMA((slices * 4 + 1,)),
        ],
        60,
        ANY,
    )(left_tensor.reshape(slices, 2, near, kk, rows), right_tensor.transpose(0, 1, 3, 2))

    with jax.named_scope("near_move"):
        x = lax.all_to_all(x, NEAR, 0, 0, tiled=True, axis_index_groups=[ORDER])

    cuts = 4
    r = kernel_call(
        spread_kernel, (cuts, 8, near * width // cuts, LANES), [SMEM, VMEM], (0, 2**18), "spread"
    )(here, x)
    with jax.named_scope("right_move"):
        r = r.reshape(cuts * 8, near * width // cuts, LANES)
        group = [(c ^ HALF) * 8 + (f + MID) % 8 for c in range(cuts) for f in range(8)]
        r = lax.all_to_all(r, CUTS + (FAR,), 0, 0, tiled=True, axis_index_groups=[group])
        r = r.reshape(cuts, 8, near * width // cuts, LANES)

    swap = [(0, 1), (1, 0)]
    pieces = [[], [], [], []]
    for i in range(slices):
        x0 = kernel_call(
            functools.partial(close_kernel, i),
            (kk, 2 * outs * rows),
            [SMEM, SMEM, VMEM],
            (2**21, 3 * 2**18),
            "close",
        )(here, closing_tensor.transpose(0, 1, 3, 2), x)
        with jax.named_scope("cuts_gather"):
            x2 = lax.ppermute(x0, "yh", swap)
            x1 = lax.ppermute(x0, "core", swap)
            x3 = lax.ppermute(x2, "core", swap)
        for piece, given in zip(pieces, (x0, x1, x2, x3)):
            piece.append(given)

    wide = 2 * outs * rows
    p = kernel_call(
        join_kernel,
        (near, 2 * outs, 8, rows),
        [SMEM] + [VMEM] * (1 + 4 * slices),
        (2**27, 2**21),
        "join",
        [pltpu.VMEM((128, cuts * LANES), F32), pltpu.VMEM((2 * cuts * slices * kk, wide), F32)],
    )(lax.axis_index(CUTS).reshape(1), r, *sum(pieces, []))

    with jax.named_scope("sum_move"):
        p = lax.all_to_all(p, NEAR, 0, 0, tiled=True)
    p = kernel_call(
        functools.partial(sum_kernel, (slices * cuts) ** -0.5),
        (8, 2 * outs, rows),
        [VMEM],
        (2**18, 2**20),
        "sum",
    )(p)

    with jax.named_scope("last_move"):
        group = [(f + LAST) % 8 for f in range(8)]
        p = lax.all_to_all(p, FAR, 0, 0, tiled=True, axis_index_groups=[group])
    p = kernel_call(finish_kernel, (outs, 2, rows), [VMEM], (2**14, 2**17), "finish")(p)
    return p.reshape(1, outs, 2, rows)


def solution(mesh):
    fine = Mesh(mesh.devices.reshape([n for _, n in PARTS]), [name for name, _ in PARTS])
    return jax.shard_map(
        shards,
        mesh=fine,
        in_specs=(
            P(CUTS, None, MODE, None, None),
            P(CUTS, None, None, MODE),
            P(CUTS, None, None, None),
        ),
        out_specs=P(CUTS + MODE, None, None, None),
        check_vma=False,
    )
```

```python
import functools

import jax
import jax.numpy as jnp
from jax import lax
from jax.experimental import pallas as pl
from jax.experimental.pallas import tpu as pltpu
from jax.sharding import Mesh
from jax.sharding import PartitionSpec as P

PARTS = (("yh", 2), ("core", 2), ("yl", 2), ("x", 4), ("za", 8), ("zb", 2))
CUTS = ("yh", "core")
MODE = ("yl", "x", "za", "zb")
NEAR = ("yl", "x", "zb")
FAR = "za"

F32 = jnp.float32
LANES = 128
MID = 6
HALF = 2
LAST = 4
ORDER = [yl * 8 + x * 2 + zb for x in (3, 1, 2, 0) for yl in (1, 0) for zb in range(2)]
SMEM = pl.BlockSpec(memory_space=pltpu.SMEM)
VMEM = pl.BlockSpec(memory_space=pltpu.VMEM)
ANY = pl.BlockSpec(memory_space=pl.ANY)


def swap_blocks(v):
    n = len(v)
    size = LANES // n
    block = lax.broadcasted_iota(jnp.int32, v[0].shape, 1) // size
    v = list(v)
    bit = 1
    while bit < n:
        low = (block & bit) == 0
        for i in range(n):
            if i & bit:
                continue
            a, b = v[i], v[i | bit]
            v[i] = jnp.where(low, a, pltpu.roll(b, size * bit, 1))
            v[i | bit] = jnp.where(low, pltpu.roll(a, LANES - size * bit, 1), b)
        bit *= 2
    return v


def pack_kernel(left_ref, right_ref, out_ref, held, right, piece, into, out_of):
    slices, _, near, depth, _ = left_ref.shape
    each = 2 * slices
    halves = [pl.ds(0, near // 2), pl.ds(near // 2, near // 2)]
    parts = [(i, half) for half in halves for i in range(each)]
    copies = []
    for n, (i, half) in enumerate(parts):
        copies.append(pltpu.make_async_copy(left_ref.at[i // 2, i % 2, half], held.at[i, half], into.at[n]))
        copies[-1].start()
    given = pltpu.make_async_copy(right_ref, right, into.at[len(parts)])
    given.start()
    last = []
    for n, (i, half) in enumerate(parts):
        copies[n].wait()
        to = out_ref.at[half, pl.ds(i * depth, depth), :]
        last.append(pltpu.make_async_copy(held.at[i, half], to, out_of.at[n]))
        last[-1].start()
    given.wait()
    width = right.shape[2]
    for t in range(near // each):
        lanes = pl.ds(t * LANES, LANES)
        w = swap_blocks([right[j % slices, j // slices, :, lanes] for j in range(each)])
        for g in range(each):
            piece[t * each + g] = w[g]
    to = out_ref.at[:, pl.ds(each * depth, width), :]
    last.append(pltpu.make_async_copy(piece, to, out_of.at[len(parts)]))
    last[-1].start()
    for copy in last:
        copy.wait()


def spread_kernel(far_ref, near_ref, out_ref):
    cuts, far, width, _ = out_ref.shape
    body = near_ref.shape[1] - cuts * width // near_ref.shape[0]
    for q87 in range(cuts):
        for q6 in range(2):
            for q0 in range(2):
                for q2 in range(2):
                    two = near_ref[ORDER.index(q87 * 4 + q6 * 2 + q2), pl.ds(body + q0, 2, stride=2), :]
                    out_ref[q87 ^ HALF, 0, pl.ds(q6 * 8 + q0 * 4 + q2 * 2, 2), :] = two
        for g in range(1, far):
            out_ref[q87 ^ HALF, g] = out_ref[q87 ^ HALF, 0]


def close_kernel(far_ref, coef_ref, left_ref, out_ref, *piece_refs):
    heads = left_ref.shape[0]
    outs = coef_ref.shape[2]
    first = far_ref[0] * 2
    rows = 8
    for s, piece_ref in enumerate(piece_refs):
        depth = piece_ref.shape[0]
        acc = [[None] * (depth // rows) for _ in range(2 * outs)]
        for h in range(heads):
            head = (ORDER[h] // 2) * 16 + first + ORDER[h] % 2
            co = [coef_ref[s, j // outs, j % outs, head] for j in range(2 * outs)]
            for kb in range(depth // rows):
                at = 2 * s * depth + kb * rows
                re = left_ref[h, pl.ds(at, rows), :]
                im = left_ref[h, pl.ds(at + depth, rows), :]
                for o in range(outs):
                    cre, cim = co[o], co[outs + o]
                    new_re = cre * re - cim * im
                    new_im = cre * im + cim * re
                    if h:
                        new_re, new_im = acc[o][kb] + new_re, acc[outs + o][kb] + new_im
                    acc[o][kb], acc[outs + o][kb] = new_re, new_im
        for kb in range(depth // rows):
            for j in range(2 * outs):
                lanes = pl.ds(j * LANES, LANES)
                piece_ref[pl.ds(kb * rows, rows), lanes] = acc[j][kb]
                out_ref[pl.ds(s * depth + kb * rows, rows), lanes] = acc[j][kb]


def join_kernel(cut_ref, right_ref, *refs):
    *x_refs, out_ref, lhs, rhs = refs
    depth, wide = x_refs[2].shape
    slices = len(x_refs) // 2 - 1
    x_refs = [x.at[pl.ds(s * depth, depth), :] for x in x_refs[:2] for s in range(slices)] + x_refs[2:]
    half = wide // 2
    first = lax.broadcasted_iota(jnp.int32, (8, LANES), 0) < 4
    for i in range(4):
        cut = cut_ref[0] ^ (i ^ HALF)
        lanes = pl.ds(i * LANES, LANES)
        for t in range(4):
            for q6 in range(2):
                at = pl.ds(q6 * 8, 8)
                low = right_ref[cut, (2 * t - MID) % 8, at, :]
                high = right_ref[cut, (2 * t + 1 - MID) % 8, at, :]
                to = (q6 * 8 + t * 2) * 8
                lhs[pl.ds(to, 8), lanes] = jnp.where(first, low, pltpu.roll(high, 4, 0))
                lhs[pl.ds(to + 8, 8), lanes] = jnp.where(first, pltpu.roll(low, 4, 0), high)
        for s in range(slices):
            x_ref = x_refs[i * slices + s]
            re = pl.ds((2 * i * slices + s) * depth, depth)
            im = pl.ds(((2 * i + 1) * slices + s) * depth, depth)
            rhs[re, :] = x_ref[...]
            rhs[im, :half] = -x_ref[:, half:]
            rhs[im, half:] = x_ref[:, :half]
    for j in range(0, wide // LANES, 2):
        right = rhs[:, pl.ds(j * LANES, 2 * LANES)]
        out = jnp.dot(lhs[...], right, precision=lax.Precision.HIGHEST, preferred_element_type=F32)
        out_ref[:, j, :, :] = out[:, :LANES].reshape(16, 8, LANES)
        out_ref[:, j + 1, :, :] = out[:, LANES:].reshape(16, 8, LANES)


def sum_kernel(scale, parts_ref, out_ref):
    for j in range(parts_ref.shape[1]):
        total = parts_ref[0, j]
        for i in range(1, parts_ref.shape[0]):
            total = total + parts_ref[i, j]
        out_ref[:, j, :] = pltpu.roll(total * scale, (8 - LAST) % 8, 0)


def finish_kernel(parts_ref, out_ref):
    total = parts_ref[0]
    for i in range(1, parts_ref.shape[0]):
        total = total + parts_ref[i]
    outs = out_ref.shape[0]
    for c in range(2):
        for o in range(outs):
            out_ref[o, pl.ds(c, 1), :] = total[c * outs + o : c * outs + o + 1, :]


def kernel_call(body, shape, specs, cost, name, scratch=(), vmem=16, to=VMEM):
    flops, size = cost
    return pl.pallas_call(
        body,
        out_shape=jax.tree.map(lambda n: jax.ShapeDtypeStruct(n, F32), shape, is_leaf=lambda n: isinstance(n, tuple)),
        in_specs=specs,
        out_specs=to,
        scratch_shapes=scratch,
        compiler_params=pltpu.CompilerParams(vmem_limit_bytes=vmem * 2**20),
        cost_estimate=pl.CostEstimate(flops=flops, bytes_accessed=size, transcendentals=0),
        name=name,
    )


def shards(left_tensor, right_tensor, closing_tensor):
    slices, _, _, depth, rows = left_tensor.shape
    width = right_tensor.shape[3]
    outs = closing_tensor.shape[3]
    near = 16
    kk = depth // near
    body = slices * 2 * kk
    here = lax.axis_index(FAR).reshape(1)

    x = kernel_call(
        pack_kernel,
        (near, body + width, LANES),
        [ANY, ANY],
        (0, 2**21),
        "pack",
        [
            pltpu.VMEM((slices * 2, near, kk, rows), F32),
            pltpu.VMEM((slices, 2, width, depth), F32),
            pltpu.VMEM((near, width, LANES), F32),
            pltpu.SemaphoreType.DMA((slices * 4 + 1,)),
            pltpu.SemaphoreType.DMA((slices * 4 + 1,)),
        ],
        60,
        ANY,
    )(left_tensor.reshape(slices, 2, near, kk, rows), right_tensor.transpose(0, 1, 3, 2))

    with jax.named_scope("near_move"):
        x = lax.all_to_all(x, NEAR, 0, 0, tiled=True, axis_index_groups=[ORDER])

    cuts = 4
    r = kernel_call(
        spread_kernel, (cuts, 8, near * width // cuts, LANES), [SMEM, VMEM], (0, 2**18), "spread"
    )(here, x)
    with jax.named_scope("right_move"):
        r = r.reshape(cuts * 8, near * width // cuts, LANES)
        group = [(c ^ HALF) * 8 + (f + MID) % 8 for c in range(cuts) for f in range(8)]
        r = lax.all_to_all(r, CUTS + (FAR,), 0, 0, tiled=True, axis_index_groups=[group])
        r = r.reshape(cuts, 8, near * width // cuts, LANES)

    swap = [(0, 1), (1, 0)]
    wide = 2 * outs * rows
    x0, *pieces = kernel_call(
        close_kernel,
        [(slices * kk, wide)] + [(kk, wide)] * slices,
        [SMEM, SMEM, VMEM],
        (2**22, 6 * 2**18),
        "close",
        to=[VMEM] * (1 + slices),
    )(here, closing_tensor.transpose(0, 1, 3, 2), x)
    with jax.named_scope("cuts_gather"):
        x2 = [lax.ppermute(piece, "yh", swap) for piece in pieces]
        x1 = lax.ppermute(x0, "core", swap)
        x3 = [lax.ppermute(piece, "core", swap) for piece in x2]

    p = kernel_call(
        join_kernel,
        (near, 2 * outs, 8, rows),
        [SMEM] + [VMEM] * (3 + 2 * slices),
        (2**27, 2**21),
        "join",
        [pltpu.VMEM((128, cuts * LANES), F32), pltpu.VMEM((2 * cuts * slices * kk, wide), F32)],
    )(lax.axis_index(CUTS).reshape(1), r, x0, x1, *x2, *x3)

    with jax.named_scope("sum_move"):
        p = lax.all_to_all(p, NEAR, 0, 0, tiled=True)
    p = kernel_call(
        functools.partial(sum_kernel, (slices * cuts) ** -0.5),
        (8, 2 * outs, rows),
        [VMEM],
        (2**18, 2**20),
        "sum",
    )(p)

    with jax.named_scope("last_move"):
        group = [(f + LAST) % 8 for f in range(8)]
        p = lax.all_to_all(p, FAR, 0, 0, tiled=True, axis_index_groups=[group])
    p = kernel_call(finish_kernel, (outs, 2, rows), [VMEM], (2**14, 2**17), "finish")(p)
    return p.reshape(1, outs, 2, rows)


def solution(mesh):
    fine = Mesh(mesh.devices.reshape([n for _, n in PARTS]), [name for name, _ in PARTS])
    return jax.shard_map(
        shards,
        mesh=fine,
        in_specs=(
            P(CUTS, None, MODE, None, None),
            P(CUTS, None, None, MODE),
            P(CUTS, None, None, None),
        ),
        out_specs=P(CUTS + MODE, None, None, None),
        check_vma=False,
    )
```

```python
import functools

import jax
import jax.numpy as jnp
from jax import lax
from jax.experimental import pallas as pl
from jax.experimental.pallas import tpu as pltpu
from jax.sharding import Mesh
from jax.sharding import PartitionSpec as P

PARTS = (("yh", 2), ("core", 2), ("yl", 2), ("x", 4), ("za", 8), ("zb", 2))
CUTS = ("yh", "core")
MODE = ("yl", "x", "za", "zb")
NEAR = ("yl", "x", "zb")
FAR = "za"

F32 = jnp.float32
LANES = 128
MID = 6
HALF = 2
LAST = 4
ORDER = [yl * 8 + x * 2 + zb for x in (3, 1, 2, 0) for yl in (1, 0) for zb in range(2)]
SMEM = pl.BlockSpec(memory_space=pltpu.SMEM)
VMEM = pl.BlockSpec(memory_space=pltpu.VMEM)
ANY = pl.BlockSpec(memory_space=pl.ANY)


def swap_blocks(v):
    n = len(v)
    size = LANES // n
    block = lax.broadcasted_iota(jnp.int32, v[0].shape, 1) // size
    v = list(v)
    bit = 1
    while bit < n:
        low = (block & bit) == 0
        for i in range(n):
            if i & bit:
                continue
            a, b = v[i], v[i | bit]
            v[i] = jnp.where(low, a, pltpu.roll(b, size * bit, 1))
            v[i | bit] = jnp.where(low, pltpu.roll(a, LANES - size * bit, 1), b)
        bit *= 2
    return v


def pack_kernel(left_ref, right_ref, out_ref, held, right, piece, into, out_of):
    slices, _, near, depth, _ = left_ref.shape
    each = 2 * slices
    halves = [pl.ds(0, near // 2), pl.ds(near // 2, near // 2)]
    parts = [(i, half) for half in halves for i in range(each)]
    copies = []
    for n, (i, half) in enumerate(parts):
        copies.append(pltpu.make_async_copy(left_ref.at[i // 2, i % 2, half], held.at[i, half], into.at[n]))
        copies[-1].start()
    given = pltpu.make_async_copy(right_ref, right, into.at[len(parts)])
    given.start()
    last = []
    for n, (i, half) in enumerate(parts):
        copies[n].wait()
        to = out_ref.at[half, pl.ds(i * depth, depth), :]
        last.append(pltpu.make_async_copy(held.at[i, half], to, out_of.at[n]))
        last[-1].start()
    given.wait()
    width = right.shape[2]
    for t in range(near // each):
        lanes = pl.ds(t * LANES, LANES)
        w = swap_blocks([right[j % slices, j // slices, :, lanes] for j in range(each)])
        for g in range(each):
            piece[t * each + g] = w[g]
    to = out_ref.at[:, pl.ds(each * depth, width), :]
    last.append(pltpu.make_async_copy(piece, to, out_of.at[len(parts)]))
    last[-1].start()
    for copy in last:
        copy.wait()


def spread_kernel(far_ref, near_ref, out_ref):
    cuts, far, width, _ = out_ref.shape
    body = near_ref.shape[1] - cuts * width // near_ref.shape[0]
    for q87 in range(cuts):
        for q6 in range(2):
            for q0 in range(2):
                for q2 in range(2):
                    two = near_ref[ORDER.index(q87 * 4 + q6 * 2 + q2), pl.ds(body + q0, 2, stride=2), :]
                    out_ref[q87 ^ HALF, 0, pl.ds(q6 * 8 + q0 * 4 + q2 * 2, 2), :] = two
        for g in range(1, far):
            out_ref[q87 ^ HALF, g] = out_ref[q87 ^ HALF, 0]


def close_kernel(far_ref, coef_ref, left_ref, out_ref, *piece_refs):
    heads = left_ref.shape[0]
    outs = coef_ref.shape[2]
    first = far_ref[0] * 2
    rows = 8
    for s, piece_ref in enumerate(piece_refs):
        depth = piece_ref.shape[0]
        acc = [[None] * (depth // rows) for _ in range(2 * outs)]
        for h in range(heads):
            head = (ORDER[h] // 2) * 16 + first + ORDER[h] % 2
            co = [coef_ref[s, j // outs, j % outs, head] for j in range(2 * outs)]
            for kb in range(depth // rows):
                at = 2 * s * depth + kb * rows
                re = left_ref[h, pl.ds(at, rows), :]
                im = left_ref[h, pl.ds(at + depth, rows), :]
                for o in range(outs):
                    cre, cim = co[o], co[outs + o]
                    new_re = cre * re - cim * im
                    new_im = cre * im + cim * re
                    if h:
                        new_re, new_im = acc[o][kb] + new_re, acc[outs + o][kb] + new_im
                    acc[o][kb], acc[outs + o][kb] = new_re, new_im
        for kb in range(depth // rows):
            for j in range(2 * outs):
                lanes = pl.ds(j * LANES, LANES)
                piece_ref[pl.ds(kb * rows, rows), lanes] = acc[j][kb]
                out_ref[pl.ds(s * depth + kb * rows, rows), lanes] = acc[j][kb]


def join_kernel(cut_ref, right_ref, *refs):
    *x_refs, out_ref, lhs, rhs = refs
    depth, wide = x_refs[2].shape
    slices = len(x_refs) // 2 - 1
    x_refs = [x.at[pl.ds(s * depth, depth), :] for x in x_refs[:2] for s in range(slices)] + x_refs[2:]
    half = wide // 2
    first = lax.broadcasted_iota(jnp.int32, (8, LANES), 0) < 4
    for i in range(4):
        cut = cut_ref[0] ^ (i ^ HALF)
        lanes = pl.ds(i * LANES, LANES)
        for t in range(4):
            for q6 in range(2):
                at = pl.ds(q6 * 8, 8)
                low = right_ref[cut, (2 * t - MID) % 8, at, :]
                high = right_ref[cut, (2 * t + 1 - MID) % 8, at, :]
                to = (q6 * 8 + t * 2) * 8
                lhs[pl.ds(to, 8), lanes] = jnp.where(first, low, pltpu.roll(high, 4, 0))
                lhs[pl.ds(to + 8, 8), lanes] = jnp.where(first, pltpu.roll(low, 4, 0), high)
        for s in range(slices):
            x_ref = x_refs[i * slices + s]
            re = pl.ds((2 * i * slices + s) * depth, depth)
            im = pl.ds(((2 * i + 1) * slices + s) * depth, depth)
            rhs[re, :] = x_ref[...]
            rhs[im, :half] = -x_ref[:, half:]
            rhs[im, half:] = x_ref[:, :half]
    for j in range(0, wide // LANES, 2):
        right = rhs[:, pl.ds(j * LANES, 2 * LANES)]
        out = jnp.dot(lhs[...], right, precision=lax.Precision.HIGHEST, preferred_element_type=F32)
        out_ref[:, j, :, :] = out[:, :LANES].reshape(16, 8, LANES)
        out_ref[:, j + 1, :, :] = out[:, LANES:].reshape(16, 8, LANES)


def sum_kernel(scale, parts_ref, out_ref):
    for j in range(parts_ref.shape[1]):
        total = parts_ref[0, j]
        for i in range(1, parts_ref.shape[0]):
            total = total + parts_ref[i, j]
        out_ref[:, j, :] = pltpu.roll(total * scale, (8 - LAST) % 8, 0)


def finish_kernel(parts_ref, out_ref):
    total = parts_ref[0]
    for i in range(1, parts_ref.shape[0]):
        total = total + parts_ref[i]
    outs = out_ref.shape[0]
    for c in range(2):
        for o in range(outs):
            out_ref[o, pl.ds(c, 1), :] = total[c * outs + o : c * outs + o + 1, :]


def kernel_call(body, shape, specs, cost, name, scratch=(), vmem=16, to=VMEM):
    flops, size = cost
    return pl.pallas_call(
        body,
        out_shape=jax.tree.map(lambda n: jax.ShapeDtypeStruct(n, F32), shape, is_leaf=lambda n: isinstance(n, tuple)),
        in_specs=specs,
        out_specs=to,
        scratch_shapes=scratch,
        compiler_params=pltpu.CompilerParams(vmem_limit_bytes=vmem * 2**20),
        cost_estimate=pl.CostEstimate(flops=flops, bytes_accessed=size, transcendentals=0),
        name=name,
    )


def shards(left_tensor, right_tensor, closing_tensor):
    slices, _, _, depth, rows = left_tensor.shape
    width = right_tensor.shape[3]
    outs = closing_tensor.shape[3]
    near = 16
    kk = depth // near
    body = slices * 2 * kk
    here = lax.axis_index(FAR).reshape(1)

    x = kernel_call(
        pack_kernel,
        (near, body + width, LANES),
        [ANY, ANY],
        (0, 2**21),
        "pack",
        [
            pltpu.VMEM((slices * 2, near, kk, rows), F32),
            pltpu.VMEM((slices, 2, width, depth), F32),
            pltpu.VMEM((near, width, LANES), F32),
            pltpu.SemaphoreType.DMA((slices * 4 + 1,)),
            pltpu.SemaphoreType.DMA((slices * 4 + 1,)),
        ],
        60,
        ANY,
    )(left_tensor.reshape(slices, 2, near, kk, rows), right_tensor.transpose(0, 1, 3, 2))

    with jax.named_scope("near_move"):
        x = lax.all_to_all(x, NEAR, 0, 0, tiled=True, axis_index_groups=[ORDER])

    cuts = 4
    r = kernel_call(
        spread_kernel, (cuts, 8, near * width // cuts, LANES), [SMEM, VMEM], (0, 2**18), "spread"
    )(here, x)
    with jax.named_scope("right_move"):
        r = r.reshape(cuts * 8, near * width // cuts, LANES)
        group = [(c ^ HALF) * 8 + (f + MID) % 8 for c in range(cuts) for f in range(8)]
        r = lax.all_to_all(r, CUTS + (FAR,), 0, 0, tiled=True, axis_index_groups=[group])
        r = r.reshape(cuts, 8, near * width // cuts, LANES)

    swap = [(0, 1), (1, 0)]
    wide = 2 * outs * rows
    x0, *pieces = kernel_call(
        close_kernel,
        [(slices * kk, wide)] + [(kk, wide)] * slices,
        [SMEM, SMEM, VMEM],
        (2**22, 6 * 2**18),
        "close",
        to=[VMEM] * (1 + slices),
    )(here, closing_tensor.transpose(0, 1, 3, 2), x)
    with jax.named_scope("cuts_gather"):
        x2 = [lax.ppermute(pieces[0], "yh", swap)]
        x1 = lax.ppermute(x0, "core", swap)
        *pieces, x1 = lax.optimization_barrier((*pieces, x1))
        x2 += [lax.ppermute(piece, "yh", swap) for piece in pieces[1:]]
        x3 = [lax.ppermute(piece, "core", swap) for piece in x2]

    p = kernel_call(
        join_kernel,
        (near, 2 * outs, 8, rows),
        [SMEM] + [VMEM] * (3 + 2 * slices),
        (2**27, 2**21),
        "join",
        [pltpu.VMEM((128, cuts * LANES), F32), pltpu.VMEM((2 * cuts * slices * kk, wide), F32)],
    )(lax.axis_index(CUTS).reshape(1), r, x0, x1, *x2, *x3)

    with jax.named_scope("sum_move"):
        p = lax.all_to_all(p, NEAR, 0, 0, tiled=True)
    p = kernel_call(
        functools.partial(sum_kernel, (slices * cuts) ** -0.5),
        (8, 2 * outs, rows),
        [VMEM],
        (2**18, 2**20),
        "sum",
    )(p)

    with jax.named_scope("last_move"):
        group = [(f + LAST) % 8 for f in range(8)]
        p = lax.all_to_all(p, FAR, 0, 0, tiled=True, axis_index_groups=[group])
    p = kernel_call(finish_kernel, (outs, 2, rows), [VMEM], (2**14, 2**17), "finish")(p)
    return p.reshape(1, outs, 2, rows)


def solution(mesh):
    fine = Mesh(mesh.devices.reshape([n for _, n in PARTS]), [name for name, _ in PARTS])
    return jax.shard_map(
        shards,
        mesh=fine,
        in_specs=(
            P(CUTS, None, MODE, None, None),
            P(CUTS, None, None, MODE),
            P(CUTS, None, None, None),
        ),
        out_specs=P(CUTS + MODE, None, None, None),
        check_vma=False,
    )
```

```python
import functools

import jax
import jax.numpy as jnp
from jax import lax
from jax.experimental import pallas as pl
from jax.experimental.pallas import tpu as pltpu
from jax.sharding import Mesh
from jax.sharding import PartitionSpec as P

PARTS = (("yh", 2), ("core", 2), ("yl", 2), ("x", 4), ("za", 8), ("zb", 2))
CUTS = ("yh", "core")
MODE = ("yl", "x", "za", "zb")
NEAR = ("yl", "x", "zb")
FAR = "za"

F32 = jnp.float32
LANES = 128
MID = 6
HALF = 2
LAST = 4
ORDER = [yl * 8 + x * 2 + zb for x in (3, 1, 2, 0) for yl in (1, 0) for zb in range(2)]
SMEM = pl.BlockSpec(memory_space=pltpu.SMEM)
VMEM = pl.BlockSpec(memory_space=pltpu.VMEM)
ANY = pl.BlockSpec(memory_space=pl.ANY)


def swap_blocks(v):
    n = len(v)
    size = LANES // n
    block = lax.broadcasted_iota(jnp.int32, v[0].shape, 1) // size
    v = list(v)
    bit = 1
    while bit < n:
        low = (block & bit) == 0
        for i in range(n):
            if i & bit:
                continue
            a, b = v[i], v[i | bit]
            v[i] = jnp.where(low, a, pltpu.roll(b, size * bit, 1))
            v[i | bit] = jnp.where(low, pltpu.roll(a, LANES - size * bit, 1), b)
        bit *= 2
    return v


def pack_kernel(left_ref, right_ref, out_ref, held, right, piece, into, out_of):
    slices, _, near, depth, _ = left_ref.shape
    each = 2 * slices
    halves = [pl.ds(0, near // 2), pl.ds(near // 2, near // 2)]
    parts = [(i, half) for half in halves for i in range(each)]
    copies = []
    for n, (i, half) in enumerate(parts):
        copies.append(pltpu.make_async_copy(left_ref.at[i // 2, i % 2, half], held.at[i, half], into.at[n]))
        copies[-1].start()
    given = pltpu.make_async_copy(right_ref, right, into.at[len(parts)])
    given.start()
    last = []
    for n, (i, half) in enumerate(parts):
        copies[n].wait()
        to = out_ref.at[half, pl.ds(i * depth, depth), :]
        last.append(pltpu.make_async_copy(held.at[i, half], to, out_of.at[n]))
        last[-1].start()
    given.wait()
    width = right.shape[2]
    for t in range(near // each):
        lanes = pl.ds(t * LANES, LANES)
        w = swap_blocks([right[j % slices, j // slices, :, lanes] for j in range(each)])
        for g in range(each):
            piece[t * each + g] = w[g]
    to = out_ref.at[:, pl.ds(each * depth, width), :]
    last.append(pltpu.make_async_copy(piece, to, out_of.at[len(parts)]))
    last[-1].start()
    for copy in last:
        copy.wait()


def spread_kernel(coef_ref, near_ref, out_ref):
    cuts, far, width, _ = out_ref.shape
    body = near_ref.shape[1] - cuts * width // near_ref.shape[0]
    for q87 in range(cuts):
        for q6 in range(2):
            for q0 in range(2):
                for q2 in range(2):
                    two = near_ref[ORDER.index(q87 * 4 + q6 * 2 + q2), pl.ds(body + q0, 2, stride=2), :]
                    out_ref[q87 ^ HALF, 0, pl.ds(q6 * 8 + q0 * 4 + q2 * 2, 2), :] = two
        for g in range(1, far):
            out_ref[q87 ^ HALF, g] = out_ref[q87 ^ HALF, 0]


def coef_kernel(far_ref, closing_ref, out_ref):
    slices, heads, each, _ = out_ref.shape
    first = far_ref[0] * 2
    lane = lax.broadcasted_iota(jnp.int32, (each, LANES), 1)
    for s in range(slices):
        rows = closing_ref[pl.ds(s * each, each), :]
        for h in range(heads):
            head = (ORDER[h] // 2) * 16 + first + ORDER[h] % 2
            one = jnp.sum(jnp.where(lane == head, rows, 0.0), axis=1, keepdims=True)
            out_ref[s, h] = jnp.broadcast_to(one, (each, LANES))


def close_kernel(coef_ref, left_ref, out_ref, *piece_refs):
    heads = left_ref.shape[0]
    outs = coef_ref.shape[2] // 2
    rows = 8
    for s, piece_ref in enumerate(piece_refs):
        depth = piece_ref.shape[0]
        acc = [[None] * (depth // rows) for _ in range(2 * outs)]
        for h in range(heads):
            co = [jnp.broadcast_to(coef_ref[s, h, pl.ds(j, 1), :], (rows, LANES)) for j in range(2 * outs)]
            for kb in range(depth // rows):
                at = 2 * s * depth + kb * rows
                re = left_ref[h, pl.ds(at, rows), :]
                im = left_ref[h, pl.ds(at + depth, rows), :]
                for o in range(outs):
                    cre, cim = co[o], co[outs + o]
                    new_re = cre * re - cim * im
                    new_im = cre * im + cim * re
                    if h:
                        new_re, new_im = acc[o][kb] + new_re, acc[outs + o][kb] + new_im
                    acc[o][kb], acc[outs + o][kb] = new_re, new_im
        for kb in range(depth // rows):
            for j in range(2 * outs):
                lanes = pl.ds(j * LANES, LANES)
                piece_ref[pl.ds(kb * rows, rows), lanes] = acc[j][kb]
                out_ref[pl.ds(s * depth + kb * rows, rows), lanes] = acc[j][kb]


def join_kernel(cut_ref, right_ref, *refs):
    *x_refs, out_ref, lhs, rhs = refs
    depth, wide = x_refs[2].shape
    slices = len(x_refs) // 2 - 1
    x_refs = [x.at[pl.ds(s * depth, depth), :] for x in x_refs[:2] for s in range(slices)] + x_refs[2:]
    half = wide // 2
    first = lax.broadcasted_iota(jnp.int32, (8, LANES), 0) < 4
    for i in range(4):
        cut = cut_ref[0] ^ (i ^ HALF)
        lanes = pl.ds(i * LANES, LANES)
        for t in range(4):
            for q6 in range(2):
                at = pl.ds(q6 * 8, 8)
                low = right_ref[cut, (2 * t - MID) % 8, at, :]
                high = right_ref[cut, (2 * t + 1 - MID) % 8, at, :]
                to = (q6 * 8 + t * 2) * 8
                lhs[pl.ds(to, 8), lanes] = jnp.where(first, low, pltpu.roll(high, 4, 0))
                lhs[pl.ds(to + 8, 8), lanes] = jnp.where(first, pltpu.roll(low, 4, 0), high)
        for s in range(slices):
            x_ref = x_refs[i * slices + s]
            re = pl.ds((2 * i * slices + s) * depth, depth)
            im = pl.ds(((2 * i + 1) * slices + s) * depth, depth)
            rhs[re, :] = x_ref[...]
            rhs[im, :half] = -x_ref[:, half:]
            rhs[im, half:] = x_ref[:, :half]
    for j in range(0, wide // LANES, 2):
        right = rhs[:, pl.ds(j * LANES, 2 * LANES)]
        out = jnp.dot(lhs[...], right, precision=lax.Precision.HIGHEST, preferred_element_type=F32)
        out_ref[:, j, :, :] = out[:, :LANES].reshape(16, 8, LANES)
        out_ref[:, j + 1, :, :] = out[:, LANES:].reshape(16, 8, LANES)


def sum_kernel(scale, parts_ref, out_ref):
    for j in range(parts_ref.shape[1]):
        total = parts_ref[0, j]
        for i in range(1, parts_ref.shape[0]):
            total = total + parts_ref[i, j]
        out_ref[:, j, :] = pltpu.roll(total * scale, (8 - LAST) % 8, 0)


def finish_kernel(parts_ref, out_ref):
    total = parts_ref[0]
    for i in range(1, parts_ref.shape[0]):
        total = total + parts_ref[i]
    outs = out_ref.shape[0]
    for c in range(2):
        for o in range(outs):
            out_ref[o, pl.ds(c, 1), :] = total[c * outs + o : c * outs + o + 1, :]


def kernel_call(body, shape, specs, cost, name, scratch=(), vmem=16, to=VMEM):
    flops, size = cost
    return pl.pallas_call(
        body,
        out_shape=jax.tree.map(lambda n: jax.ShapeDtypeStruct(n, F32), shape, is_leaf=lambda n: isinstance(n, tuple)),
        in_specs=specs,
        out_specs=to,
        scratch_shapes=scratch,
        compiler_params=pltpu.CompilerParams(vmem_limit_bytes=vmem * 2**20),
        cost_estimate=pl.CostEstimate(flops=flops, bytes_accessed=size, transcendentals=0),
        name=name,
    )


def shards(left_tensor, right_tensor, closing_tensor):
    slices, _, _, depth, rows = left_tensor.shape
    width = right_tensor.shape[3]
    outs = closing_tensor.shape[3]
    near = 16
    kk = depth // near
    body = slices * 2 * kk
    here = lax.axis_index(FAR).reshape(1)

    x = kernel_call(
        pack_kernel,
        (near, body + width, LANES),
        [ANY, ANY],
        (0, 2**21),
        "pack",
        [
            pltpu.VMEM((slices * 2, near, kk, rows), F32),
            pltpu.VMEM((slices, 2, width, depth), F32),
            pltpu.VMEM((near, width, LANES), F32),
            pltpu.SemaphoreType.DMA((slices * 4 + 1,)),
            pltpu.SemaphoreType.DMA((slices * 4 + 1,)),
        ],
        60,
        ANY,
    )(left_tensor.reshape(slices, 2, near, kk, rows), right_tensor.transpose(0, 1, 3, 2))

    with jax.named_scope("near_move"):
        x = lax.all_to_all(x, NEAR, 0, 0, tiled=True, axis_index_groups=[ORDER])

    heads = closing_tensor.shape[2]
    co = kernel_call(
        coef_kernel, (slices, near, 2 * outs, LANES), [SMEM, VMEM], (2**18, 2**18), "coef"
    )(here, closing_tensor.transpose(0, 1, 3, 2).reshape(slices * 2 * outs, heads))

    cuts = 4
    r = kernel_call(
        spread_kernel, (cuts, 8, near * width // cuts, LANES), [ANY, VMEM], (0, 2**18), "spread"
    )(co, x)
    with jax.named_scope("right_move"):
        r = r.reshape(cuts * 8, near * width // cuts, LANES)
        group = [(c ^ HALF) * 8 + (f + MID) % 8 for c in range(cuts) for f in range(8)]
        r = lax.all_to_all(r, CUTS + (FAR,), 0, 0, tiled=True, axis_index_groups=[group])
        r = r.reshape(cuts, 8, near * width // cuts, LANES)

    swap = [(0, 1), (1, 0)]
    wide = 2 * outs * rows
    x0, *pieces = kernel_call(
        close_kernel,
        [(slices * kk, wide)] + [(kk, wide)] * slices,
        [VMEM, VMEM],
        (2**22, 6 * 2**18),
        "close",
        to=[VMEM] * (1 + slices),
    )(co, x)
    with jax.named_scope("cuts_gather"):
        x2 = [lax.ppermute(piece, "yh", swap) for piece in pieces]
        x1 = lax.ppermute(x0, "core", swap)
        x3 = [lax.ppermute(piece, "core", swap) for piece in x2]

    p = kernel_call(
        join_kernel,
        (near, 2 * outs, 8, rows),
        [SMEM] + [VMEM] * (3 + 2 * slices),
        (2**27, 2**21),
        "join",
        [pltpu.VMEM((128, cuts * LANES), F32), pltpu.VMEM((2 * cuts * slices * kk, wide), F32)],
    )(lax.axis_index(CUTS).reshape(1), r, x0, x1, *x2, *x3)

    with jax.named_scope("sum_move"):
        p = lax.all_to_all(p, NEAR, 0, 0, tiled=True)
    p = kernel_call(
        functools.partial(sum_kernel, (slices * cuts) ** -0.5),
        (8, 2 * outs, rows),
        [VMEM],
        (2**18, 2**20),
        "sum",
    )(p)

    with jax.named_scope("last_move"):
        group = [(f + LAST) % 8 for f in range(8)]
        p = lax.all_to_all(p, FAR, 0, 0, tiled=True, axis_index_groups=[group])
    p = kernel_call(finish_kernel, (outs, 2, rows), [VMEM], (2**14, 2**17), "finish")(p)
    return p.reshape(1, outs, 2, rows)


def solution(mesh):
    fine = Mesh(mesh.devices.reshape([n for _, n in PARTS]), [name for name, _ in PARTS])
    return jax.shard_map(
        shards,
        mesh=fine,
        in_specs=(
            P(CUTS, None, MODE, None, None),
            P(CUTS, None, None, MODE),
            P(CUTS, None, None, None),
        ),
        out_specs=P(CUTS + MODE, None, None, None),
        check_vma=False,
    )
```

```python
import functools

import jax
import jax.numpy as jnp
from jax import lax
from jax.experimental import pallas as pl
from jax.experimental.pallas import tpu as pltpu
from jax.sharding import Mesh
from jax.sharding import PartitionSpec as P

PARTS = (("yh", 2), ("core", 2), ("yl", 2), ("x", 4), ("za", 8), ("zb", 2))
CUTS = ("yh", "core")
MODE = ("yl", "x", "za", "zb")
NEAR = ("yl", "x", "zb")
FAR = "za"

F32 = jnp.float32
LANES = 128
MID = 6
HALF = 2
LAST = 4
ORDER = [yl * 8 + x * 2 + zb for x in (3, 1, 2, 0) for yl in (1, 0) for zb in range(2)]
SMEM = pl.BlockSpec(memory_space=pltpu.SMEM)
VMEM = pl.BlockSpec(memory_space=pltpu.VMEM)
ANY = pl.BlockSpec(memory_space=pl.ANY)


def swap_blocks(v):
    n = len(v)
    size = LANES // n
    block = lax.broadcasted_iota(jnp.int32, v[0].shape, 1) // size
    v = list(v)
    bit = 1
    while bit < n:
        low = (block & bit) == 0
        for i in range(n):
            if i & bit:
                continue
            a, b = v[i], v[i | bit]
            v[i] = jnp.where(low, a, pltpu.roll(b, size * bit, 1))
            v[i | bit] = jnp.where(low, pltpu.roll(a, LANES - size * bit, 1), b)
        bit *= 2
    return v


def pack_kernel(left_ref, right_ref, out_ref, held, right, piece, into, out_of):
    slices, _, near, depth, _ = left_ref.shape
    each = 2 * slices
    halves = [pl.ds(0, near // 2), pl.ds(near // 2, near // 2)]
    parts = [(i, half) for half in halves for i in range(each)]
    copies = []
    for n, (i, half) in enumerate(parts):
        copies.append(pltpu.make_async_copy(left_ref.at[i // 2, i % 2, half], held.at[i, half], into.at[n]))
        copies[-1].start()
    given = pltpu.make_async_copy(right_ref, right, into.at[len(parts)])
    given.start()
    last = []
    for n, (i, half) in enumerate(parts):
        copies[n].wait()
        to = out_ref.at[half, pl.ds(i * depth, depth), :]
        last.append(pltpu.make_async_copy(held.at[i, half], to, out_of.at[n]))
        last[-1].start()
    given.wait()
    width = right.shape[2]
    for t in range(near // each):
        lanes = pl.ds(t * LANES, LANES)
        w = swap_blocks([right[j % slices, j // slices, :, lanes] for j in range(each)])
        for g in range(each):
            piece[t * each + g] = w[g]
    to = out_ref.at[:, pl.ds(each * depth, width), :]
    last.append(pltpu.make_async_copy(piece, to, out_of.at[len(parts)]))
    last[-1].start()
    for copy in last:
        copy.wait()


def spread_kernel(coef_ref, near_ref, out_ref):
    cuts, far, width, _ = out_ref.shape
    body = near_ref.shape[1] - cuts * width // near_ref.shape[0]
    for q87 in range(cuts):
        for q6 in range(2):
            for q0 in range(2):
                for q2 in range(2):
                    two = near_ref[ORDER.index(q87 * 4 + q6 * 2 + q2), pl.ds(body + q0, 2, stride=2), :]
                    out_ref[q87 ^ HALF, 0, pl.ds(q6 * 8 + q0 * 4 + q2 * 2, 2), :] = two
        for g in range(1, far):
            out_ref[q87 ^ HALF, g] = out_ref[q87 ^ HALF, 0]


def coef_kernel(far_ref, closing_ref, out_ref):
    slices, heads, each, _ = out_ref.shape
    first = far_ref[0] * 2
    lane = lax.broadcasted_iota(jnp.int32, (each, LANES), 1)
    for s in range(slices):
        rows = closing_ref[pl.ds(s * each, each), :]
        for h in range(heads):
            head = (ORDER[h] // 2) * 16 + first + ORDER[h] % 2
            one = jnp.sum(jnp.where(lane == head, rows, 0.0), axis=1, keepdims=True)
            out_ref[s, h] = jnp.broadcast_to(one, (each, LANES))


def close_kernel(coef_ref, left_ref, out_ref, *piece_refs):
    heads = left_ref.shape[0]
    outs = coef_ref.shape[2] // 2
    rows = 8
    for s, piece_ref in enumerate(piece_refs):
        depth = piece_ref.shape[0]
        acc = [[None] * (depth // rows) for _ in range(2 * outs)]
        for h in range(heads):
            co = [jnp.broadcast_to(coef_ref[s, h, pl.ds(j, 1), :], (rows, LANES)) for j in range(2 * outs)]
            for kb in range(depth // rows):
                at = 2 * s * depth + kb * rows
                re = left_ref[h, pl.ds(at, rows), :]
                im = left_ref[h, pl.ds(at + depth, rows), :]
                for o in range(outs):
                    cre, cim = co[o], co[outs + o]
                    new_re = cre * re - cim * im
                    new_im = cre * im + cim * re
                    if h:
                        new_re, new_im = acc[o][kb] + new_re, acc[outs + o][kb] + new_im
                    acc[o][kb], acc[outs + o][kb] = new_re, new_im
        for kb in range(depth // rows):
            for j in range(2 * outs):
                lanes = pl.ds(j * LANES, LANES)
                piece_ref[pl.ds(kb * rows, rows), lanes] = acc[j][kb]
                out_ref[pl.ds(s * depth + kb * rows, rows), lanes] = acc[j][kb]


def join_kernel(cut_ref, right_ref, *refs):
    *x_refs, out_ref, lhs, rhs = refs
    depth, wide = x_refs[2].shape
    slices = len(x_refs) // 2 - 1
    x_refs = [x.at[pl.ds(s * depth, depth), :] for x in x_refs[:2] for s in range(slices)] + x_refs[2:]
    half = wide // 2
    first = lax.broadcasted_iota(jnp.int32, (8, LANES), 0) < 4
    for i in range(4):
        cut = cut_ref[0] ^ (i ^ HALF)
        lanes = pl.ds(i * LANES, LANES)
        for t in range(4):
            for q6 in range(2):
                at = pl.ds(q6 * 8, 8)
                low = right_ref[cut, (2 * t - MID) % 8, at, :]
                high = right_ref[cut, (2 * t + 1 - MID) % 8, at, :]
                to = (q6 * 8 + t * 2) * 8
                lhs[pl.ds(to, 8), lanes] = jnp.where(first, low, pltpu.roll(high, 4, 0))
                lhs[pl.ds(to + 8, 8), lanes] = jnp.where(first, pltpu.roll(low, 4, 0), high)
        for s in range(slices):
            x_ref = x_refs[i * slices + s]
            re = pl.ds((2 * i * slices + s) * depth, depth)
            im = pl.ds(((2 * i + 1) * slices + s) * depth, depth)
            rhs[re, :] = x_ref[...]
            rhs[im, :half] = -x_ref[:, half:]
            rhs[im, half:] = x_ref[:, :half]
    for j in range(0, wide // LANES, 2):
        right = rhs[:, pl.ds(j * LANES, 2 * LANES)]
        out = jnp.dot(lhs[...], right, precision=lax.Precision.HIGHEST, preferred_element_type=F32)
        out_ref[:, j, :, :] = out[:, :LANES].reshape(16, 8, LANES)
        out_ref[:, j + 1, :, :] = out[:, LANES:].reshape(16, 8, LANES)


def sum_kernel(scale, tie_ref, parts_ref, out_ref):
    for j in range(parts_ref.shape[1]):
        total = parts_ref[0, j]
        for i in range(1, parts_ref.shape[0]):
            total = total + parts_ref[i, j]
        out_ref[:, j, :] = pltpu.roll(total * scale, (8 - LAST) % 8, 0)


def finish_kernel(tie_ref, parts_ref, out_ref):
    total = parts_ref[0]
    for i in range(1, parts_ref.shape[0]):
        total = total + parts_ref[i]
    outs = out_ref.shape[0]
    for c in range(2):
        for o in range(outs):
            out_ref[o, pl.ds(c, 1), :] = total[c * outs + o : c * outs + o + 1, :]


def kernel_call(body, shape, specs, cost, name, scratch=(), vmem=16, to=VMEM):
    flops, size = cost
    return pl.pallas_call(
        body,
        out_shape=jax.tree.map(lambda n: jax.ShapeDtypeStruct(n, F32), shape, is_leaf=lambda n: isinstance(n, tuple)),
        in_specs=specs,
        out_specs=to,
        scratch_shapes=scratch,
        compiler_params=pltpu.CompilerParams(vmem_limit_bytes=vmem * 2**20),
        cost_estimate=pl.CostEstimate(flops=flops, bytes_accessed=size, transcendentals=0),
        name=name,
    )


def shards(left_tensor, right_tensor, closing_tensor):
    slices, _, _, depth, rows = left_tensor.shape
    width = right_tensor.shape[3]
    outs = closing_tensor.shape[3]
    near = 16
    kk = depth // near
    body = slices * 2 * kk
    here = lax.axis_index(FAR).reshape(1)

    x = kernel_call(
        pack_kernel,
        (near, body + width, LANES),
        [ANY, ANY],
        (0, 2**21),
        "pack",
        [
            pltpu.VMEM((slices * 2, near, kk, rows), F32),
            pltpu.VMEM((slices, 2, width, depth), F32),
            pltpu.VMEM((near, width, LANES), F32),
            pltpu.SemaphoreType.DMA((slices * 4 + 1,)),
            pltpu.SemaphoreType.DMA((slices * 4 + 1,)),
        ],
        60,
        ANY,
    )(left_tensor.reshape(slices, 2, near, kk, rows), right_tensor.transpose(0, 1, 3, 2))

    with jax.named_scope("near_move"):
        x = lax.all_to_all(x, NEAR, 0, 0, tiled=True, axis_index_groups=[ORDER])

    heads = closing_tensor.shape[2]
    co = kernel_call(
        coef_kernel, (slices, near, 2 * outs, LANES), [SMEM, VMEM], (2**18, 2**18), "coef"
    )(here, closing_tensor.transpose(0, 1, 3, 2).reshape(slices * 2 * outs, heads))

    cuts = 4
    r = kernel_call(
        spread_kernel, (cuts, 8, near * width // cuts, LANES), [ANY, VMEM], (0, 2**18), "spread"
    )(co, x)
    with jax.named_scope("right_move"):
        r = r.reshape(cuts * 8, near * width // cuts, LANES)
        group = [(c ^ HALF) * 8 + (f + MID) % 8 for c in range(cuts) for f in range(8)]
        r = lax.all_to_all(r, CUTS + (FAR,), 0, 0, tiled=True, axis_index_groups=[group])
        r = r.reshape(cuts, 8, near * width // cuts, LANES)

    swap = [(0, 1), (1, 0)]
    wide = 2 * outs * rows
    x0, *pieces = kernel_call(
        close_kernel,
        [(slices * kk, wide)] + [(kk, wide)] * slices,
        [VMEM, VMEM],
        (2**22, 6 * 2**18),
        "close",
        to=[VMEM] * (1 + slices),
    )(co, x)
    with jax.named_scope("cuts_gather"):
        x2 = [lax.ppermute(piece, "yh", swap) for piece in pieces]
        x1 = lax.ppermute(x0, "core", swap)
        x3 = [lax.ppermute(piece, "core", swap) for piece in x2]

    p = kernel_call(
        join_kernel,
        (near, 2 * outs, 8, rows),
        [SMEM] + [VMEM] * (3 + 2 * slices),
        (2**27, 2**21),
        "join",
        [pltpu.VMEM((128, cuts * LANES), F32), pltpu.VMEM((2 * cuts * slices * kk, wide), F32)],
    )(lax.axis_index(CUTS).reshape(1), r, x0, x1, *x2, *x3)

    with jax.named_scope("sum_move"):
        tie = p[:1, :1]
        p = lax.all_to_all(p, NEAR, 0, 0, tiled=True)
    p = kernel_call(
        functools.partial(sum_kernel, (slices * cuts) ** -0.5),
        (8, 2 * outs, rows),
        [ANY, VMEM],
        (2**18, 2**20),
        "sum",
    )(tie, p)

    with jax.named_scope("last_move"):
        tie = p[:1]
        group = [(f + LAST) % 8 for f in range(8)]
        p = lax.all_to_all(p, FAR, 0, 0, tiled=True, axis_index_groups=[group])
    p = kernel_call(finish_kernel, (outs, 2, rows), [ANY, VMEM], (2**14, 2**17), "finish")(tie, p)
    return p.reshape(1, outs, 2, rows)


def solution(mesh):
    fine = Mesh(mesh.devices.reshape([n for _, n in PARTS]), [name for name, _ in PARTS])
    return jax.shard_map(
        shards,
        mesh=fine,
        in_specs=(
            P(CUTS, None, MODE, None, None),
            P(CUTS, None, None, MODE),
            P(CUTS, None, None, None),
        ),
        out_specs=P(CUTS + MODE, None, None, None),
        check_vma=False,
    )
```

```python
import functools

import jax
import jax.numpy as jnp
from jax import lax
from jax.experimental import pallas as pl
from jax.experimental.pallas import tpu as pltpu
from jax.sharding import Mesh
from jax.sharding import PartitionSpec as P

PARTS = (("yh", 2), ("core", 2), ("yl", 2), ("x", 4), ("za", 8), ("zb", 2))
CUTS = ("yh", "core")
MODE = ("yl", "x", "za", "zb")
NEAR = ("yl", "x", "zb")
FAR = "za"

F32 = jnp.float32
LANES = 128
MID = 5
HALF = 2
LAST = 4
ORDER = [yl * 8 + x * 2 + zb for x in (3, 1, 2, 0) for yl in (1, 0) for zb in range(2)]
SMEM = pl.BlockSpec(memory_space=pltpu.SMEM)
VMEM = pl.BlockSpec(memory_space=pltpu.VMEM)
ANY = pl.BlockSpec(memory_space=pl.ANY)


def swap_blocks(v):
    n = len(v)
    size = LANES // n
    block = lax.broadcasted_iota(jnp.int32, v[0].shape, 1) // size
    v = list(v)
    bit = 1
    while bit < n:
        low = (block & bit) == 0
        for i in range(n):
            if i & bit:
                continue
            a, b = v[i], v[i | bit]
            v[i] = jnp.where(low, a, pltpu.roll(b, size * bit, 1))
            v[i | bit] = jnp.where(low, pltpu.roll(a, LANES - size * bit, 1), b)
        bit *= 2
    return v


def pack_kernel(left_ref, right_ref, out_ref, held, right, piece, into, out_of):
    slices, _, near, depth, _ = left_ref.shape
    each = 2 * slices
    halves = [pl.ds(0, near // 2), pl.ds(near // 2, near // 2)]
    parts = [(i, half) for half in halves for i in range(each)]
    copies = []
    for n, (i, half) in enumerate(parts):
        copies.append(pltpu.make_async_copy(left_ref.at[i // 2, i % 2, half], held.at[i, half], into.at[n]))
        copies[-1].start()
    given = pltpu.make_async_copy(right_ref, right, into.at[len(parts)])
    given.start()
    last = []
    for n, (i, half) in enumerate(parts):
        copies[n].wait()
        to = out_ref.at[half, pl.ds(i * depth, depth), :]
        last.append(pltpu.make_async_copy(held.at[i, half], to, out_of.at[n]))
        last[-1].start()
    given.wait()
    width = right.shape[2]
    for t in range(near // each):
        lanes = pl.ds(t * LANES, LANES)
        w = swap_blocks([right[j % slices, j // slices, :, lanes] for j in range(each)])
        for g in range(each):
            piece[t * each + g] = w[g]
    to = out_ref.at[:, pl.ds(each * depth, width), :]
    last.append(pltpu.make_async_copy(piece, to, out_of.at[len(parts)]))
    last[-1].start()
    for copy in last:
        copy.wait()


def spread_kernel(coef_ref, near_ref, out_ref):
    cuts, far, width, _ = out_ref.shape
    body = near_ref.shape[1] - cuts * width // near_ref.shape[0]
    for q87 in range(cuts):
        for q6 in range(2):
            for q0 in range(2):
                for q2 in range(2):
                    two = near_ref[ORDER.index(q87 * 4 + q6 * 2 + q2), pl.ds(body + q0, 2, stride=2), :]
                    out_ref[q87 ^ HALF, 0, pl.ds(q6 * 8 + q0 * 4 + q2 * 2, 2), :] = two
        for g in range(1, far):
            out_ref[q87 ^ HALF, g] = out_ref[q87 ^ HALF, 0]


def coef_kernel(far_ref, closing_ref, out_ref):
    slices, heads, each, _ = out_ref.shape
    first = far_ref[0] * 2
    lane = lax.broadcasted_iota(jnp.int32, (each, LANES), 1)
    for s in range(slices):
        rows = closing_ref[pl.ds(s * each, each), :]
        for h in range(heads):
            head = (ORDER[h] // 2) * 16 + first + ORDER[h] % 2
            one = jnp.sum(jnp.where(lane == head, rows, 0.0), axis=1, keepdims=True)
            out_ref[s, h] = jnp.broadcast_to(one, (each, LANES))


def close_kernel(coef_ref, left_ref, out_ref, *piece_refs):
    heads = left_ref.shape[0]
    outs = coef_ref.shape[2] // 2
    rows = 8
    for s, piece_ref in enumerate(piece_refs):
        depth = piece_ref.shape[0]
        acc = [[None] * (depth // rows) for _ in range(2 * outs)]
        for h in range(heads):
            co = [jnp.broadcast_to(coef_ref[s, h, pl.ds(j, 1), :], (rows, LANES)) for j in range(2 * outs)]
            for kb in range(depth // rows):
                at = 2 * s * depth + kb * rows
                re = left_ref[h, pl.ds(at, rows), :]
                im = left_ref[h, pl.ds(at + depth, rows), :]
                for o in range(outs):
                    cre, cim = co[o], co[outs + o]
                    new_re = cre * re - cim * im
                    new_im = cre * im + cim * re
                    if h:
                        new_re, new_im = acc[o][kb] + new_re, acc[outs + o][kb] + new_im
                    acc[o][kb], acc[outs + o][kb] = new_re, new_im
        for kb in range(depth // rows):
            for j in range(2 * outs):
                lanes = pl.ds(j * LANES, LANES)
                piece_ref[pl.ds(kb * rows, rows), lanes] = acc[j][kb]
                out_ref[pl.ds(s * depth + kb * rows, rows), lanes] = acc[j][kb]


def join_kernel(cut_ref, right_ref, *refs):
    *x_refs, out_ref, lhs, rhs = refs
    depth, wide = x_refs[2].shape
    slices = len(x_refs) // 2 - 1
    x_refs = [x.at[pl.ds(s * depth, depth), :] for x in x_refs[:2] for s in range(slices)] + x_refs[2:]
    half = wide // 2
    first = lax.broadcasted_iota(jnp.int32, (8, LANES), 0) < 4
    for i in range(4):
        cut = cut_ref[0] ^ (i ^ HALF)
        lanes = pl.ds(i * LANES, LANES)
        for t in range(4):
            for q6 in range(2):
                at = pl.ds(q6 * 8, 8)
                low = right_ref[cut, (2 * t - MID) % 8, at, :]
                high = right_ref[cut, (2 * t + 1 - MID) % 8, at, :]
                to = (q6 * 8 + t * 2) * 8
                lhs[pl.ds(to, 8), lanes] = jnp.where(first, low, pltpu.roll(high, 4, 0))
                lhs[pl.ds(to + 8, 8), lanes] = jnp.where(first, pltpu.roll(low, 4, 0), high)
        for s in range(slices):
            x_ref = x_refs[i * slices + s]
            re = pl.ds((2 * i * slices + s) * depth, depth)
            im = pl.ds(((2 * i + 1) * slices + s) * depth, depth)
            rhs[re, :] = x_ref[...]
            rhs[im, :half] = -x_ref[:, half:]
            rhs[im, half:] = x_ref[:, :half]
    for j in range(0, wide // LANES, 2):
        right = rhs[:, pl.ds(j * LANES, 2 * LANES)]
        out = jnp.dot(lhs[...], right, precision=lax.Precision.HIGHEST, preferred_element_type=F32)
        out_ref[:, j, :, :] = out[:, :LANES].reshape(16, 8, LANES)
        out_ref[:, j + 1, :, :] = out[:, LANES:].reshape(16, 8, LANES)


def sum_kernel(scale, parts_ref, out_ref):
    for j in range(parts_ref.shape[1]):
        total = parts_ref[0, j]
        for i in range(1, parts_ref.shape[0]):
            total = total + parts_ref[i, j]
        out_ref[:, j, :] = pltpu.roll(total * scale, (8 - LAST) % 8, 0)


def finish_kernel(parts_ref, out_ref):
    total = parts_ref[0]
    for i in range(1, parts_ref.shape[0]):
        total = total + parts_ref[i]
    outs = out_ref.shape[0]
    for c in range(2):
        for o in range(outs):
            out_ref[o, pl.ds(c, 1), :] = total[c * outs + o : c * outs + o + 1, :]


def kernel_call(body, shape, specs, cost, name, scratch=(), vmem=16, to=VMEM):
    flops, size = cost
    return pl.pallas_call(
        body,
        out_shape=jax.tree.map(lambda n: jax.ShapeDtypeStruct(n, F32), shape, is_leaf=lambda n: isinstance(n, tuple)),
        in_specs=specs,
        out_specs=to,
        scratch_shapes=scratch,
        compiler_params=pltpu.CompilerParams(vmem_limit_bytes=vmem * 2**20),
        cost_estimate=pl.CostEstimate(flops=flops, bytes_accessed=size, transcendentals=0),
        name=name,
    )


def shards(left_tensor, right_tensor, closing_tensor):
    slices, _, _, depth, rows = left_tensor.shape
    width = right_tensor.shape[3]
    outs = closing_tensor.shape[3]
    near = 16
    kk = depth // near
    body = slices * 2 * kk
    here = lax.axis_index(FAR).reshape(1)

    x = kernel_call(
        pack_kernel,
        (near, body + width, LANES),
        [ANY, ANY],
        (0, 2**21),
        "pack",
        [
            pltpu.VMEM((slices * 2, near, kk, rows), F32),
            pltpu.VMEM((slices, 2, width, depth), F32),
            pltpu.VMEM((near, width, LANES), F32),
            pltpu.SemaphoreType.DMA((slices * 4 + 1,)),
            pltpu.SemaphoreType.DMA((slices * 4 + 1,)),
        ],
        60,
        ANY,
    )(left_tensor.reshape(slices, 2, near, kk, rows), right_tensor.transpose(0, 1, 3, 2))

    with jax.named_scope("near_move"):
        x = lax.all_to_all(x, NEAR, 0, 0, tiled=True, axis_index_groups=[ORDER])

    heads = closing_tensor.shape[2]
    co = kernel_call(
        coef_kernel, (slices, near, 2 * outs, LANES), [SMEM, VMEM], (2**18, 2**18), "coef"
    )(here, closing_tensor.transpose(0, 1, 3, 2).reshape(slices * 2 * outs, heads))

    cuts = 4
    r = kernel_call(
        spread_kernel, (cuts, 8, near * width // cuts, LANES), [ANY, VMEM], (0, 2**18), "spread"
    )(co, x)
    with jax.named_scope("right_move"):
        r = r.reshape(cuts * 8, near * width // cuts, LANES)
        group = [(c ^ HALF) * 8 + (f + MID) % 8 for c in range(cuts) for f in range(8)]
        r = lax.all_to_all(r, CUTS + (FAR,), 0, 0, tiled=True, axis_index_groups=[group])
        r = r.reshape(cuts, 8, near * width // cuts, LANES)

    swap = [(0, 1), (1, 0)]
    wide = 2 * outs * rows
    x0, *pieces = kernel_call(
        close_kernel,
        [(slices * kk, wide)] + [(kk, wide)] * slices,
        [VMEM, VMEM],
        (2**22, 6 * 2**18),
        "close",
        to=[VMEM] * (1 + slices),
    )(co, x)
    with jax.named_scope("cuts_gather"):
        x2 = [lax.ppermute(piece, "yh", swap) for piece in pieces]
        x1 = lax.ppermute(x0, "core", swap)
        x3 = [lax.ppermute(piece, "core", swap) for piece in x2]

    p = kernel_call(
        join_kernel,
        (near, 2 * outs, 8, rows),
        [SMEM] + [VMEM] * (3 + 2 * slices),
        (2**27, 2**21),
        "join",
        [pltpu.VMEM((128, cuts * LANES), F32), pltpu.VMEM((2 * cuts * slices * kk, wide), F32)],
    )(lax.axis_index(CUTS).reshape(1), r, x0, x1, *x2, *x3)

    with jax.named_scope("sum_move"):
        p = lax.all_to_all(p, NEAR, 0, 0, tiled=True)
    p = kernel_call(
        functools.partial(sum_kernel, (slices * cuts) ** -0.5),
        (8, 2 * outs, rows),
        [VMEM],
        (2**18, 2**20),
        "sum",
    )(p)

    with jax.named_scope("last_move"):
        group = [(f + LAST) % 8 for f in range(8)]
        p = lax.all_to_all(p, FAR, 0, 0, tiled=True, axis_index_groups=[group])
    p = kernel_call(finish_kernel, (outs, 2, rows), [VMEM], (2**14, 2**17), "finish")(p)
    return p.reshape(1, outs, 2, rows)


def solution(mesh):
    fine = Mesh(mesh.devices.reshape([n for _, n in PARTS]), [name for name, _ in PARTS])
    return jax.shard_map(
        shards,
        mesh=fine,
        in_specs=(
            P(CUTS, None, MODE, None, None),
            P(CUTS, None, None, MODE),
            P(CUTS, None, None, None),
        ),
        out_specs=P(CUTS + MODE, None, None, None),
        check_vma=False,
    )
```

```python
import functools

import jax
import jax.numpy as jnp
from jax import lax
from jax.experimental import pallas as pl
from jax.experimental.pallas import tpu as pltpu
from jax.sharding import Mesh
from jax.sharding import PartitionSpec as P

PARTS = (("yh", 2), ("core", 2), ("yl", 2), ("x", 4), ("za", 8), ("zb", 2))
CUTS = ("yh", "core")
MODE = ("yl", "x", "za", "zb")
NEAR = ("yl", "x", "zb")
FAR = "za"

F32 = jnp.float32
LANES = 128
MID = 6
HALF = 2
LAST = 4
ORDER = [yl * 8 + x * 2 + zb for x in (3, 1, 2, 0) for yl in (1, 0) for zb in range(2)]
SMEM = pl.BlockSpec(memory_space=pltpu.SMEM)
VMEM = pl.BlockSpec(memory_space=pltpu.VMEM)
ANY = pl.BlockSpec(memory_space=pl.ANY)


def swap_blocks(v):
    n = len(v)
    size = LANES // n
    block = lax.broadcasted_iota(jnp.int32, v[0].shape, 1) // size
    v = list(v)
    bit = 1
    while bit < n:
        low = (block & bit) == 0
        for i in range(n):
            if i & bit:
                continue
            a, b = v[i], v[i | bit]
            v[i] = jnp.where(low, a, pltpu.roll(b, size * bit, 1))
            v[i | bit] = jnp.where(low, pltpu.roll(a, LANES - size * bit, 1), b)
        bit *= 2
    return v


def pack_kernel(left_ref, right_ref, out_ref, held, right, piece, into, out_of):
    slices, _, near, depth, _ = left_ref.shape
    each = 2 * slices
    halves = [pl.ds(0, near // 2), pl.ds(near // 2, near // 2)]
    parts = [(i, half) for half in halves for i in range(each)]
    copies = []
    for n, (i, half) in enumerate(parts):
        copies.append(pltpu.make_async_copy(left_ref.at[i // 2, i % 2, half], held.at[i, half], into.at[n]))
        copies[-1].start()
    given = pltpu.make_async_copy(right_ref, right, into.at[len(parts)])
    given.start()
    last = []
    for n, (i, half) in enumerate(parts):
        copies[n].wait()
        to = out_ref.at[half, pl.ds(i * depth, depth), :]
        last.append(pltpu.make_async_copy(held.at[i, half], to, out_of.at[n]))
        last[-1].start()
    given.wait()
    width = right.shape[2]
    for t in range(near // each):
        lanes = pl.ds(t * LANES, LANES)
        w = swap_blocks([right[j % slices, j // slices, :, lanes] for j in range(each)])
        for g in range(each):
            piece[t * each + g] = w[g]
    to = out_ref.at[:, pl.ds(each * depth, width), :]
    last.append(pltpu.make_async_copy(piece, to, out_of.at[len(parts)]))
    last[-1].start()
    for copy in last:
        copy.wait()


def spread_kernel(coef_ref, near_ref, out_ref):
    cuts, far, width, _ = out_ref.shape
    body = near_ref.shape[1] - cuts * width // near_ref.shape[0]
    for q87 in range(cuts):
        for q6 in range(2):
            for q0 in range(2):
                for q2 in range(2):
                    two = near_ref[ORDER.index(q87 * 4 + q6 * 2 + q2), pl.ds(body + q0, 2, stride=2), :]
                    out_ref[q87 ^ HALF, 0, pl.ds(q6 * 8 + q0 * 4 + q2 * 2, 2), :] = two
        for g in range(1, far):
            out_ref[q87 ^ HALF, g] = out_ref[q87 ^ HALF, 0]


def coef_kernel(far_ref, closing_ref, out_ref):
    slices, heads, each, _ = out_ref.shape
    first = far_ref[0] * 2
    lane = lax.broadcasted_iota(jnp.int32, (each, LANES), 1)
    for s in range(slices):
        rows = closing_ref[pl.ds(s * each, each), :]
        for h in range(heads):
            head = (ORDER[h] // 2) * 16 + first + ORDER[h] % 2
            one = jnp.sum(jnp.where(lane == head, rows, 0.0), axis=1, keepdims=True)
            out_ref[s, h] = jnp.broadcast_to(one, (each, LANES))


def close_kernel(coef_ref, left_ref, out_ref, *piece_refs):
    heads = left_ref.shape[0]
    outs = coef_ref.shape[2] // 2
    rows = 8
    for s, piece_ref in enumerate(piece_refs):
        depth = piece_ref.shape[0]
        acc = [[None] * (depth // rows) for _ in range(2 * outs)]
        for h in range(heads):
            co = [jnp.broadcast_to(coef_ref[s, h, pl.ds(j, 1), :], (rows, LANES)) for j in range(2 * outs)]
            for kb in range(depth // rows):
                at = 2 * s * depth + kb * rows
                re = left_ref[h, pl.ds(at, rows), :]
                im = left_ref[h, pl.ds(at + depth, rows), :]
                for o in range(outs):
                    cre, cim = co[o], co[outs + o]
                    new_re = cre * re - cim * im
                    new_im = cre * im + cim * re
                    if h:
                        new_re, new_im = acc[o][kb] + new_re, acc[outs + o][kb] + new_im
                    acc[o][kb], acc[outs + o][kb] = new_re, new_im
        for kb in range(depth // rows):
            for j in range(2 * outs):
                lanes = pl.ds(j * LANES, LANES)
                piece_ref[pl.ds(kb * rows, rows), lanes] = acc[j][kb]
                out_ref[pl.ds(s * depth + kb * rows, rows), lanes] = acc[j][kb]


def join_kernel(cut_ref, right_ref, *refs):
    *x_refs, out_ref, lhs, rhs = refs
    depth, wide = x_refs[2].shape
    slices = len(x_refs) // 2 - 1
    x_refs = [x.at[pl.ds(s * depth, depth), :] for x in x_refs[:2] for s in range(slices)] + x_refs[2:]
    half = wide // 2
    first = lax.broadcasted_iota(jnp.int32, (8, LANES), 0) < 4
    for i in range(4):
        cut = cut_ref[0] ^ (i ^ HALF)
        lanes = pl.ds(i * LANES, LANES)
        for t in range(4):
            for q6 in range(2):
                at = pl.ds(q6 * 8, 8)
                low = right_ref[cut, (2 * t - MID) % 8, at, :]
                high = right_ref[cut, (2 * t + 1 - MID) % 8, at, :]
                to = (q6 * 8 + t * 2) * 8
                lhs[pl.ds(to, 8), lanes] = jnp.where(first, low, pltpu.roll(high, 4, 0))
                lhs[pl.ds(to + 8, 8), lanes] = jnp.where(first, pltpu.roll(low, 4, 0), high)
        for s in range(slices):
            x_ref = x_refs[i * slices + s]
            re = pl.ds((2 * i * slices + s) * depth, depth)
            im = pl.ds(((2 * i + 1) * slices + s) * depth, depth)
            rhs[re, :] = x_ref[...]
            rhs[im, :half] = -x_ref[:, half:]
            rhs[im, half:] = x_ref[:, :half]
    for j in range(0, wide // LANES, 2):
        right = rhs[:, pl.ds(j * LANES, 2 * LANES)]
        out = jnp.dot(lhs[...], right, precision=lax.Precision.HIGH, preferred_element_type=F32)
        out_ref[:, j, :, :] = out[:, :LANES].reshape(16, 8, LANES)
        out_ref[:, j + 1, :, :] = out[:, LANES:].reshape(16, 8, LANES)


def sum_kernel(scale, parts_ref, out_ref):
    for j in range(parts_ref.shape[1]):
        total = parts_ref[0, j]
        for i in range(1, parts_ref.shape[0]):
            total = total + parts_ref[i, j]
        out_ref[:, j, :] = pltpu.roll(total * scale, (8 - LAST) % 8, 0)


def finish_kernel(parts_ref, out_ref):
    total = parts_ref[0]
    for i in range(1, parts_ref.shape[0]):
        total = total + parts_ref[i]
    outs = out_ref.shape[0]
    for c in range(2):
        for o in range(outs):
            out_ref[o, pl.ds(c, 1), :] = total[c * outs + o : c * outs + o + 1, :]


def kernel_call(body, shape, specs, cost, name, scratch=(), vmem=16, to=VMEM):
    flops, size = cost
    return pl.pallas_call(
        body,
        out_shape=jax.tree.map(lambda n: jax.ShapeDtypeStruct(n, F32), shape, is_leaf=lambda n: isinstance(n, tuple)),
        in_specs=specs,
        out_specs=to,
        scratch_shapes=scratch,
        compiler_params=pltpu.CompilerParams(vmem_limit_bytes=vmem * 2**20),
        cost_estimate=pl.CostEstimate(flops=flops, bytes_accessed=size, transcendentals=0),
        name=name,
    )


def shards(left_tensor, right_tensor, closing_tensor):
    slices, _, _, depth, rows = left_tensor.shape
    width = right_tensor.shape[3]
    outs = closing_tensor.shape[3]
    near = 16
    kk = depth // near
    body = slices * 2 * kk
    here = lax.axis_index(FAR).reshape(1)

    x = kernel_call(
        pack_kernel,
        (near, body + width, LANES),
        [ANY, ANY],
        (0, 2**21),
        "pack",
        [
            pltpu.VMEM((slices * 2, near, kk, rows), F32),
            pltpu.VMEM((slices, 2, width, depth), F32),
            pltpu.VMEM((near, width, LANES), F32),
            pltpu.SemaphoreType.DMA((slices * 4 + 1,)),
            pltpu.SemaphoreType.DMA((slices * 4 + 1,)),
        ],
        60,
        ANY,
    )(left_tensor.reshape(slices, 2, near, kk, rows), right_tensor.transpose(0, 1, 3, 2))

    with jax.named_scope("near_move"):
        x = lax.all_to_all(x, NEAR, 0, 0, tiled=True, axis_index_groups=[ORDER])

    heads = closing_tensor.shape[2]
    co = kernel_call(
        coef_kernel, (slices, near, 2 * outs, LANES), [SMEM, VMEM], (2**18, 2**18), "coef"
    )(here, closing_tensor.transpose(0, 1, 3, 2).reshape(slices * 2 * outs, heads))

    cuts = 4
    r = kernel_call(
        spread_kernel, (cuts, 8, near * width // cuts, LANES), [ANY, VMEM], (0, 2**18), "spread"
    )(co, x)
    with jax.named_scope("right_move"):
        r = r.reshape(cuts * 8, near * width // cuts, LANES)
        group = [(c ^ HALF) * 8 + (f + MID) % 8 for c in range(cuts) for f in range(8)]
        r = lax.all_to_all(r, CUTS + (FAR,), 0, 0, tiled=True, axis_index_groups=[group])
        r = r.reshape(cuts, 8, near * width // cuts, LANES)

    swap = [(0, 1), (1, 0)]
    wide = 2 * outs * rows
    x0, *pieces = kernel_call(
        close_kernel,
        [(slices * kk, wide)] + [(kk, wide)] * slices,
        [VMEM, VMEM],
        (2**22, 6 * 2**18),
        "close",
        to=[VMEM] * (1 + slices),
    )(co, x)
    with jax.named_scope("cuts_gather"):
        x2 = [lax.ppermute(piece, "yh", swap) for piece in pieces]
        x1 = lax.ppermute(x0, "core", swap)
        x3 = [lax.ppermute(piece, "core", swap) for piece in x2]

    p = kernel_call(
        join_kernel,
        (near, 2 * outs, 8, rows),
        [SMEM] + [VMEM] * (3 + 2 * slices),
        (2**27, 2**21),
        "join",
        [pltpu.VMEM((128, cuts * LANES), F32), pltpu.VMEM((2 * cuts * slices * kk, wide), F32)],
    )(lax.axis_index(CUTS).reshape(1), r, x0, x1, *x2, *x3)

    with jax.named_scope("sum_move"):
        p = lax.all_to_all(p, NEAR, 0, 0, tiled=True)
    p = kernel_call(
        functools.partial(sum_kernel, (slices * cuts) ** -0.5),
        (8, 2 * outs, rows),
        [VMEM],
        (2**18, 2**20),
        "sum",
    )(p)

    with jax.named_scope("last_move"):
        group = [(f + LAST) % 8 for f in range(8)]
        p = lax.all_to_all(p, FAR, 0, 0, tiled=True, axis_index_groups=[group])
    p = kernel_call(finish_kernel, (outs, 2, rows), [VMEM], (2**14, 2**17), "finish")(p)
    return p.reshape(1, outs, 2, rows)


def solution(mesh):
    fine = Mesh(mesh.devices.reshape([n for _, n in PARTS]), [name for name, _ in PARTS])
    return jax.shard_map(
        shards,
        mesh=fine,
        in_specs=(
            P(CUTS, None, MODE, None, None),
            P(CUTS, None, None, MODE),
            P(CUTS, None, None, None),
        ),
        out_specs=P(CUTS + MODE, None, None, None),
        check_vma=False,
    )
```

```python
import functools

import jax
import jax.numpy as jnp
from jax import lax
from jax.experimental import pallas as pl
from jax.experimental.pallas import tpu as pltpu
from jax.sharding import Mesh
from jax.sharding import PartitionSpec as P

PARTS = (("yh", 2), ("core", 2), ("yl", 2), ("x", 4), ("za", 8), ("zb", 2))
CUTS = ("yh", "core")
MODE = ("yl", "x", "za", "zb")
NEAR = ("yl", "x", "zb")
FAR = "za"

F32 = jnp.float32
LANES = 128
MID = 6
HALF = 0
LAST = 4
ORDER = [yl * 8 + x * 2 + zb for x in (3, 1, 2, 0) for yl in (1, 0) for zb in range(2)]
SMEM = pl.BlockSpec(memory_space=pltpu.SMEM)
VMEM = pl.BlockSpec(memory_space=pltpu.VMEM)
ANY = pl.BlockSpec(memory_space=pl.ANY)


def swap_blocks(v):
    n = len(v)
    size = LANES // n
    block = lax.broadcasted_iota(jnp.int32, v[0].shape, 1) // size
    v = list(v)
    bit = 1
    while bit < n:
        low = (block & bit) == 0
        for i in range(n):
            if i & bit:
                continue
            a, b = v[i], v[i | bit]
            v[i] = jnp.where(low, a, pltpu.roll(b, size * bit, 1))
            v[i | bit] = jnp.where(low, pltpu.roll(a, LANES - size * bit, 1), b)
        bit *= 2
    return v


def pack_kernel(left_ref, right_ref, out_ref, held, right, piece, into, out_of):
    slices, _, near, depth, _ = left_ref.shape
    each = 2 * slices
    halves = [pl.ds(0, near // 2), pl.ds(near // 2, near // 2)]
    parts = [(i, half) for half in halves for i in range(each)]
    copies = []
    for n, (i, half) in enumerate(parts):
        copies.append(pltpu.make_async_copy(left_ref.at[i // 2, i % 2, half], held.at[i, half], into.at[n]))
        copies[-1].start()
    given = pltpu.make_async_copy(right_ref, right, into.at[len(parts)])
    given.start()
    last = []
    for n, (i, half) in enumerate(parts):
        copies[n].wait()
        to = out_ref.at[half, pl.ds(i * depth, depth), :]
        last.append(pltpu.make_async_copy(held.at[i, half], to, out_of.at[n]))
        last[-1].start()
    given.wait()
    width = right.shape[2]
    for t in range(near // each):
        lanes = pl.ds(t * LANES, LANES)
        w = swap_blocks([right[j % slices, j // slices, :, lanes] for j in range(each)])
        for g in range(each):
            piece[t * each + g] = w[g]
    to = out_ref.at[:, pl.ds(each * depth, width), :]
    last.append(pltpu.make_async_copy(piece, to, out_of.at[len(parts)]))
    last[-1].start()
    for copy in last:
        copy.wait()


def spread_kernel(coef_ref, near_ref, out_ref):
    cuts, far, width, _ = out_ref.shape
    body = near_ref.shape[1] - cuts * width // near_ref.shape[0]
    for q87 in range(cuts):
        for q6 in range(2):
            for q0 in range(2):
                for q2 in range(2):
                    two = near_ref[ORDER.index(q87 * 4 + q6 * 2 + q2), pl.ds(body + q0, 2, stride=2), :]
                    out_ref[q87 ^ HALF, 0, pl.ds(q6 * 8 + q0 * 4 + q2 * 2, 2), :] = two
        for g in range(1, far):
            out_ref[q87 ^ HALF, g] = out_ref[q87 ^ HALF, 0]


def coef_kernel(far_ref, closing_ref, out_ref):
    slices, heads, each, _ = out_ref.shape
    first = far_ref[0] * 2
    lane = lax.broadcasted_iota(jnp.int32, (each, LANES), 1)
    for s in range(slices):
        rows = closing_ref[pl.ds(s * each, each), :]
        for h in range(heads):
            head = (ORDER[h] // 2) * 16 + first + ORDER[h] % 2
            one = jnp.sum(jnp.where(lane == head, rows, 0.0), axis=1, keepdims=True)
            out_ref[s, h] = jnp.broadcast_to(one, (each, LANES))


def close_kernel(coef_ref, left_ref, out_ref, *piece_refs):
    heads = left_ref.shape[0]
    outs = coef_ref.shape[2] // 2
    rows = 8
    for s, piece_ref in enumerate(piece_refs):
        depth = piece_ref.shape[0]
        acc = [[None] * (depth // rows) for _ in range(2 * outs)]
        for h in range(heads):
            co = [jnp.broadcast_to(coef_ref[s, h, pl.ds(j, 1), :], (rows, LANES)) for j in range(2 * outs)]
            for kb in range(depth // rows):
                at = 2 * s * depth + kb * rows
                re = left_ref[h, pl.ds(at, rows), :]
                im = left_ref[h, pl.ds(at + depth, rows), :]
                for o in range(outs):
                    cre, cim = co[o], co[outs + o]
                    new_re = cre * re - cim * im
                    new_im = cre * im + cim * re
                    if h:
                        new_re, new_im = acc[o][kb] + new_re, acc[outs + o][kb] + new_im
                    acc[o][kb], acc[outs + o][kb] = new_re, new_im
        for kb in range(depth // rows):
            for j in range(2 * outs):
                lanes = pl.ds(j * LANES, LANES)
                piece_ref[pl.ds(kb * rows, rows), lanes] = acc[j][kb]
                out_ref[pl.ds(s * depth + kb * rows, rows), lanes] = acc[j][kb]


def join_kernel(cut_ref, right_ref, *refs):
    *x_refs, out_ref, lhs, rhs = refs
    depth, wide = x_refs[2].shape
    slices = len(x_refs) // 2 - 1
    x_refs = [x.at[pl.ds(s * depth, depth), :] for x in x_refs[:2] for s in range(slices)] + x_refs[2:]
    half = wide // 2
    first = lax.broadcasted_iota(jnp.int32, (8, LANES), 0) < 4
    for i in range(4):
        cut = cut_ref[0] ^ (i ^ HALF)
        lanes = pl.ds(i * LANES, LANES)
        for t in range(4):
            for q6 in range(2):
                at = pl.ds(q6 * 8, 8)
                low = right_ref[cut, (2 * t - MID) % 8, at, :]
                high = right_ref[cut, (2 * t + 1 - MID) % 8, at, :]
                to = (q6 * 8 + t * 2) * 8
                lhs[pl.ds(to, 8), lanes] = jnp.where(first, low, pltpu.roll(high, 4, 0))
                lhs[pl.ds(to + 8, 8), lanes] = jnp.where(first, pltpu.roll(low, 4, 0), high)
        for s in range(slices):
            x_ref = x_refs[i * slices + s]
            re = pl.ds((2 * i * slices + s) * depth, depth)
            im = pl.ds(((2 * i + 1) * slices + s) * depth, depth)
            rhs[re, :] = x_ref[...]
            rhs[im, :half] = -x_ref[:, half:]
            rhs[im, half:] = x_ref[:, :half]
    for j in range(0, wide // LANES, 2):
        right = rhs[:, pl.ds(j * LANES, 2 * LANES)]
        out = jnp.dot(lhs[...], right, precision=lax.Precision.HIGHEST, preferred_element_type=F32)
        out_ref[:, j, :, :] = out[:, :LANES].reshape(16, 8, LANES)
        out_ref[:, j + 1, :, :] = out[:, LANES:].reshape(16, 8, LANES)


def sum_kernel(scale, parts_ref, out_ref):
    for j in range(parts_ref.shape[1]):
        total = parts_ref[0, j]
        for i in range(1, parts_ref.shape[0]):
            total = total + parts_ref[i, j]
        out_ref[:, j, :] = pltpu.roll(total * scale, (8 - LAST) % 8, 0)


def finish_kernel(parts_ref, out_ref):
    total = parts_ref[0]
    for i in range(1, parts_ref.shape[0]):
        total = total + parts_ref[i]
    outs = out_ref.shape[0]
    for c in range(2):
        for o in range(outs):
            out_ref[o, pl.ds(c, 1), :] = total[c * outs + o : c * outs + o + 1, :]


def kernel_call(body, shape, specs, cost, name, scratch=(), vmem=16, to=VMEM):
    flops, size = cost
    return pl.pallas_call(
        body,
        out_shape=jax.tree.map(lambda n: jax.ShapeDtypeStruct(n, F32), shape, is_leaf=lambda n: isinstance(n, tuple)),
        in_specs=specs,
        out_specs=to,
        scratch_shapes=scratch,
        compiler_params=pltpu.CompilerParams(vmem_limit_bytes=vmem * 2**20),
        cost_estimate=pl.CostEstimate(flops=flops, bytes_accessed=size, transcendentals=0),
        name=name,
    )


def shards(left_tensor, right_tensor, closing_tensor):
    slices, _, _, depth, rows = left_tensor.shape
    width = right_tensor.shape[3]
    outs = closing_tensor.shape[3]
    near = 16
    kk = depth // near
    body = slices * 2 * kk
    here = lax.axis_index(FAR).reshape(1)

    x = kernel_call(
        pack_kernel,
        (near, body + width, LANES),
        [ANY, ANY],
        (0, 2**21),
        "pack",
        [
            pltpu.VMEM((slices * 2, near, kk, rows), F32),
            pltpu.VMEM((slices, 2, width, depth), F32),
            pltpu.VMEM((near, width, LANES), F32),
            pltpu.SemaphoreType.DMA((slices * 4 + 1,)),
            pltpu.SemaphoreType.DMA((slices * 4 + 1,)),
        ],
        60,
        ANY,
    )(left_tensor.reshape(slices, 2, near, kk, rows), right_tensor.transpose(0, 1, 3, 2))

    with jax.named_scope("near_move"):
        x = lax.all_to_all(x, NEAR, 0, 0, tiled=True, axis_index_groups=[ORDER])

    heads = closing_tensor.shape[2]
    co = kernel_call(
        coef_kernel, (slices, near, 2 * outs, LANES), [SMEM, VMEM], (2**18, 2**18), "coef"
    )(here, closing_tensor.transpose(0, 1, 3, 2).reshape(slices * 2 * outs, heads))

    cuts = 4
    r = kernel_call(
        spread_kernel, (cuts, 8, near * width // cuts, LANES), [ANY, VMEM], (0, 2**18), "spread"
    )(co, x)
    with jax.named_scope("right_move"):
        r = r.reshape(cuts * 8, near * width // cuts, LANES)
        group = [(c ^ HALF) * 8 + (f + MID) % 8 for c in range(cuts) for f in range(8)]
        r = lax.all_to_all(r, CUTS + (FAR,), 0, 0, tiled=True, axis_index_groups=[group])
        r = r.reshape(cuts, 8, near * width // cuts, LANES)

    swap = [(0, 1), (1, 0)]
    wide = 2 * outs * rows
    x0, *pieces = kernel_call(
        close_kernel,
        [(slices * kk, wide)] + [(kk, wide)] * slices,
        [VMEM, VMEM],
        (2**22, 6 * 2**18),
        "close",
        to=[VMEM] * (1 + slices),
    )(co, x)
    with jax.named_scope("cuts_gather"):
        x2 = [lax.ppermute(piece, "yh", swap) for piece in pieces]
        x1 = lax.ppermute(x0, "core", swap)
        x3 = [lax.ppermute(piece, "core", swap) for piece in x2]

    p = kernel_call(
        join_kernel,
        (near, 2 * outs, 8, rows),
        [SMEM] + [VMEM] * (3 + 2 * slices),
        (2**27, 2**21),
        "join",
        [pltpu.VMEM((128, cuts * LANES), F32), pltpu.VMEM((2 * cuts * slices * kk, wide), F32)],
    )(lax.axis_index(CUTS).reshape(1), r, x0, x1, *x2, *x3)

    with jax.named_scope("sum_move"):
        p = lax.all_to_all(p, NEAR, 0, 0, tiled=True)
    p = kernel_call(
        functools.partial(sum_kernel, (slices * cuts) ** -0.5),
        (8, 2 * outs, rows),
        [VMEM],
        (2**18, 2**20),
        "sum",
    )(p)

    with jax.named_scope("last_move"):
        group = [(f + LAST) % 8 for f in range(8)]
        p = lax.all_to_all(p, FAR, 0, 0, tiled=True, axis_index_groups=[group])
    p = kernel_call(finish_kernel, (outs, 2, rows), [VMEM], (2**14, 2**17), "finish")(p)
    return p.reshape(1, outs, 2, rows)


def solution(mesh):
    fine = Mesh(mesh.devices.reshape([n for _, n in PARTS]), [name for name, _ in PARTS])
    return jax.shard_map(
        shards,
        mesh=fine,
        in_specs=(
            P(CUTS, None, MODE, None, None),
            P(CUTS, None, None, MODE),
            P(CUTS, None, None, None),
        ),
        out_specs=P(CUTS + MODE, None, None, None),
        check_vma=False,
    )
```
